32 devices in a mesh: dp: 8 (over y, x, core), tensor: 4 (over z).
Axes of the slice: x: 2, y: 2, z: 4, core: 2. Of those that a mesh axis runs over, the one named last changes fastest.
Arguments:
- image_in: bfloat16 [16384, 1536], P(('dp', 'tensor')), may hold values from -6 to 6
- text_in: bfloat16 [2464, 1536], P(('dp', 'tensor')), may hold values from -6 to 6
- condition: bfloat16 [16, 1536], P('dp'), may hold values from -6 to 6
- live_slots: int32 [16], P('dp'), may hold values from 0 to 1, as said below
- ada_weight: bfloat16 [2, 1536, 6, 1536], P(None, 'dp', None, 'tensor'), may hold values from -0.15625 to 0.15625
- ada_bias: bfloat16 [2, 6, 1536], replicated, may hold values from -3 to 3
- qkv_weight: bfloat16 [2, 3, 1536, 1536], P(None, None, 'dp', 'tensor'), may hold values from -0.21875 to 0.21875
- qv_bias: bfloat16 [2, 2, 1536], replicated, may hold values from -3 to 3
- proj_weight: bfloat16 [2, 1536, 1536], P(None, 'tensor', 'dp'), may hold values from -0.875 to 0.875
- proj_bias: bfloat16 [2, 1536], replicated, may hold values from -3 to 3
- up_weight: bfloat16 [2, 1536, 6144], P(None, 'dp', 'tensor'), may hold values from -0.15625 to 0.15625
- up_bias: bfloat16 [2, 6144], replicated, may hold values from -3 to 3
- down_weight: bfloat16 [2, 6144, 1536], P(None, 'tensor', 'dp'), may hold values from -0.078125 to 0.078125
- down_bias: bfloat16 [2, 1536], replicated, may hold values from -3 to 3
- image_grad: bfloat16 [16384, 1536], P(('dp', 'tensor')), may hold values from -6 to 6
- text_grad: bfloat16 [2464, 1536], P(('dp', 'tensor')), may hold values from -6 to 6
Outputs:
- image_out: bfloat16 [16384, 1536], P(('dp', 'tensor'))
- text_out: bfloat16 [2464, 1536], P(('dp', 'tensor'))
- image_in_grad: float32 [16384, 1536], P(('dp', 'tensor'))
- text_in_grad: float32 [2464, 1536], P(('dp', 'tensor'))
- condition_grad: float32 [16, 1536], P('dp', 'tensor')
- ada_weight_grad: float32 [2, 1536, 6, 1536], P(None, 'dp', None, 'tensor')
- ada_bias_grad: float32 [2, 6, 1536], replicated
- qkv_weight_grad: float32 [2, 3, 1536, 1536], P(None, None, 'dp', 'tensor')
- qv_bias_grad: float32 [2, 2, 1536], replicated
- proj_weight_grad: float32 [2, 1536, 1536], P(None, 'tensor', 'dp')
- proj_bias_grad: float32 [2, 1536], replicated
- up_weight_grad: float32 [2, 1536, 6144], P(None, 'dp', 'tensor')
- up_bias_grad: float32 [2, 6144], replicated
- down_weight_grad: float32 [2, 6144, 1536], P(None, 'tensor', 'dp')
- down_bias_grad: float32 [2, 1536], replicated
The draws below stay inside these ranges and needn't reach their ends.
Inputs may be any that keep to these rules, and one draw needn't show every extreme that they name: `live_slots`: entry 2 * g + j is 1 when slot j of group g holds a sequence; the live slots of a group come first, every group has one or more, and some group has all 2.
All inputs are finite; a program needn't handle non-finite values.
Results may differ from the reference program's by a relative error of at most 0.015.
The reference program's roundings to bfloat16 on the way count: a program that leaves them out, or rounds other values in their place, can miss the bound.
Values may be sent and summed in bfloat16 or wider, within the bound.
A program may use at most 384 MiB of HBM per device.

```python
import jax
import jax.numpy as jnp
from jax import lax

D = 1536
HEADS = 24
FF = 6144
IMG = 1024
TXT = 154
HEAD_DIM = 64
SLOTS = 2
SEQS = 16


def draw_live_slots(key, part):
    groups = SEQS // SLOTS
    counts = jax.random.randint(jax.random.fold_in(key, 11), (groups,), 1, SLOTS + 1)
    fullest = jax.random.randint(jax.random.fold_in(key, 12), (), 0, groups)
    counts = jnp.where(jnp.arange(groups) == fullest, SLOTS, counts)
    position = jnp.arange(SLOTS)
    return (position[None, :] < counts[:, None]).astype(jnp.int32).reshape(SEQS)


def shard_levels(own_key, extent, shards, least, top_value):
    def one(axis_at, shards_of):
        draws = jax.random.uniform(jax.random.fold_in(jax.random.fold_in(own_key, 6), axis_at), (shards_of,), jnp.float32, least / len(shards), top_value / len(shards))
        return jnp.repeat(jnp.exp(draws), extent[axis_at] // shards_of).reshape((-1,) + (1,) * (len(extent) - axis_at - 1))

    factor_of = one(*shards[0])
    for cut in shards[1:]:
        factor_of = factor_of * one(*cut)
    return factor_of


def gaussian(rng, dims, deviation, reach, split=(), dtype=jnp.bfloat16):
    drawn = deviation * jax.random.normal(rng, dims, jnp.float32)
    if split:
        drawn = drawn * shard_levels(rng, dims, split, -0.22, 0.18)
    return jnp.clip(drawn, -reach, reach).astype(dtype)


def setup_inputs(seed: int = 0) -> dict:
    arg_keys = jax.random.split(jax.random.key(seed), 17)
    return {
        "image_in": gaussian(arg_keys[0], (SEQS * IMG, D), 1.0, 6.0, ((0, 32),)),
        "text_in": gaussian(arg_keys[1], (SEQS * TXT, D), 1.0, 6.0, ((0, 32),)),
        "condition": gaussian(arg_keys[2], (SEQS, D), 1.0, 6.0, ((0, 8),)),
        "live_slots": draw_live_slots(jax.random.fold_in(arg_keys[16], 71), 0),
        "ada_weight": gaussian(arg_keys[4], (2, D, 6, D), D ** -0.5, 0.15625, ((1, 8), (3, 4))),
        "ada_bias": gaussian(arg_keys[5], (2, 6, D), 0.5, 3.0),
        "qkv_weight": gaussian(arg_keys[6], (2, 3, D, D), (D // 2) ** -0.5, 0.21875, ((2, 8), (3, 4))),
        "qv_bias": gaussian(arg_keys[7], (2, 2, D), 0.5, 3.0),
        "proj_weight": gaussian(arg_keys[8], (2, D, D), (D // 32) ** -0.5, 0.875, ((1, 4), (2, 8))),
        "proj_bias": gaussian(arg_keys[9], (2, D), 0.5, 3.0),
        "up_weight": gaussian(arg_keys[10], (2, D, FF), D ** -0.5, 0.15625, ((1, 8), (2, 4))),
        "up_bias": gaussian(arg_keys[11], (2, FF), 0.5, 3.0),
        "down_weight": gaussian(arg_keys[12], (2, FF, D), FF ** -0.5, 0.078125, ((1, 4), (2, 8))),
        "down_bias": gaussian(arg_keys[13], (2, D), 0.5, 3.0),
        "image_grad": gaussian(arg_keys[14], (SEQS * IMG, D), 1.0, 6.0, ((0, 32),)),
        "text_grad": gaussian(arg_keys[15], (SEQS * TXT, D), 1.0, 6.0, ((0, 32),)),
    }


@jax.custom_vjp
def low(v):
    return lax.optimization_barrier(v.astype(jnp.bfloat16)).astype(jnp.float32)

@jax.custom_vjp
def low_back(v):
    return v

def low_keep(v):
    return (low(v), None)

def low_pass(kept, grad):
    return (grad,)

def back_keep(v):
    return (v, None)

def back_low(kept, grad):
    return (low(grad),)
low.defvjp(low_keep, low_pass)
low_back.defvjp(back_keep, back_low)

def product(left_side, right_side):
    return jnp.dot(left_side, right_side, precision=lax.Precision.HIGHEST)

def normalize(values):
    average = lax.optimization_barrier(jnp.mean(values, axis=-1, keepdims=True))
    centred = values - average
    variance = lax.optimization_barrier(jnp.mean(centred * centred, axis=-1, keepdims=True))
    return centred * lax.rsqrt(variance + 1e-06)

def one_sequence(params, image_rows, text_rows, condition, active):
    ada_weight, ada_bias, qkv_weight, qv_bias, proj_weight, proj_bias, up_weight, up_bias, down_weight, down_bias = params
    silu_cond = low(jax.nn.silu(condition))
    inputs = (image_rows, text_rows)
    modulation = []
    queries = []
    keys_list = []
    values_list = []
    for stream in range(2):
        factors = jnp.einsum('d,dkc->kc', silu_cond, ada_weight[stream], precision=lax.Precision.HIGHEST) + ada_bias[stream]
        modulation.append(factors)
        hidden = low(normalize(inputs[stream]) * (1.0 + factors[1]) + factors[0])
        queries.append(low_back(low(product(hidden, qkv_weight[stream, 0]) + qv_bias[stream, 0])))
        keys_list.append(low_back(low(product(hidden, qkv_weight[stream, 1]))))
        values_list.append(low_back(low(product(hidden, qkv_weight[stream, 2]) + qv_bias[stream, 1])))
    length = IMG + TXT
    query_all = jnp.concatenate(queries, 0).reshape(length, HEADS, HEAD_DIM)
    key_all = jnp.concatenate(keys_list, 0).reshape(length, HEADS, HEAD_DIM)
    value_all = jnp.concatenate(values_list, 0).reshape(length, HEADS, HEAD_DIM)
    scores = low_back(jnp.einsum('qhd,khd->hqk', query_all, key_all, precision=lax.Precision.HIGHEST) * HEAD_DIM ** (-0.5))
    weights = low(jax.nn.softmax(scores, axis=-1))
    attended = jnp.einsum('hqk,khd->qhd', weights, value_all, precision=lax.Precision.HIGHEST).reshape(length, D)
    attended = low_back(low(attended))
    pieces = (attended[:IMG], attended[IMG:])
    results = []
    for stream in range(2):
        factors = modulation[stream]
        branch = low_back(product(pieces[stream], proj_weight[stream]) + proj_bias[stream])
        middle = inputs[stream] + factors[2] * branch
        hidden = low(normalize(middle) * (1.0 + factors[4]) + factors[3])
        inner_rows = low_back(product(hidden, up_weight[stream]) + up_bias[stream])
        activated = low(jax.nn.gelu(inner_rows, approximate=True))
        output = low_back(product(activated, down_weight[stream]) + down_bias[stream])
        results.append(active * (middle + factors[5] * output))
    return (results[0], results[1])

def forward(params, image_rows, text_rows, condition, active):

    def scan_step(carried, slot_items):
        return (carried, jax.checkpoint(one_sequence)(params, slot_items[0], slot_items[1], slot_items[2], slot_items[3]))
    slot_items = (image_rows.reshape(SEQS, IMG, D), text_rows.reshape(SEQS, TXT, D), condition, active)
    carried, outputs = lax.scan(scan_step, None, slot_items)
    return (outputs[0].reshape(SEQS * IMG, D), outputs[1].reshape(SEQS * TXT, D))

def reference(image_in, text_in, condition, live_slots, ada_weight, ada_bias, qkv_weight, qv_bias, proj_weight, proj_bias, up_weight, up_bias, down_weight, down_bias, image_grad, text_grad):
    params = tuple((source.astype(jnp.float32) for source in (ada_weight, ada_bias, qkv_weight, qv_bias, proj_weight, proj_bias, up_weight, up_bias, down_weight, down_bias)))
    active = live_slots.astype(jnp.float32)

    def closed(params_in, image_rows, text_rows, cond_rows):
        return forward(params_in, image_rows, text_rows, cond_rows, active)
    outputs, pullback = jax.vjp(closed, params, image_in.astype(jnp.float32), text_in.astype(jnp.float32), condition.astype(jnp.float32))
    grad_params, grad_image, grad_text, grad_cond = pullback((image_grad.astype(jnp.float32), text_grad.astype(jnp.float32)))
    return (outputs[0].astype(jnp.bfloat16), outputs[1].astype(jnp.bfloat16), grad_image, grad_text, grad_cond, grad_params[0], grad_params[1], grad_params[2], grad_params[3], grad_params[4], grad_params[5], grad_params[6], grad_params[7], grad_params[8], grad_params[9])
```

```python
import functools

import jax
import jax.numpy as jnp
from jax import lax
from jax.experimental import pallas as pl
from jax.experimental.pallas import tpu as pltpu
from jax.sharding import Mesh
from jax.sharding import PartitionSpec as P

HEAD_DIM = 64
SCALE = HEAD_DIM ** (-0.5)
BF = jnp.bfloat16
F32 = jnp.float32
NEG = -1e30


def swap(v, axis):
    return lax.ppermute(v, axis, [(0, 1), (1, 0)])


def gather_bits(v, axes):
    for axis in axes:
        other = swap(v, axis)
        first = lax.axis_index(axis) == 0
        v = jnp.concatenate([jnp.where(first, v, other), jnp.where(first, other, v)], 0)
    return v


def scatter_bits(v, axes):
    for axis in axes:
        first = lax.axis_index(axis) == 0
        half = v.shape[0] // 2
        low, high = v[:half], v[half:]
        v = jnp.where(first, low, high) + swap(jnp.where(first, high, low), axis)
    return v


def sum_bits(v, axes):
    for axis in axes:
        v = v + swap(v, axis)
    return v


def index_of(axes):
    out = 0
    for axis in axes:
        out = out * 2 + lax.axis_index(axis)
    return out


def nt(a, b):
    return lax.dot_general(a, b, (((1,), (1,)), ((), ())), preferred_element_type=F32)


def nn(a, b):
    return lax.dot_general(a, b, (((1,), (0,)), ((), ())), preferred_element_type=F32)


def tn(a, b):
    return lax.dot_general(a, b, (((0,), (0,)), ((), ())), preferred_element_type=F32)


def flat(ref, h):
    whole = ref[...]
    merged = whole.reshape(whole.shape[0] * whole.shape[2], whole.shape[3])
    return merged[:, h * HEAD_DIM : (h + 1) * HEAD_DIM]


def pad_key(position, padded, real):
    return lax.rem(position, padded) >= real


def attend_kernel(
    chunk, txt, qi, ki, vi, qt, kt, vt, oi, ot, lse_i, lse_t
):
    rows = qi.shape[2]
    per = rows // chunk
    tp = qt.shape[2]
    keys_i = [flat(ki, h) for h in range(2)]
    vals_i = [flat(vi, h) for h in range(2)]
    keys_t = [flat(kt, h) for h in range(2)]
    vals_t = [flat(vt, h) for h in range(2)]
    mask = jnp.where(
        pad_key(lax.broadcasted_iota(jnp.int32, (1, 2 * tp), 1), tp, txt), NEG, 0.0
    ).astype(F32)

    def one(q_pair):
        outs, logs = [], []
        for h in range(2):
            q = q_pair[:, h * HEAD_DIM : (h + 1) * HEAD_DIM] * jnp.asarray(SCALE, BF)
            s_i = nt(q, keys_i[h])
            s_t = nt(q, keys_t[h]) + mask
            top = jnp.maximum(
                jnp.max(s_i, axis=1, keepdims=True), jnp.max(s_t, axis=1, keepdims=True)
            )
            p_i = jnp.exp(s_i - top)
            p_t = jnp.exp(s_t - top)
            total = jnp.sum(p_i, axis=1, keepdims=True) + jnp.sum(p_t, axis=1, keepdims=True)
            inv = 1.0 / total
            o = nn((p_i * inv).astype(BF), vals_i[h]) + nn((p_t * inv).astype(BF), vals_t[h])
            outs.append(o.astype(BF))
            logs.append((top + jnp.log(total)).reshape(1, -1))
        return jnp.concatenate(outs, axis=1), logs

    def step(c, carry):
        z = c // per
        r = pl.multiple_of(lax.rem(c, per) * chunk, chunk)
        o, logs = one(qi[z, 0, pl.ds(r, chunk), :])
        oi[z, 0, pl.ds(r, chunk), :] = o
        for h in range(2):
            lse_i[0, 0, h, pl.ds(c, 1), :] = logs[h]
        return carry

    lax.fori_loop(0, 2 * per, step, 0)
    whole = qt[...]
    o, logs = one(whole.reshape(2 * tp, whole.shape[3]))
    ot[...] = o.reshape(2, 1, tp, o.shape[1])
    for h in range(2):
        lse_t[0, 0, h, 0:1, :] = logs[h]


def attend_back_kernel(
    chunk, txt, qi, ki, vi, qt, kt, vt, gi, gt, lse_i, lse_t, di, dt, dk_i, dv_i, dk_t, dv_t
):
    rows = qi.shape[2]
    per = rows // chunk
    tp = qt.shape[2]
    hp = pl.program_id(1)
    pairs = pl.num_programs(1)
    width = 2 * HEAD_DIM
    keys_i = [flat(ki, h) for h in range(2)]
    vals_i = [flat(vi, h) for h in range(2)]
    keys_t = [flat(kt, h) for h in range(2)]
    vals_t = [flat(vt, h) for h in range(2)]
    mask = jnp.where(
        pad_key(lax.broadcasted_iota(jnp.int32, (2 * tp, 1), 0), tp, txt), NEG, 0.0
    ).astype(F32)
    dk_i[...] = jnp.zeros_like(dk_i)
    dv_i[...] = jnp.zeros_like(dv_i)
    dk_t[...] = jnp.zeros_like(dk_t)
    dv_t[...] = jnp.zeros_like(dv_t)

    def one(q_pair, g_pair, logs):
        outs = []
        for h in range(2):
            cols = slice(h * HEAD_DIM, (h + 1) * HEAD_DIM)
            q = q_pair[:, cols] * jnp.asarray(SCALE, BF)
            g = g_pair[:, cols]
            p_i = jnp.exp(nt(keys_i[h], q) - logs[h])
            p_t = jnp.exp(nt(keys_t[h], q) + mask - logs[h])
            dp_i = nt(vals_i[h], g)
            dp_t = nt(vals_t[h], g)
            delta = jnp.sum(p_i * dp_i, axis=0, keepdims=True) + jnp.sum(
                p_t * dp_t, axis=0, keepdims=True
            )
            dv_i[h] += nn(p_i.astype(BF), g)
            dv_t[h] += nn(p_t.astype(BF), g)
            ds_i = (p_i * (dp_i - delta)).astype(BF)
            ds_t = (p_t * (dp_t - delta)).astype(BF)
            dk_i[h] += nn(ds_i, q)
            dk_t[h] += nn(ds_t, q)
            dq = tn(ds_i, keys_i[h]) + tn(ds_t, keys_t[h])
            outs.append((dq * SCALE).astype(BF))
        return jnp.concatenate(outs, axis=1)

    def cols_of(kind):
        return pl.ds(pl.multiple_of((kind * pairs + hp) * width, width), width)

    def step(c, carry):
        z = c // per
        r = pl.multiple_of(lax.rem(c, per) * chunk, chunk)
        logs = [lse_i[0, 0, h, pl.ds(c, 1), :] for h in range(2)]
        dq = one(qi[z, 0, pl.ds(r, chunk), :], gi[z, 0, pl.ds(r, chunk), :], logs)
        di[z, 0, pl.ds(r, chunk), cols_of(0)] = dq
        return carry

    lax.fori_loop(0, 2 * per, step, 0)
    q_all, g_all = qt[...], gt[...]
    logs = [lse_t[0, 0, h, 0:1, :] for h in range(2)]
    dq = one(q_all.reshape(2 * tp, width), g_all.reshape(2 * tp, width), logs)
    dt[:, :, :, cols_of(0)] = dq.reshape(2, 1, tp, width)
    for kind, img, text in ((1, dk_i, dk_t), (2, dv_i, dv_t)):
        both = jnp.concatenate([img[0].astype(BF), img[1].astype(BF)], axis=1)
        di[:, :, :, cols_of(kind)] = both.reshape(2, 1, rows, width)
        both = jnp.concatenate([text[0].astype(BF), text[1].astype(BF)], axis=1)
        dt[:, :, :, cols_of(kind)] = both.reshape(2, 1, tp, width)


def qkv_specs(rows, tp, pairs):
    width = 2 * HEAD_DIM

    def spec(length, kind):
        return pl.BlockSpec(
            (2, 1, length, width), lambda s, h, kind=kind: (0, s, 0, kind * pairs + h)
        )

    return [spec(rows, kind) for kind in range(3)] + [spec(tp, kind) for kind in range(3)]


def lse_specs(n_chunks, chunk, tp):
    return [
        pl.BlockSpec((1, 1, 2, n_chunks, chunk), lambda s, h: (s, h, 0, 0, 0)),
        pl.BlockSpec((1, 1, 2, 1, 2 * tp), lambda s, h: (s, h, 0, 0, 0)),
    ]


def attention(img, text, txt, chunk):
    slots, rows, tp = img.shape[1], img.shape[2], text.shape[2]
    columns = img.shape[3] // 3
    width = 2 * HEAD_DIM
    pairs = columns // width
    n_chunks = 2 * rows // chunk
    keys = 2 * (rows + tp)
    out_spec = lambda length: pl.BlockSpec((2, 1, length, width), lambda s, h: (0, s, 0, h))
    return pl.pallas_call(
        functools.partial(attend_kernel, chunk, txt),
        grid=(slots, pairs),
        in_specs=qkv_specs(rows, tp, pairs),
        out_specs=[out_spec(rows), out_spec(tp)] + lse_specs(n_chunks, chunk, tp),
        out_shape=[
            jax.ShapeDtypeStruct((2, slots, rows, columns), BF),
            jax.ShapeDtypeStruct((2, slots, tp, columns), BF),
            jax.ShapeDtypeStruct((slots, pairs, 2, n_chunks, chunk), F32),
            jax.ShapeDtypeStruct((slots, pairs, 2, 1, 2 * tp), F32),
        ],
        compiler_params=pltpu.CompilerParams(vmem_limit_bytes=40 * 2**20),
        cost_estimate=pl.CostEstimate(
            flops=16 * slots * pairs * keys * keys * HEAD_DIM,
            bytes_accessed=slots * keys * columns * 8,
            transcendentals=2 * slots * pairs * keys * keys,
        ),
        name="attend",
    )(img, img, img, text, text, text)


def attention_back(img, text, grad_img, grad_text, lse_i, lse_t, txt, chunk):
    slots, rows, tp = img.shape[1], img.shape[2], text.shape[2]
    columns = img.shape[3] // 3
    width = 2 * HEAD_DIM
    pairs = columns // width
    n_chunks = 2 * rows // chunk
    keys = 2 * (rows + tp)
    g_spec = lambda length: pl.BlockSpec((2, 1, length, width), lambda s, h: (0, s, 0, h))
    d_spec = lambda length: pl.BlockSpec((2, 1, length, 3 * columns), lambda s, h: (0, s, 0, 0))
    return pl.pallas_call(
        functools.partial(attend_back_kernel, chunk, txt),
        grid=(slots, pairs),
        in_specs=qkv_specs(rows, tp, pairs)
        + [g_spec(rows), g_spec(tp)]
        + lse_specs(n_chunks, chunk, tp),
        out_specs=[d_spec(rows), d_spec(tp)],
        out_shape=[
            jax.ShapeDtypeStruct(img.shape, BF),
            jax.ShapeDtypeStruct(text.shape, BF),
        ],
        scratch_shapes=[
            pltpu.VMEM((2, 2 * rows, HEAD_DIM), F32),
            pltpu.VMEM((2, 2 * rows, HEAD_DIM), F32),
            pltpu.VMEM((2, 2 * tp, HEAD_DIM), F32),
            pltpu.VMEM((2, 2 * tp, HEAD_DIM), F32),
        ],
        compiler_params=pltpu.CompilerParams(vmem_limit_bytes=48 * 2**20),
        cost_estimate=pl.CostEstimate(
            flops=40 * slots * pairs * keys * keys * HEAD_DIM,
            bytes_accessed=slots * keys * columns * 16,
            transcendentals=2 * slots * pairs * keys * keys,
        ),
        name="attend_back",
    )(img, img, img, text, text, text, grad_img, grad_text, lse_i, lse_t)


class Layout:
    def __init__(self, dp_size, tensor_size):
        dp_bits = dp_size.bit_length() - 1
        t_bits = tensor_size.bit_length() - 1
        self.dp = tuple(f"d{i}" for i in range(dp_bits))
        self.tensor = tuple(f"t{i}" for i in range(t_bits))
        self.names = self.dp + self.tensor
        self.compact = dp_size == 8 and tensor_size == 4
        self.p = self.tensor[-1]
        if self.compact:
            self.y, self.x, self.q = self.dp
            self.zh = self.tensor[0]
            self.upper = ()
        else:
            self.q = self.tensor[-2]
            self.upper = self.tensor[:-2]
        self.rest = tuple(n for n in self.names if n not in (self.p, self.q))

    def my_columns(self, v):
        shards = 2 ** len(self.upper)
        part = v.shape[-1] // (4 * shards)
        v = v.reshape(v.shape[:-1] + (shards, 4, part))
        at = index_of((self.q, self.p))
        v = lax.dynamic_index_in_dim(v, at, v.ndim - 2, keepdims=False)
        return v.reshape(v.shape[:-2] + (shards * part,))

    def all_columns(self, v):
        shards = 2 ** len(self.upper)
        g = gather_bits(v[None], (self.p, self.q))
        g = g.reshape((4,) + v.shape[:-1] + (shards, v.shape[-1] // shards))
        g = jnp.moveaxis(g, 0, -2)
        return g.reshape(v.shape[:-1] + (4 * v.shape[-1],))

    def gather_rows(self, own):
        pair = swap(own, self.p)
        return jnp.concatenate([own, swap(own, self.q), pair, swap(pair, self.q)], 0)

    def sum_rows(self, product, factor):
        block = factor.shape[0] // 4
        far = product(factor[2 * block :])
        far = far[:block] + swap(far[block:].astype(BF), self.q).astype(F32)
        far = swap(far.astype(BF), self.p)
        near = product(factor[: 2 * block])
        near = near[:block] + swap(near[block:].astype(BF), self.q).astype(F32)
        return near + far.astype(F32)

    def gather_weight(self, w):
        two, part, kinds, columns = w.shape
        if not self.compact:
            w = lax.all_gather(w, self.dp, axis=1, tiled=True)
            if self.upper:
                w = lax.all_gather(w, self.upper, axis=3, tiled=True)
            return w.reshape(2, w.shape[1], -1)
        w = w.reshape(2, part, kinds * columns)
        joint = (self.q, self.zh)
        same = lax.axis_index(self.zh) == lax.axis_index(self.q)
        cross = lax.ppermute(w, joint, [(1, 2), (2, 1)])
        second = lax.ppermute(w, joint, [(0, 1), (3, 2), (2, 0), (1, 3)])
        first = jnp.where(same, w, cross)
        low = lax.axis_index(self.zh) == 0
        own = jnp.concatenate(
            [jnp.where(low, first, second), jnp.where(low, second, first)], axis=1
        )
        x, y = lax.axis_index(self.x), lax.axis_index(self.y)
        results = []
        for stream, (near_axis, far_axis) in enumerate(((self.x, self.y), (self.y, self.x))):
            mine = own[stream]
            near = swap(mine, near_axis)
            far, both = swap(mine, far_axis), swap(near, far_axis)
            dx, dy = (near, far) if stream == 0 else (far, near)
            whole = jnp.zeros((4,) + mine.shape, BF)
            for block, at in (
                (mine, 2 * y + x),
                (dx, 2 * y + 1 - x),
                (dy, 2 * (1 - y) + x),
                (both, 2 * (1 - y) + 1 - x),
            ):
                whole = lax.dynamic_update_index_in_dim(whole, block, at, 0)
            results.append(whole.reshape(-1, kinds * columns))
        return results

    def scatter_grad(self, grads, kinds):
        if not self.compact:
            d = grads[0].shape[0]
            g = jnp.stack(grads).astype(F32).reshape(2, d, kinds, -1)
            g = lax.psum_scatter(g, self.dp, scatter_dimension=1, tiled=True)
            if self.upper:
                g = lax.psum_scatter(g, self.upper, scatter_dimension=3, tiled=True)
            return g
        x, y = lax.axis_index(self.x), lax.axis_index(self.y)
        done = []
        for stream in range(2):
            g = grads[stream]
            n = g.shape[1]
            g = g.reshape(2, 2, -1, n)
            first = (self.x, x, 1, self.y, y) if stream == 0 else (self.y, y, 0, self.x, x)
            near_axis, near, dim, far_axis, far = first
            pick = lambda v, i, dim: lax.dynamic_index_in_dim(v, i, dim, keepdims=False)
            send = pick(g, 1 - near, dim).astype(BF)
            g = pick(g, near, dim).astype(F32) + swap(send, near_axis).astype(F32)
            g = pick(g, far, 0) + swap(pick(g, 1 - far, 0).astype(BF), far_axis).astype(F32)
            done.append(g)
        g = jnp.stack(done).reshape(2, 2, -1, n)
        zh = lax.axis_index(self.zh)
        joint = (self.q, self.zh)
        first = lax.dynamic_index_in_dim(g, zh, 1, keepdims=False)
        second = lax.dynamic_index_in_dim(g, 1 - zh, 1, keepdims=False)
        cross = lax.ppermute(first.astype(BF), joint, [(1, 2), (2, 1)])
        second = lax.ppermute(second.astype(BF), joint, [(1, 0), (2, 3), (0, 2), (3, 1)])
        same = zh == lax.axis_index(self.q)
        total = jnp.where(same, first, cross.astype(F32)) + second.astype(F32)
        return total.reshape(2, total.shape[1], kinds, -1)


def norm_parts(values):
    average = jnp.mean(values, axis=-1, keepdims=True)
    centred = values - average
    variance = jnp.mean(centred * centred, axis=-1, keepdims=True)
    inverse = lax.rsqrt(variance + 1e-06)
    return centred * inverse, inverse


def norm_back(normed, inverse, grad_in):
    first_mean = jnp.mean(grad_in, axis=-1, keepdims=True)
    cross_mean = jnp.mean(grad_in * normed, axis=-1, keepdims=True)
    return inverse * (grad_in - first_mean - normed * cross_mean)


def dot32(a, b):
    return jnp.dot(a, b, preferred_element_type=F32)


def dot_nt(a, b):
    return jnp.einsum("ij,kj->ik", a, b, preferred_element_type=F32)


def dot_tn(a, b):
    return jnp.einsum("ri,rj->ij", a, b, preferred_element_type=F32)


def gelu_slope(v):
    c = 0.7978845608028654
    inner = jnp.tanh(c * (v + 0.044715 * (v * v * v)))
    return 0.5 * (1.0 + inner) + 0.5 * v * (1.0 - inner * inner) * (
        c * (1.0 + 3 * 0.044715 * (v * v))
    )


def body(
    lay,
    image_in,
    text_in,
    condition,
    live_slots,
    ada_weight,
    ada_bias,
    qkv_weight,
    qv_bias,
    proj_weight,
    proj_bias,
    up_weight,
    up_bias,
    down_weight,
    down_bias,
    image_grad,
    text_grad,
):
    streams = range(2)
    width = image_in.shape[1]
    part = qkv_weight.shape[2]
    columns = qkv_weight.shape[3]
    img_rows, txt_rows = image_in.shape[0], text_in.shape[0]
    txt_pad = -(-txt_rows // 16) * 16
    group_slots = condition.shape[0]
    dp_index, t_index = index_of(lay.dp), index_of(lay.tensor)
    t_count = 2 ** len(lay.tensor)
    assert group_slots * 2 == t_count
    my_slot = t_index // 2
    dp_up, t_up = lay.dp[::-1], lay.tensor[::-1]

    def pad(v):
        return jnp.pad(v, ((0, txt_pad - txt_rows), (0, 0)))

    qkv_full = lay.gather_weight(jnp.swapaxes(qkv_weight, 1, 2))
    proj_full = lay.gather_weight(jnp.swapaxes(proj_weight, 1, 2)[:, :, None])
    up_full = lay.gather_weight(up_weight[:, :, None])
    down_full = lay.gather_weight(jnp.swapaxes(down_weight, 1, 2)[:, :, None])

    cond_all = gather_bits(condition, dp_up).astype(F32)
    silu_all = jax.nn.silu(cond_all).astype(BF)
    silu_mine = lax.dynamic_slice_in_dim(silu_all, dp_index * part, part, 1)
    mod = jnp.einsum("sd,tdkc->stkc", silu_mine, ada_weight, preferred_element_type=F32)
    mod = scatter_bits(mod, lay.dp)
    mod = gather_bits(mod[None], t_up)
    mod = lax.dynamic_index_in_dim(mod, my_slot, 1, keepdims=False)
    mod = jnp.moveaxis(mod, 0, 2).reshape(2, 6, width) + ada_bias.astype(F32)
    live = lax.dynamic_index_in_dim(live_slots, my_slot, 0, keepdims=False).astype(F32)

    inputs = (image_in.astype(F32), pad(text_in).astype(F32))
    grad_out = [live * g.astype(F32) for g in (image_grad, pad(text_grad))]
    grad_two = [(mod[s, 5] * grad_out[s]).astype(BF) for s in streams]

    first_norm = [norm_parts(inputs[s]) for s in streams]
    first_hidden = [
        (first_norm[s][0] * (1.0 + mod[s, 1]) + mod[s, 0]).astype(BF) for s in streams
    ]
    first_full = [lay.gather_rows(v) for v in first_hidden]
    qv = lay.my_columns(qv_bias.astype(F32))
    qkv_bias = jnp.concatenate([qv[:, 0], jnp.zeros_like(qv[:, 0]), qv[:, 1]], axis=1)
    qkv = [
        (dot32(first_full[s], qkv_full[s]) + qkv_bias[s])
        .astype(BF)
        .reshape(2, 2, first_hidden[s].shape[0], -1)
        for s in streams
    ]
    chunk = min(256, img_rows)
    heads_img, heads_txt, lse_i, lse_t = attention(qkv[0], qkv[1], txt_rows, chunk)
    heads_out = [v.reshape(-1, v.shape[3]) for v in (heads_img, heads_txt)]

    branch_one = [
        lay.sum_rows(lambda v, s=s: dot_nt(v, proj_full[s]), heads_out[s])
        + proj_bias[s].astype(F32)
        for s in streams
    ]
    middle = [inputs[s] + mod[s, 2] * branch_one[s] for s in streams]
    second_norm = [norm_parts(middle[s]) for s in streams]
    second_hidden = [
        (second_norm[s][0] * (1.0 + mod[s, 4]) + mod[s, 3]).astype(BF) for s in streams
    ]
    second_full = [lay.gather_rows(v) for v in second_hidden]
    grad_two_full = [lay.gather_rows(v) for v in grad_two]
    up_mine = lay.my_columns(up_bias.astype(F32))
    inner = [dot32(second_full[s], up_full[s]) + up_mine[s] for s in streams]
    activated = [jax.nn.gelu(v, approximate=True).astype(BF) for v in inner]
    branch_two = [
        lay.sum_rows(lambda v, s=s: dot_nt(v, down_full[s]), activated[s])
        + down_bias[s].astype(F32)
        for s in streams
    ]
    outputs = [(live * (middle[s] + mod[s, 5] * branch_two[s])).astype(BF) for s in streams]

    grad_inner = [
        (dot32(grad_two_full[s], down_full[s]) * gelu_slope(inner[s])).astype(BF) for s in streams
    ]
    grad_hidden_two = [
        lay.sum_rows(lambda v, s=s: dot_nt(v, up_full[s]), grad_inner[s]) for s in streams
    ]
    down_grads = [dot_tn(grad_two_full[s], activated[s]).astype(BF) for s in streams]
    up_grads = [dot_tn(second_full[s], grad_inner[s]).astype(BF) for s in streams]
    down_grad = jnp.swapaxes(lay.scatter_grad(down_grads, 1)[:, :, 0], 1, 2)
    up_grad = lay.scatter_grad(up_grads, 1)[:, :, 0]
    grad_middle = [
        grad_out[s]
        + norm_back(
            second_norm[s][0], second_norm[s][1], grad_hidden_two[s] * (1.0 + mod[s, 4])
        )
        for s in streams
    ]
    grad_one = [(mod[s, 2] * grad_middle[s]).astype(BF) for s in streams]
    grad_one_full = [lay.gather_rows(v) for v in grad_one]
    grad_heads = [dot32(grad_one_full[s], proj_full[s]).astype(BF) for s in streams]
    proj_grads = [dot_tn(grad_one_full[s], heads_out[s]).astype(BF) for s in streams]
    proj_grad = jnp.swapaxes(lay.scatter_grad(proj_grads, 1)[:, :, 0], 1, 2)
    grad_qkv = attention_back(
        qkv[0],
        qkv[1],
        grad_heads[0].reshape(heads_img.shape),
        grad_heads[1].reshape(heads_txt.shape),
        lse_i,
        lse_t,
        txt_rows,
        chunk,
    )
    grad_qkv = [v.reshape(-1, v.shape[3]) for v in grad_qkv]
    grad_hidden_one = [
        lay.sum_rows(lambda v, s=s: dot_nt(v, qkv_full[s]), grad_qkv[s]) for s in streams
    ]
    qkv_grads = [dot_tn(first_full[s], grad_qkv[s]).astype(BF) for s in streams]
    qkv_grad = jnp.swapaxes(lay.scatter_grad(qkv_grads, 3), 1, 2)
    input_grads = [
        grad_middle[s]
        + norm_back(first_norm[s][0], first_norm[s][1], grad_hidden_one[s] * (1.0 + mod[s, 1]))
        for s in streams
    ]

    total = lambda v: jnp.sum(v, axis=0)
    grad_mod = jnp.stack(
        [
            jnp.stack(
                [
                    total(grad_hidden_one[s]),
                    total(grad_hidden_one[s] * first_norm[s][0]),
                    total(branch_one[s] * grad_middle[s]),
                    total(grad_hidden_two[s]),
                    total(grad_hidden_two[s] * second_norm[s][0]),
                    total(branch_two[s] * grad_out[s]),
                ]
            )
            for s in streams
        ]
    )
    grad_mod = sum_bits(grad_mod, (lay.p,))
    grad_mod = gather_bits(grad_mod[None], t_up[1:])
    grad_mod = lax.dynamic_slice_in_dim(grad_mod, t_index * columns, columns, 3)
    grad_mod = gather_bits(grad_mod, dp_up)
    high = lax.Precision.HIGHEST
    ada_grad = jnp.einsum("sd,stkc->tdkc", silu_mine.astype(F32), grad_mod, precision=high)
    cond_terms = jnp.einsum("stkc,tdkc->sd", grad_mod, ada_weight.astype(F32), precision=high)
    cond_terms = gather_bits(sum_bits(cond_terms, t_up)[None], dp_up)
    cond_terms = lax.dynamic_slice_in_dim(cond_terms, dp_index * group_slots, group_slots, 1)
    cond_terms = jnp.swapaxes(cond_terms, 0, 1).reshape(group_slots, width)
    cond_terms = lax.dynamic_slice_in_dim(cond_terms, t_index * columns, columns, 1)
    cond_slice = lax.dynamic_slice_in_dim(condition.astype(F32), t_index * columns, columns, 1)
    unused, silu_pull = jax.vjp(jax.nn.silu, cond_slice)
    condition_grad = silu_pull(cond_terms)[0]
    ada_bias_grad = gather_bits(jnp.sum(grad_mod, axis=0)[None], t_up)
    ada_bias_grad = jnp.moveaxis(ada_bias_grad, 0, 2).reshape(2, 6, width)

    proj_bias_part = jnp.stack([total(grad_one[s].astype(F32)) for s in streams])
    down_bias_part = jnp.stack([total(grad_two[s].astype(F32)) for s in streams])
    own_part = sum_bits(jnp.stack([proj_bias_part, down_bias_part]), (lay.p, lay.q))
    heads = grad_qkv[0].shape[1] // 3
    qv_part = jnp.stack(
        [
            jnp.stack([total(grad_qkv[s][:, k * heads : (k + 1) * heads].astype(F32)) for k in (0, 2)])
            for s in streams
        ]
    )
    up_part = jnp.stack([total(grad_inner[s].astype(F32)) for s in streams])
    packed = jnp.concatenate([qv_part.reshape(-1), up_part.reshape(-1), own_part.reshape(-1)])
    packed = sum_bits(packed.reshape(-1, 128), lay.rest).reshape(-1)
    cut_one, cut_two = qv_part.size, qv_part.size + up_part.size
    qv_bias_grad = lay.all_columns(packed[:cut_one].reshape(qv_part.shape))
    up_bias_grad = lay.all_columns(packed[cut_one:cut_two].reshape(up_part.shape))
    own_part = packed[cut_two:].reshape(own_part.shape)
    return (
        outputs[0],
        outputs[1][:txt_rows],
        input_grads[0],
        input_grads[1][:txt_rows],
        condition_grad,
        ada_grad,
        ada_bias_grad,
        qkv_grad,
        qv_bias_grad,
        proj_grad,
        own_part[0],
        up_grad,
        up_bias_grad,
        down_grad,
        own_part[1],
    )


def solution(mesh):
    lay = Layout(mesh.shape["dp"], mesh.shape["tensor"])
    bits = Mesh(mesh.devices.reshape((2,) * len(lay.names)), lay.names)
    dp, tensor, every = lay.dp, lay.tensor, lay.names
    in_specs = (
        P(every, None),
        P(every, None),
        P(dp, None),
        P(dp),
        P(None, dp, None, tensor),
        P(),
        P(None, None, dp, tensor),
        P(),
        P(None, tensor, dp),
        P(),
        P(None, dp, tensor),
        P(),
        P(None, tensor, dp),
        P(),
        P(every, None),
        P(every, None),
    )
    out_specs = (
        P(every, None),
        P(every, None),
        P(every, None),
        P(every, None),
        P(dp, tensor),
        P(None, dp, None, tensor),
        P(),
        P(None, None, dp, tensor),
        P(),
        P(None, tensor, dp),
        P(),
        P(None, dp, tensor),
        P(),
        P(None, tensor, dp),
        P(),
    )
    return jax.shard_map(
        functools.partial(body, lay), mesh=bits, in_specs=in_specs, out_specs=out_specs, check_vma=False
    )
```

```python
import functools

import jax
import jax.numpy as jnp
from jax import lax
from jax.experimental import pallas as pl
from jax.experimental.pallas import tpu as pltpu
from jax.sharding import Mesh
from jax.sharding import PartitionSpec as P

HEAD_DIM = 64
SCALE = HEAD_DIM ** (-0.5)
BF = jnp.bfloat16
F32 = jnp.float32
NEG = -1e30


def swap(v, axis):
    return lax.ppermute(v, axis, [(0, 1), (1, 0)])


def gather_bits(v, axes):
    for axis in axes:
        other = swap(v, axis)
        first = lax.axis_index(axis) == 0
        v = jnp.concatenate([jnp.where(first, v, other), jnp.where(first, other, v)], 0)
    return v


def scatter_bits(v, axes):
    for axis in axes:
        first = lax.axis_index(axis) == 0
        half = v.shape[0] // 2
        low, high = v[:half], v[half:]
        v = jnp.where(first, low, high) + swap(jnp.where(first, high, low), axis)
    return v


def sum_bits(v, axes):
    for axis in axes:
        v = v + swap(v, axis)
    return v


def after(v, *deps):
    return lax.optimization_barrier((v,) + deps)[0]


def index_of(axes):
    out = 0
    for axis in axes:
        out = out * 2 + lax.axis_index(axis)
    return out


def nt(a, b):
    return lax.dot_general(a, b, (((1,), (1,)), ((), ())), preferred_element_type=F32)


def nn(a, b):
    return lax.dot_general(a, b, (((1,), (0,)), ((), ())), preferred_element_type=F32)


def tn(a, b):
    return lax.dot_general(a, b, (((0,), (0,)), ((), ())), preferred_element_type=F32)


VMEM_LIMIT = 52 * 2**20
GELU_C = 0.7978845608028654


def launch(kernel, grid, in_specs, out_specs, out_shape, args, name, flops, scratch=(), rides=(), cid=None):
    n_in, n_out = len(args), len(out_shape)
    params = dict(vmem_limit_bytes=VMEM_LIMIT)
    cost = pl.CostEstimate(flops=flops, bytes_accessed=flops // 512, transcendentals=0)
    if not rides:
        outs = pl.pallas_call(
            kernel,
            grid=grid,
            in_specs=in_specs,
            out_specs=out_specs,
            out_shape=out_shape,
            scratch_shapes=list(scratch),
            compiler_params=pltpu.CompilerParams(**params),
            cost_estimate=cost,
            name=name,
        )(*args)
        return list(outs), []
    partners = sorted({partner for ride in rides for partner in ride.partners})
    n_rides, sems = len(rides), sum(ride.sems for ride in rides)

    def body(*refs):
        ins, rest = refs[:n_in], refs[n_in:]
        sources, rest = rest[:n_rides], rest[n_rides:]
        outs, rest = rest[:n_out], rest[n_out:]
        targets, rest = rest[:n_rides], rest[n_rides:]
        own, (send, recv) = rest[:-2], rest[-2:]
        steps, at = [], 0
        for source, target, ride in zip(sources, targets, rides):
            steps.append(ride.moves(source, target, lambda k, at=at: send.at[at + k], lambda k, at=at: recv.at[at + k]))
            at += ride.sems

        @pl.when(pl.program_id(0) == 0)
        def _():
            barrier = pltpu.get_barrier_semaphore()
            for partner in partners:
                pl.semaphore_signal(
                    barrier,
                    1,
                    device_id={axis: 1 - lax.axis_index(axis) for axis in partner},
                    device_id_type=pl.DeviceIdType.MESH,
                )
            pl.semaphore_wait(barrier, len(partners))
            for start, unused in steps:
                start()

        kernel(*ins, *outs, *own)

        @pl.when(pl.program_id(0) == grid[0] - 1)
        def _():
            for unused, wait in steps:
                wait()

    anywhere = pl.BlockSpec(memory_space=pl.ANY)
    outs = pl.pallas_call(
        body,
        grid=grid,
        in_specs=list(in_specs) + [anywhere] * n_rides,
        out_specs=list(out_specs) + [anywhere] * n_rides,
        out_shape=list(out_shape) + [ride.shape for ride in rides],
        scratch_shapes=list(scratch)
        + [pltpu.SemaphoreType.DMA((sems,)), pltpu.SemaphoreType.DMA((sems,))],
        compiler_params=pltpu.CompilerParams(collective_id=cid, has_side_effects=True, **params),
        cost_estimate=cost,
        name=f"{name}_{cid}",
    )(*args, *[ride.array for ride in rides])
    return list(outs[:n_out]), list(outs[n_out:])


class NeighbourRide:
    def __init__(self, array, axis, shape, views, sems):
        self.array, self.axis, self.views, self.sems = array, axis, views, sems
        self.shape = jax.ShapeDtypeStruct(shape, array.dtype)
        self.partners = [(axis,)]

    def moves(self, source, target, send, recv):
        other = {self.axis: 1 - lax.axis_index(self.axis)}
        made = [
            pltpu.make_async_remote_copy(
                src_ref=src,
                dst_ref=dst,
                send_sem=send(k),
                recv_sem=recv(k),
                device_id=other,
                device_id_type=pl.DeviceIdType.MESH,
            )
            for k, (src, dst) in enumerate(self.views(source, target))
        ]

        def start():
            for move in made:
                move.start()

        def wait():
            for move in made:
                move.wait()

        return start, wait


def row_ride(array, axis, start, stop):
    views = lambda source, target: [(source.at[pl.ds(start, stop - start)], target)]
    return NeighbourRide(array, axis, (stop - start,) + array.shape[1:], views, 1)


class TradeRide:
    sems = 3

    def __init__(self, array, zh, q, back):
        self.array, self.zh, self.q, self.back = array, zh, q, back
        streams, part, n = array.shape[0], array.shape[-2], array.shape[-1]
        shape = (2, streams, part, n) if back else (streams, 2, part, n)
        self.shape = jax.ShapeDtypeStruct(shape, array.dtype)
        self.partners = [(q,), (zh,), (q, zh)]

    def moves(self, source, target, send, recv):
        zh, q = lax.axis_index(self.zh), lax.axis_index(self.q)
        same = zh == q

        def remote(k, src, dst, at, to_zh, to_q):
            return pltpu.make_async_remote_copy(
                src_ref=src,
                dst_ref=dst,
                send_sem=send(k),
                recv_sem=recv(at),
                device_id={self.zh: to_zh, self.q: to_q},
                device_id_type=pl.DeviceIdType.MESH,
            )

        if self.back:
            outgoing = [remote(j, source.at[:, j], target.at[zh], zh, q, j) for j in range(2)]
            arriving = [remote(j, source.at[:, j], target.at[j], j, q, j) for j in range(2)]
            local = pltpu.make_async_copy(source.at[:, q], target.at[zh], send(2))
            mine = [jnp.logical_and(same, q == j) for j in range(2)]
        else:
            outgoing = [remote(j, source, target.at[:, q], q, j, zh) for j in range(2)]
            arriving = [remote(j, source, target.at[:, j], j, j, zh) for j in range(2)]
            local = pltpu.make_async_copy(source, target.at[:, q], send(2))
            mine = [jnp.logical_and(same, zh == j) for j in range(2)]

        def start():
            for move, own in zip(outgoing, mine):
                pl.when(jnp.logical_not(own))(move.start)
            pl.when(same)(local.start)

        def wait():
            for move, own in zip(outgoing, mine):
                pl.when(jnp.logical_not(own))(move.wait_send)
            for move, own in zip(arriving, mine):
                pl.when(jnp.logical_not(own))(move.wait_recv)
            pl.when(same)(local.wait)

        return start, wait


def once(shape, index):
    return pl.BlockSpec(shape, index, pipeline_mode=pl.Buffered(1))


def by_stream(w):
    return [(w[0], 0), (w[1], 0)] if isinstance(w, (list, tuple)) else [(w, 0), (w, 1)]


def rows_nn_kernel(nb, img, mode, *refs):
    xs, w0, w1 = refs[:nb], refs[nb], refs[nb + 1]
    rest = refs[nb + 2 :]
    depth, tile = xs[0].shape[1], w0.shape[3]
    text = xs[0].shape[0] - img
    y_text = nn(
        jnp.concatenate([x[img:, :] for x in xs], axis=0), w1[:, 0].reshape(depth, tile)
    )
    w_img = w0[:, 0].reshape(depth, tile)
    if mode == "slope":
        sums = rest[2 * nb]
        total = [jnp.zeros((1, tile), F32), jnp.zeros((1, tile), F32)]
    for b in range(nb):
        for stream, rows in ((0, slice(0, img)), (1, slice(img, img + text))):
            y = nn(xs[b][rows, :], w_img) if stream == 0 else y_text[b * text : (b + 1) * text]
            if mode == "plain":
                rest[b][rows, :] = y.astype(BF)
            elif mode == "bias":
                rest[1 + b][rows, :] = (y + rest[0][stream]).astype(BF)
            elif mode == "gelu":
                v = y + rest[0][stream]
                inner = jnp.tanh(GELU_C * (v + 0.044715 * (v * v * v)))
                half = 0.5 * (1.0 + inner)
                rest[1 + b][rows, :] = (v * half).astype(BF)
                rest[1 + nb + b][rows, :] = half + 0.5 * v * (1.0 - inner * inner) * (
                    GELU_C * (1.0 + 3 * 0.044715 * (v * v))
                )
            else:
                y = (y * rest[b][rows, :]).astype(BF)
                rest[nb + b][rows, :] = y
                total[stream] += jnp.sum(y.astype(F32), axis=0, keepdims=True)
    if mode == "slope":
        sums[0] = total[0]
        sums[1] = total[1]


def rows_nn(xs, w, img, mode, bias=None, slopes=(), tile=384, rides=(), cid=None):
    (w0, s0), (w1, s1) = by_stream(w)
    n = w0.shape[3]
    nb, (rows, depth) = len(xs), xs[0].shape
    in_specs = [once((rows, depth), lambda j: (0, 0))] * nb
    in_specs += [
        pl.BlockSpec((4, 1, depth // 4, tile), lambda j, at=at: (0, at, 0, j)) for at in (s0, s1)
    ]
    args = list(xs) + [w0, w1]
    out_tile = pl.BlockSpec((rows, tile), lambda j: (0, j))
    vector = pl.BlockSpec((2, 1, tile), lambda j: (0, 0, j))
    shape = lambda dtype: jax.ShapeDtypeStruct((rows, n), dtype)
    if bias is not None:
        in_specs.append(vector)
        args.append(bias.reshape(2, 1, n))
    in_specs += [out_tile] * len(slopes)
    args += list(slopes)
    out_specs, out_shape = [out_tile] * nb, [shape(BF)] * nb
    if mode == "gelu":
        out_specs, out_shape = out_specs + [out_tile] * nb, out_shape + [shape(F32)] * nb
    if mode == "slope":
        out_specs.append(vector)
        out_shape.append(jax.ShapeDtypeStruct((2, 1, n), F32))
    return launch(
        functools.partial(rows_nn_kernel, nb, img, mode),
        (n // tile,),
        in_specs,
        out_specs,
        out_shape,
        args,
        f"rows_{mode}",
        2 * nb * rows * depth * n,
        rides=rides,
        cid=cid,
    )


def rows_nt_kernel(nb, img, *refs):
    xs, w0, w1, outs = refs[:nb], refs[nb], refs[nb + 1], refs[nb + 2 :]
    text = xs[0].shape[0] - img
    y_text = nt(jnp.concatenate([x[img:, :] for x in xs], axis=0), w1[0, 0])
    w_img = w0[0, 0]
    for b in range(nb):
        outs[b][:img, :] = nt(xs[b][:img, :], w_img).astype(outs[b].dtype)
        outs[b][img:, :] = y_text[b * text : (b + 1) * text].astype(outs[b].dtype)


def rows_nt(xs, w, img, dtypes, rides=(), cid=None):
    nb, (rows, n) = len(xs), xs[0].shape
    (w0, s0), (w1, s1) = by_stream(w)
    quarter = w0.shape[2]
    return launch(
        functools.partial(rows_nt_kernel, nb, img),
        (4,),
        [once((rows, n), lambda j: (0, 0))] * nb
        + [
            pl.BlockSpec((1, 1, quarter, n), lambda j, at=at: (j, at, 0, 0)) for at in (s0, s1)
        ],
        [pl.BlockSpec((rows, quarter), lambda j: (0, j))] * nb,
        [jax.ShapeDtypeStruct((rows, 4 * quarter), t) for t in dtypes],
        list(xs) + [w0, w1],
        "rows_back",
        8 * nb * rows * quarter * n,
        rides=rides,
        cid=cid,
    )


def weight_grad_kernel(nb, img, *refs):
    xs, ys, out = refs[:nb], refs[nb : 2 * nb], refs[2 * nb]
    total = tn(xs[0][:img, :], ys[0][:img, :])
    for b in range(1, nb):
        total += tn(xs[b][:img, :], ys[b][:img, :])
    out[0, 0] = total.astype(BF)
    x_text = jnp.concatenate([x[img:, :] for x in xs], axis=0)
    y_text = jnp.concatenate([y[img:, :] for y in ys], axis=0)
    out[0, 1] = tn(x_text, y_text).astype(BF)


def weight_grad(xs, ys, img, rides=(), cid=None):
    nb, (rows, d), n = len(xs), xs[0].shape, ys[0].shape[1]
    (out,), rode = launch(
        functools.partial(weight_grad_kernel, nb, img),
        (4,),
        [pl.BlockSpec((rows, d // 4), lambda j: (0, j))] * nb
        + [once((rows, n), lambda j: (0, 0))] * nb,
        [pl.BlockSpec((1, 2, d // 4, n), lambda j: (j, 0, 0, 0))],
        [jax.ShapeDtypeStruct((4, 2, d // 4, n), BF)],
        list(xs) + list(ys),
        "weight_grad",
        2 * nb * rows * d * n,
        rides=rides,
        cid=cid,
    )
    return out, rode


def pad_key(position, padded, real):
    return lax.rem(position, padded) >= real


def head_of(refs, img, h):
    cols = slice(h * HEAD_DIM, (h + 1) * HEAD_DIM)
    whole = [r[...] for r in refs]
    return (
        jnp.concatenate([w[:img, cols] for w in whole], axis=0),
        jnp.concatenate([w[img:, cols] for w in whole], axis=0),
    )


def attend_kernel(chunk, img, txt, q0, k0, v0, q1, k1, v1, o0, o1, lse_i, lse_t):
    per = img // chunk
    tp = q0.shape[0] - img
    keys = [head_of((k0, k1), img, h) for h in range(2)]
    vals = [head_of((v0, v1), img, h) for h in range(2)]
    mask = jnp.where(
        pad_key(lax.broadcasted_iota(jnp.int32, (1, 2 * tp), 1), tp, txt), NEG, 0.0
    ).astype(F32)

    def one(q_pair):
        outs, logs = [], []
        for h in range(2):
            q = q_pair[:, h * HEAD_DIM : (h + 1) * HEAD_DIM] * jnp.asarray(SCALE, BF)
            s_i = nt(q, keys[h][0])
            s_t = nt(q, keys[h][1]) + mask
            top = jnp.maximum(
                jnp.max(s_i, axis=1, keepdims=True), jnp.max(s_t, axis=1, keepdims=True)
            )
            p_i = jnp.exp(s_i - top)
            p_t = jnp.exp(s_t - top)
            total = jnp.sum(p_i, axis=1, keepdims=True) + jnp.sum(p_t, axis=1, keepdims=True)
            inv = 1.0 / total
            o = nn((p_i * inv).astype(BF), vals[h][0]) + nn((p_t * inv).astype(BF), vals[h][1])
            outs.append(o.astype(BF))
            logs.append((top + jnp.log(total)).reshape(1, -1))
        return jnp.concatenate(outs, axis=1), logs

    for z, (q_ref, o_ref) in enumerate(((q0, o0), (q1, o1))):

        def step(c, carry, z=z, q_ref=q_ref, o_ref=o_ref):
            r = pl.multiple_of(c * chunk, chunk)
            o, logs = one(q_ref[pl.ds(r, chunk), :])
            o_ref[pl.ds(r, chunk), :] = o
            for h in range(2):
                lse_i[0, h, pl.ds(z * per + c, 1), :] = logs[h]
            return carry

        lax.fori_loop(0, per, step, 0)
    o, logs = one(jnp.concatenate([q0[img:, :], q1[img:, :]], axis=0))
    o0[img:, :] = o[:tp]
    o1[img:, :] = o[tp:]
    for h in range(2):
        lse_t[0, h, 0:1, :] = logs[h]


def attend_back_kernel(
    chunk, img, txt, q0, k0, v0, q1, k1, v1, g0, g1, lse_i, lse_t, d0, d1, sums, dk_i, dv_i, dk_t, dv_t
):
    per = img // chunk
    tp = q0.shape[0] - img
    hp = pl.program_id(0)
    pairs = pl.num_programs(0)
    width = 2 * HEAD_DIM
    keys = [head_of((k0, k1), img, h) for h in range(2)]
    vals = [head_of((v0, v1), img, h) for h in range(2)]
    mask = jnp.where(
        pad_key(lax.broadcasted_iota(jnp.int32, (2 * tp, 1), 0), tp, txt), NEG, 0.0
    ).astype(F32)
    dk_i[...] = jnp.zeros_like(dk_i)
    dv_i[...] = jnp.zeros_like(dv_i)
    dk_t[...] = jnp.zeros_like(dk_t)
    dv_t[...] = jnp.zeros_like(dv_t)

    def one(q_pair, g_pair, logs):
        outs = []
        for h in range(2):
            cols = slice(h * HEAD_DIM, (h + 1) * HEAD_DIM)
            q = q_pair[:, cols] * jnp.asarray(SCALE, BF)
            g = g_pair[:, cols]
            p_i = jnp.exp(nt(keys[h][0], q) - logs[h])
            p_t = jnp.exp(nt(keys[h][1], q) + mask - logs[h])
            dp_i = nt(vals[h][0], g)
            dp_t = nt(vals[h][1], g)
            delta = jnp.sum(p_i * dp_i, axis=0, keepdims=True) + jnp.sum(
                p_t * dp_t, axis=0, keepdims=True
            )
            dv_i[h] += nn(p_i.astype(BF), g)
            dv_t[h] += nn(p_t.astype(BF), g)
            ds_i = (p_i * (dp_i - delta)).astype(BF)
            ds_t = (p_t * (dp_t - delta)).astype(BF)
            dk_i[h] += nn(ds_i, q)
            dk_t[h] += nn(ds_t, q)
            dq = tn(ds_i, keys[h][0]) + tn(ds_t, keys[h][1])
            outs.append((dq * SCALE).astype(BF))
        return jnp.concatenate(outs, axis=1)

    def cols_of(kind):
        return pl.ds(pl.multiple_of((kind * pairs + hp) * width, width), width)

    def column_sum(v):
        return jnp.sum(v.astype(F32), axis=0, keepdims=True)

    q_sum = jnp.zeros((1, width), F32)
    for z, (q_ref, g_ref, d_ref) in enumerate(((q0, g0, d0), (q1, g1, d1))):

        def step(c, total, z=z, q_ref=q_ref, g_ref=g_ref, d_ref=d_ref):
            r = pl.multiple_of(c * chunk, chunk)
            logs = [lse_i[0, h, pl.ds(z * per + c, 1), :] for h in range(2)]
            dq = one(q_ref[pl.ds(r, chunk), :], g_ref[pl.ds(r, chunk), :], logs)
            d_ref[pl.ds(r, chunk), cols_of(0)] = dq
            return total + column_sum(dq)

        q_sum = lax.fori_loop(0, per, step, q_sum)
    logs = [lse_t[0, h, 0:1, :] for h in range(2)]
    dq = one(
        jnp.concatenate([q0[img:, :], q1[img:, :]], axis=0),
        jnp.concatenate([g0[img:, :], g1[img:, :]], axis=0),
        logs,
    )
    d0[img:, cols_of(0)] = dq[:tp]
    d1[img:, cols_of(0)] = dq[tp:]
    sums[0, 0:1] = q_sum
    sums[0, 1:2] = column_sum(dq)
    for kind, image, text in ((1, dk_i, dk_t), (2, dv_i, dv_t)):
        both = jnp.concatenate([image[0].astype(BF), image[1].astype(BF)], axis=1)
        d0[:img, cols_of(kind)] = both[:img]
        d1[:img, cols_of(kind)] = both[img:]
        both_t = jnp.concatenate([text[0].astype(BF), text[1].astype(BF)], axis=1)
        d0[img:, cols_of(kind)] = both_t[:tp]
        d1[img:, cols_of(kind)] = both_t[tp:]
        if kind == 2:
            sums[0, 2:3] = column_sum(both)
            sums[0, 3:4] = column_sum(both_t)


def qkv_specs(rows, pairs):
    width = 2 * HEAD_DIM
    return [
        pl.BlockSpec((rows, width), lambda h, kind=kind: (0, kind * pairs + h)) for kind in range(3)
    ] * 2


def lse_specs(n_chunks, chunk, tp):
    return [
        pl.BlockSpec((1, 2, n_chunks, chunk), lambda h: (h, 0, 0, 0)),
        pl.BlockSpec((1, 2, 1, 2 * tp), lambda h: (h, 0, 0, 0)),
    ]


def attention(near, far, img, txt, chunk, slot, rides=(), cid=None):
    rows, columns = near.shape[0], near.shape[1] // 3
    tp, width = rows - img, 2 * HEAD_DIM
    pairs, n_chunks = columns // width, 2 * img // chunk
    tile = pl.BlockSpec((rows, width), lambda h: (0, h))
    return launch(
        functools.partial(attend_kernel, chunk, img, txt),
        (pairs,),
        qkv_specs(rows, pairs),
        [tile, tile] + lse_specs(n_chunks, chunk, tp),
        [jax.ShapeDtypeStruct((rows, columns), BF)] * 2
        + [
            jax.ShapeDtypeStruct((pairs, 2, n_chunks, chunk), F32),
            jax.ShapeDtypeStruct((pairs, 2, 1, 2 * tp), F32),
        ],
        [near, near, near, far, far, far],
        f"attend_{slot}",
        80 * pairs * rows * rows * HEAD_DIM,
        rides=rides,
        cid=cid,
    )


def attention_back(
    near, far, grad_near, grad_far, lse_i, lse_t, img, txt, chunk, slot, rides=(), cid=None
):
    rows, columns = near.shape[0], near.shape[1] // 3
    tp, width = rows - img, 2 * HEAD_DIM
    pairs, n_chunks = columns // width, 2 * img // chunk
    tile = pl.BlockSpec((rows, width), lambda h: (0, h))
    whole = pl.BlockSpec((rows, 3 * columns), lambda h: (0, 0))
    return launch(
        functools.partial(attend_back_kernel, chunk, img, txt),
        (pairs,),
        qkv_specs(rows, pairs) + [tile, tile] + lse_specs(n_chunks, chunk, tp),
        [whole, whole, pl.BlockSpec((1, 4, width), lambda h: (h, 0, 0))],
        [jax.ShapeDtypeStruct((rows, 3 * columns), BF)] * 2
        + [jax.ShapeDtypeStruct((pairs, 4, width), F32)],
        [near, near, near, far, far, far, grad_near, grad_far, lse_i, lse_t],
        f"attend_back_{slot}",
        200 * pairs * rows * rows * HEAD_DIM,
        scratch=[
            pltpu.VMEM((2, 2 * img, HEAD_DIM), F32),
            pltpu.VMEM((2, 2 * img, HEAD_DIM), F32),
            pltpu.VMEM((2, 2 * tp, HEAD_DIM), F32),
            pltpu.VMEM((2, 2 * tp, HEAD_DIM), F32),
        ],
        rides=rides,
        cid=cid,
    )


class Layout:
    def __init__(self, dp_size, tensor_size):
        dp_bits = dp_size.bit_length() - 1
        t_bits = tensor_size.bit_length() - 1
        self.dp = tuple(f"d{i}" for i in range(dp_bits))
        self.tensor = tuple(f"t{i}" for i in range(t_bits))
        self.names = self.dp + self.tensor
        self.compact = dp_size == 8 and tensor_size == 4
        self.p = self.tensor[-1]
        if self.compact:
            self.y, self.x, self.q = self.dp
            self.zh = self.tensor[0]
            self.upper = ()
        else:
            self.q = self.tensor[-2]
            self.upper = self.tensor[:-2]
        self.rest = tuple(n for n in self.names if n not in (self.p, self.q))

    def my_columns(self, v):
        shards = 2 ** len(self.upper)
        part = v.shape[-1] // (4 * shards)
        v = v.reshape(v.shape[:-1] + (shards, 4, part))
        at = index_of((self.q, self.p))
        v = lax.dynamic_index_in_dim(v, at, v.ndim - 2, keepdims=False)
        return v.reshape(v.shape[:-2] + (shards * part,))

    def all_columns(self, v):
        shards = 2 ** len(self.upper)
        g = gather_bits(v[None], (self.p, self.q))
        g = g.reshape((4,) + v.shape[:-1] + (shards, v.shape[-1] // shards))
        g = jnp.moveaxis(g, 0, -2)
        return g.reshape(v.shape[:-1] + (4 * v.shape[-1],))

    def gather_rows(self, own, end=()):
        pair = after(swap(own, self.p), *end)
        return [[own, swap(own, self.q)], [pair, swap(pair, self.q)]]

    def sum_far(self, w, blocks, img):
        (send, keep), unused = rows_nt([blocks[1][1], blocks[1][0]], w, img, (BF, F32))
        return (keep + swap(send, self.q).astype(F32)).astype(BF)

    def sum_near(self, w, blocks, img, rides=(), cid=None):
        (send, keep), rode = rows_nt([blocks[0][1], blocks[0][0]], w, img, (BF, F32), rides, cid)
        return keep + swap(send, self.q).astype(F32), rode

    def gather_weight(self, w):
        w = lax.all_gather(w, self.dp, axis=1, tiled=True)
        if self.upper:
            w = lax.all_gather(w, self.upper, axis=3, tiled=True)
        return jnp.swapaxes(w.reshape(2, 4, w.shape[1] // 4, -1), 0, 1)

    def trade_shards(self, w, end=()):
        w = w.reshape(w.shape[0], w.shape[1], -1)
        joint = (self.q, self.zh)
        same = lax.axis_index(self.zh) == lax.axis_index(self.q)
        cross = lax.ppermute(w, joint, [(1, 2), (2, 1)])
        second = lax.ppermute(w, joint, [(0, 1), (3, 2), (2, 0), (1, 3)])
        cross, second = after((cross, second), *end)
        first = jnp.where(same, w, cross)
        low = lax.axis_index(self.zh) == 0
        return jnp.concatenate(
            [jnp.where(low, first, second), jnp.where(low, second, first)], axis=1
        )

    def spread_near(self, own):
        return [swap(own[0], self.x), swap(own[1], self.y)]

    def spread_rows(self, own, nears):
        x, y = lax.axis_index(self.x), lax.axis_index(self.y)
        whole = jnp.zeros((4,) + own.shape, BF)
        for stream, far_axis in enumerate((self.y, self.x)):
            mine, near = own[stream], nears[stream]
            both, far = swap(near, far_axis), swap(mine, far_axis)
            dx, dy = (near, far) if stream == 0 else (far, near)
            for block, at in (
                (mine, 2 * y + x),
                (dx, 2 * y + 1 - x),
                (dy, 2 * (1 - y) + x),
                (both, 2 * (1 - y) + 1 - x),
            ):
                whole = lax.dynamic_update_slice(whole, block[None, None], (at, stream, 0, 0))
        return whole

    def spread_rows_async(self, own):
        own = own.reshape(own.shape[0], -1, own.shape[-1])
        return lax.all_gather(own, (self.y, self.x), axis=0, tiled=False)

    def trade_ride(self, array, back=False):
        if back:
            array = array.reshape(2, 2, -1, array.shape[-1])
        return TradeRide(array, self.zh, self.q, back)

    def scatter_generic(self, g, kinds):
        g = jnp.swapaxes(g.astype(F32), 0, 1).reshape(2, 4 * g.shape[2], kinds, -1)
        g = lax.psum_scatter(g, self.dp, scatter_dimension=1, tiled=True)
        if self.upper:
            g = lax.psum_scatter(g, self.upper, scatter_dimension=3, tiled=True)
        return g

    def sum_plane_async(self, g):
        return lax.psum_scatter(g, (self.y, self.x), scatter_dimension=0, tiled=False)

    def plane_rides(self, g):
        g = g.reshape((2, 2) + g.shape[1:])
        shape = (2,) + g.shape[3:]

        def along_x(source, target):
            x = 1 - lax.axis_index(self.x)
            return [(source.at[k, x, 0], target.at[k]) for k in range(2)]

        def along_y(source, target):
            y = 1 - lax.axis_index(self.y)
            return [(source.at[y, k, 1], target.at[k]) for k in range(2)]

        return [
            NeighbourRide(g, self.x, shape, along_x, 2),
            NeighbourRide(g, self.y, shape, along_y, 2),
        ]

    def sum_plane(self, g, arrived):
        x, y = lax.axis_index(self.x), lax.axis_index(self.y)
        pick = lambda v, i, dim: lax.dynamic_index_in_dim(v, i, dim, keepdims=False)
        g = g.reshape((2, 2) + g.shape[1:])
        done = []
        for stream in range(2):
            near, dim, far_axis, far = ((x, 1, self.y, y), (y, 0, self.x, x))[stream]
            v = pick(g[:, :, stream], near, dim).astype(F32) + arrived[stream].astype(F32)
            v = pick(v, far, 0) + swap(pick(v, 1 - far, 0).astype(BF), far_axis).astype(F32)
            done.append(v)
        return jnp.stack(done)

    def trade_sums(self, g, kinds, end=()):
        g = g.reshape(2, 2, -1, g.shape[2])
        zh = lax.axis_index(self.zh)
        joint = (self.q, self.zh)
        first = lax.dynamic_index_in_dim(g, zh, 1, keepdims=False)
        second = lax.dynamic_index_in_dim(g, 1 - zh, 1, keepdims=False)
        cross = lax.ppermute(first.astype(BF), joint, [(1, 2), (2, 1)])
        second = lax.ppermute(second.astype(BF), joint, [(1, 0), (2, 3), (0, 2), (3, 1)])
        cross, second = after((cross, second), *end)
        same = zh == lax.axis_index(self.q)
        total = jnp.where(same, first.astype(F32), cross.astype(F32)) + second.astype(F32)
        return total.reshape(2, total.shape[1], kinds, -1)


def norm_parts(values):
    average = jnp.mean(values, axis=-1, keepdims=True)
    centred = values - average
    variance = jnp.mean(centred * centred, axis=-1, keepdims=True)
    inverse = lax.rsqrt(variance + 1e-06)
    return centred * inverse, inverse


def norm_back(normed, inverse, grad_in):
    first_mean = jnp.mean(grad_in, axis=-1, keepdims=True)
    cross_mean = jnp.mean(grad_in * normed, axis=-1, keepdims=True)
    return inverse * (grad_in - first_mean - normed * cross_mean)


def body(
    lay,
    image_in,
    text_in,
    condition,
    live_slots,
    ada_weight,
    ada_bias,
    qkv_weight,
    qv_bias,
    proj_weight,
    proj_bias,
    up_weight,
    up_bias,
    down_weight,
    down_bias,
    image_grad,
    text_grad,
):
    width = image_in.shape[1]
    part = qkv_weight.shape[2]
    columns = qkv_weight.shape[3]
    img_rows, txt_rows = image_in.shape[0], text_in.shape[0]
    txt_pad = -(-txt_rows // 16) * 16
    group_slots = condition.shape[0]
    dp_index, t_index = index_of(lay.dp), index_of(lay.tensor)
    t_count = 2 ** len(lay.tensor)
    assert group_slots * 2 == t_count
    my_slot = t_index // 2
    dp_up, t_up = lay.dp[::-1], lay.tensor[::-1]

    rows = img_rows + txt_pad
    is_image = lax.broadcasted_iota(jnp.int32, (rows, 1), 0) < img_rows

    def pack(image, text):
        return jnp.concatenate([image, jnp.pad(text, ((0, txt_pad - txt_rows), (0, 0)))], axis=0)

    def spread(per_stream):
        return jnp.where(is_image, per_stream[0], per_stream[1])

    def total(v):
        return jnp.stack([jnp.sum(v[:img_rows], axis=0), jnp.sum(v[img_rows:], axis=0)])

    def flat(blocks):
        return blocks[0] + blocks[1]

    def unflat(v):
        return [list(v[:2]), list(v[2:4])]

    qkv_local = jnp.swapaxes(qkv_weight, 1, 2)
    proj_local = jnp.swapaxes(proj_weight, 1, 2)[:, :, None]
    up_local = up_weight[:, :, None]
    down_local = jnp.swapaxes(down_weight, 1, 2)[:, :, None]
    compact = lay.compact
    if compact:
        qkv_own = lay.trade_shards(qkv_local)
        qkv_near = lay.spread_near(qkv_own)
    else:
        qkv_full, up_full, proj_full, down_full = [
            lay.gather_weight(w) for w in (qkv_local, up_local, proj_local, down_local)
        ]

    cond_all = gather_bits(condition, dp_up).astype(F32)
    silu_all = jax.nn.silu(cond_all).astype(BF)
    silu_mine = lax.dynamic_slice_in_dim(silu_all, dp_index * part, part, 1)
    mod = jnp.einsum("sd,tdkc->stkc", silu_mine, ada_weight, preferred_element_type=F32)
    mod = scatter_bits(mod, lay.dp)
    if compact:
        mod = after(mod, qkv_own)
    mod = gather_bits(mod[None], t_up)
    mod = lax.dynamic_index_in_dim(mod, my_slot, 1, keepdims=False)
    mod = jnp.moveaxis(mod, 0, 2).reshape(2, 6, width) + ada_bias.astype(F32)
    live = lax.dynamic_index_in_dim(live_slots, my_slot, 0, keepdims=False).astype(F32)

    mods = [spread(mod[:, k]) for k in range(6)]
    shift_one, scale_one, gate_one, shift_two, scale_two, gate_two = mods

    inputs = pack(image_in, text_in).astype(F32)
    grad_out = live * pack(image_grad, text_grad).astype(F32)
    grad_two = (gate_two * grad_out).astype(BF)

    first_norm = norm_parts(inputs)
    first_hidden = (first_norm[0] * (1.0 + scale_one) + shift_one).astype(BF)
    if compact:
        first_hidden = after(first_hidden, qkv_near)
    first = lay.gather_rows(first_hidden)
    if compact:
        qkv_full = lay.spread_rows(qkv_own, qkv_near)
    qv = lay.my_columns(qv_bias.astype(F32))
    qkv_bias = jnp.concatenate([qv[:, 0], jnp.zeros_like(qv[:, 0]), qv[:, 1]], axis=1)
    heads_n = qv.shape[2]
    img = img_rows

    def ride(array, start, stop):
        return row_ride(array, lay.p, start, stop)

    def thirds(n):
        return [0] + [n * k // 3 // 16 * 16 for k in (1, 2)] + [n]

    cut = thirds(rows)
    rides = [ride(grad_two, cut[k], cut[k + 1]) for k in range(3)]
    extra = [[], [], []]
    if compact:
        extra = [
            [lay.trade_ride(w.reshape(w.shape[0], part, -1))]
            for w in (proj_local, up_local[:1], up_local[1:])
        ]
    qkv, rode = rows_nn(
        flat(first), qkv_full, img, "bias", bias=qkv_bias, rides=[rides[0]] + extra[0], cid=1
    )
    grad_two_pair = rode[:1]
    qkv = unflat(qkv)
    chunk = min(256, img_rows)
    if compact:
        proj_full = lay.spread_rows_async(rode[1])
    other, rode = attention(
        qkv[0][1], qkv[1][1], img, txt_rows, chunk, 1, rides=[rides[1]] + extra[1], cid=2
    )
    grad_two_pair += rode[:1]
    if compact:
        up_full = [lay.spread_rows_async(rode[1])]
        qkv, other = after((qkv, other), proj_full)
    mine, rode = attention(
        qkv[0][0], qkv[1][0], img, txt_rows, chunk, 0, rides=[rides[2]] + extra[2], cid=10
    )
    grad_two_pair = jnp.concatenate(grad_two_pair + rode[:1], axis=0)
    heads_out = [[mine[z], other[z]] for z in range(2)]
    grad_two_blocks = [
        [grad_two, swap(grad_two, lay.q)], [grad_two_pair, swap(grad_two_pair, lay.q)]
    ]
    if compact:
        up_full.append(lay.spread_rows_async(rode[1]))
        down_local = after(down_local, mine)

    far = swap(lay.sum_far(proj_full, heads_out, img), lay.p)
    near, unused = lay.sum_near(proj_full, heads_out, img)
    branch_one = near + far.astype(F32) + spread(proj_bias.astype(F32))
    middle = inputs + gate_one * branch_one
    second_norm = norm_parts(middle)
    second_hidden = (second_norm[0] * (1.0 + scale_two) + shift_two).astype(BF)
    if compact:
        down_own = lay.trade_shards(down_local, (second_hidden,))
        down_full = lay.spread_rows_async(down_own)
    second = lay.gather_rows(second_hidden)
    up_mine = lay.my_columns(up_bias.astype(F32))
    up_n = up_mine.shape[1]
    up_out, unused = rows_nn(flat(second), up_full, img, "gelu", bias=up_mine)
    activated, slopes = up_out[:4], up_out[4:]
    far = lay.sum_far(down_full, unflat(activated), img)
    cut = rows * 21 // 37 // 16 * 16
    back_out, rode = rows_nn(
        flat(grad_two_blocks), down_full, img, "slope", slopes=slopes, rides=[ride(far, 0, cut)], cid=3
    )
    grad_inner, up_part = back_out[:4], back_out[4].reshape(2, up_n)
    down_grads, rode_two = weight_grad(
        after(flat(grad_two_blocks), grad_inner), activated, img, rides=[ride(far, cut, rows)], cid=4
    )
    far = jnp.concatenate(rode + rode_two, axis=0)
    if compact:
        down_plane = lay.sum_plane_async(down_grads)
    far_two = lay.sum_far(up_full, after(unflat(grad_inner), down_grads), img)
    cut, cut_two = rows * 11 // 37 // 16 * 16, rows * 22 // 37 // 16 * 16
    near_two, rode = lay.sum_near(up_full, unflat(grad_inner), img, [ride(far_two, 0, cut)], 5)
    up_grads, rode_two = weight_grad(
        after(flat(second), near_two), grad_inner, img, rides=[ride(far_two, cut_two, rows)], cid=6
    )
    if compact:
        up_plane = lay.sum_plane_async(up_grads)
    near, rode_three = lay.sum_near(
        down_full, after(unflat(activated), up_grads), img, [ride(far_two, cut, cut_two)], 7
    )
    far_two = jnp.concatenate(rode + rode_three + rode_two, axis=0)
    branch_two = near + far.astype(F32) + spread(down_bias.astype(F32))
    outputs = (live * (middle + gate_two * branch_two)).astype(BF)
    grad_hidden_two = near_two + far_two.astype(F32)
    grad_middle = grad_out + norm_back(
        second_norm[0], second_norm[1], grad_hidden_two * (1.0 + scale_two)
    )
    grad_one = (gate_one * grad_middle).astype(BF)
    if compact:
        grad_one = after(grad_one, down_plane)
    grad_one_blocks = lay.gather_rows(grad_one)
    grad_heads = unflat(rows_nn(flat(grad_one_blocks), proj_full, img, "plain")[0])

    def back(c, saved, heads, rides, cid):
        return attention_back(
            qkv[0][c],
            qkv[1][c],
            heads[0][c],
            heads[1][c],
            saved[2],
            saved[3],
            img,
            txt_rows,
            chunk,
            c,
            rides,
            cid,
        )

    grad_other, down_sums = back(
        1, other, grad_heads, [lay.trade_ride(down_plane, True)] if compact else (), 11
    )
    proj_grads, unused = weight_grad(
        after(flat(grad_one_blocks), grad_other), flat(heads_out), img
    )
    if compact:
        proj_plane = lay.sum_plane_async(proj_grads)
    grad_mine, up_sums = back(
        0,
        mine,
        after(grad_heads, proj_grads),
        [lay.trade_ride(up_plane, True)] if compact else (),
        12,
    )
    grad_qkv = [[grad_mine[z], grad_other[z]] for z in range(2)]
    far = lay.sum_far(qkv_full, grad_qkv, img)
    cut = rows * 20 // 37 // 16 * 16
    qkv_grads, rode = weight_grad(
        flat(first), flat(grad_qkv), img, rides=[ride(far, 0, cut)], cid=8
    )
    rides = [ride(far, cut, rows)]
    if compact:
        rides += lay.plane_rides(qkv_grads) + [lay.trade_ride(proj_plane, True)]
    near, rode_two = lay.sum_near(qkv_full, after(grad_qkv, qkv_grads), img, rides, 9)
    far = jnp.concatenate(rode + rode_two[:1], axis=0)
    if compact:
        down_grad, up_grad, proj_grad = [
            (v[0].astype(F32) + v[1].astype(F32))[:, :, None]
            for v in (down_sums[0], up_sums[0], rode_two[3])
        ]
        qkv_plane = lay.sum_plane(qkv_grads, rode_two[1:3])
    else:
        down_grad, up_grad, proj_grad = [
            lay.scatter_generic(g, 1) for g in (down_grads, up_grads, proj_grads)
        ]
        qkv_grad = lay.scatter_generic(qkv_grads, 3)
    grad_hidden_one = near + far.astype(F32)
    input_grads = grad_middle + norm_back(
        first_norm[0], first_norm[1], grad_hidden_one * (1.0 + scale_one)
    )

    grad_mod = jnp.stack(
        [
            total(grad_hidden_one),
            total(grad_hidden_one * first_norm[0]),
            total(branch_one * grad_middle),
            total(grad_hidden_two),
            total(grad_hidden_two * second_norm[0]),
            total(branch_two * grad_out),
        ],
        axis=1,
    )
    grad_mod = sum_bits(grad_mod, (lay.p,))
    grad_mod = gather_bits(grad_mod[None], t_up[1:])
    if compact:
        qkv_grad = lay.trade_sums(after(qkv_plane, grad_mod), 3)
    down_grad = jnp.swapaxes(down_grad[:, :, 0], 1, 2)
    proj_grad = jnp.swapaxes(proj_grad[:, :, 0], 1, 2)
    up_grad = up_grad[:, :, 0]
    qkv_grad = jnp.swapaxes(qkv_grad, 1, 2)
    grad_mod = lax.dynamic_slice_in_dim(grad_mod, t_index * columns, columns, 3)
    grad_mod = gather_bits(grad_mod, dp_up)
    high = lax.Precision.HIGHEST
    ada_grad = jnp.einsum("sd,stkc->tdkc", silu_mine.astype(F32), grad_mod, precision=high)
    cond_terms = jnp.einsum("stkc,tdkc->sd", grad_mod, ada_weight.astype(F32), precision=high)
    cond_terms = gather_bits(sum_bits(cond_terms, t_up)[None], dp_up)
    cond_terms = lax.dynamic_slice_in_dim(cond_terms, dp_index * group_slots, group_slots, 1)
    cond_terms = jnp.swapaxes(cond_terms, 0, 1).reshape(group_slots, width)
    cond_terms = lax.dynamic_slice_in_dim(cond_terms, t_index * columns, columns, 1)
    cond_slice = lax.dynamic_slice_in_dim(condition.astype(F32), t_index * columns, columns, 1)
    unused, silu_pull = jax.vjp(jax.nn.silu, cond_slice)
    condition_grad = silu_pull(cond_terms)[0]
    ada_bias_grad = gather_bits(jnp.sum(grad_mod, axis=0)[None], t_up)
    ada_bias_grad = jnp.moveaxis(ada_bias_grad, 0, 2).reshape(2, 6, width)

    own_part = sum_bits(
        jnp.stack([total(grad_one.astype(F32)), total(grad_two.astype(F32))]), (lay.p, lay.q)
    )
    sums = grad_mine[2] + grad_other[2]
    pairs = sums.shape[0]
    qv_part = jnp.transpose(sums.reshape(pairs, 2, 2, -1), (2, 1, 0, 3)).reshape(2, 2, heads_n)
    if compact:
        qv_part = after(qv_part, near)
    packed = jnp.concatenate([qv_part.reshape(-1), up_part.reshape(-1), own_part.reshape(-1)])
    packed = sum_bits(packed.reshape(-1, 128), lay.rest).reshape(-1)
    cut_one, cut_two = qv_part.size, qv_part.size + up_part.size
    qv_bias_grad = lay.all_columns(packed[:cut_one].reshape(qv_part.shape))
    up_bias_grad = lay.all_columns(packed[cut_one:cut_two].reshape(up_part.shape))
    own_part = packed[cut_two:].reshape(own_part.shape)
    return (
        outputs[:img_rows],
        outputs[img_rows : img_rows + txt_rows],
        input_grads[:img_rows],
        input_grads[img_rows : img_rows + txt_rows],
        condition_grad,
        ada_grad,
        ada_bias_grad,
        qkv_grad,
        qv_bias_grad,
        proj_grad,
        own_part[0],
        up_grad,
        up_bias_grad,
        down_grad,
        own_part[1],
    )


def solution(mesh):
    lay = Layout(mesh.shape["dp"], mesh.shape["tensor"])
    bits = Mesh(mesh.devices.reshape((2,) * len(lay.names)), lay.names)
    dp, tensor, every = lay.dp, lay.tensor, lay.names
    in_specs = (
        P(every, None),
        P(every, None),
        P(dp, None),
        P(dp),
        P(None, dp, None, tensor),
        P(),
        P(None, None, dp, tensor),
        P(),
        P(None, tensor, dp),
        P(),
        P(None, dp, tensor),
        P(),
        P(None, tensor, dp),
        P(),
        P(every, None),
        P(every, None),
    )
    out_specs = (
        P(every, None),
        P(every, None),
        P(every, None),
        P(every, None),
        P(dp, tensor),
        P(None, dp, None, tensor),
        P(),
        P(None, None, dp, tensor),
        P(),
        P(None, tensor, dp),
        P(),
        P(None, dp, tensor),
        P(),
        P(None, tensor, dp),
        P(),
    )
    return jax.shard_map(
        functools.partial(body, lay), mesh=bits, in_specs=in_specs, out_specs=out_specs, check_vma=False
    )
```

```python
import functools

import jax
import jax.numpy as jnp
from jax import lax
from jax.experimental import pallas as pl
from jax.experimental.pallas import tpu as pltpu
from jax.sharding import Mesh
from jax.sharding import PartitionSpec as P

HEAD_DIM = 64
SCALE = HEAD_DIM ** (-0.5)
BF = jnp.bfloat16
F32 = jnp.float32
NEG = -1e30


def swap(v, axis):
    return lax.ppermute(v, axis, [(0, 1), (1, 0)])


def gather_bits(v, axes):
    for axis in axes:
        other = swap(v, axis)
        first = lax.axis_index(axis) == 0
        v = jnp.concatenate([jnp.where(first, v, other), jnp.where(first, other, v)], 0)
    return v


def scatter_bits(v, axes):
    for axis in axes:
        first = lax.axis_index(axis) == 0
        half = v.shape[0] // 2
        low, high = v[:half], v[half:]
        v = jnp.where(first, low, high) + swap(jnp.where(first, high, low), axis)
    return v


def sum_bits(v, axes):
    for axis in axes:
        v = v + swap(v, axis)
    return v


def after(v, *deps):
    return lax.optimization_barrier((v,) + deps)[0]


def tie(*vs):
    return lax.optimization_barrier(vs)


def index_of(axes):
    out = 0
    for axis in axes:
        out = out * 2 + lax.axis_index(axis)
    return out


def nt(a, b):
    return lax.dot_general(a, b, (((1,), (1,)), ((), ())), preferred_element_type=F32)


def nn(a, b):
    return lax.dot_general(a, b, (((1,), (0,)), ((), ())), preferred_element_type=F32)


def tn(a, b):
    return lax.dot_general(a, b, (((0,), (0,)), ((), ())), preferred_element_type=F32)


VMEM_LIMIT = 52 * 2**20
GELU_C = 0.7978845608028654


def launch(kernel, grid, in_specs, out_specs, out_shape, args, name, flops, scratch=(), rides=(), cid=None):
    n_in, n_out = len(args), len(out_shape)
    params = dict(vmem_limit_bytes=VMEM_LIMIT)
    cost = pl.CostEstimate(flops=flops, bytes_accessed=flops // 512, transcendentals=0)
    if not rides:
        outs = pl.pallas_call(
            kernel,
            grid=grid,
            in_specs=in_specs,
            out_specs=out_specs,
            out_shape=out_shape,
            scratch_shapes=list(scratch),
            compiler_params=pltpu.CompilerParams(**params),
            cost_estimate=cost,
            name=name,
        )(*args)
        return list(outs), []
    partners = sorted({partner for ride in rides for partner in ride.partners})
    n_rides, sems = len(rides), sum(ride.sems for ride in rides)

    def body(*refs):
        ins, rest = refs[:n_in], refs[n_in:]
        sources, rest = rest[:n_rides], rest[n_rides:]
        outs, rest = rest[:n_out], rest[n_out:]
        targets, rest = rest[:n_rides], rest[n_rides:]
        own, (send, recv) = rest[:-2], rest[-2:]
        steps, at = [], 0
        for source, target, ride in zip(sources, targets, rides):
            steps.append(ride.moves(source, target, lambda k, at=at: send.at[at + k], lambda k, at=at: recv.at[at + k]))
            at += ride.sems

        barrier = pltpu.get_barrier_semaphore()
        for partner in partners:
            pl.semaphore_signal(
                barrier,
                1,
                device_id={axis: 1 - lax.axis_index(axis) for axis in partner},
                device_id_type=pl.DeviceIdType.MESH,
            )
        pl.semaphore_wait(barrier, len(partners))
        for start, unused in steps:
            start()
        pltpu.emit_pipeline(
            lambda *blocks: kernel(*blocks, *own),
            grid=grid,
            in_specs=list(in_specs),
            out_specs=list(out_specs),
        )(*ins, *outs)
        for unused, wait in steps:
            wait()

    anywhere = pl.BlockSpec(memory_space=pl.ANY)
    outs = pl.pallas_call(
        body,
        in_specs=[anywhere] * (n_in + n_rides),
        out_specs=[anywhere] * (n_out + n_rides),
        out_shape=list(out_shape) + [ride.shape for ride in rides],
        scratch_shapes=list(scratch)
        + [pltpu.SemaphoreType.DMA((sems,)), pltpu.SemaphoreType.DMA((sems,))],
        compiler_params=pltpu.CompilerParams(collective_id=cid, has_side_effects=True, **params),
        cost_estimate=cost,
        name=f"{name}_{cid}",
    )(*args, *[ride.array for ride in rides])
    return list(outs[:n_out]), list(outs[n_out:])


class NeighbourRide:
    def __init__(self, array, axis, shape, views, sems):
        self.array, self.axis, self.views, self.sems = array, axis, views, sems
        self.shape = jax.ShapeDtypeStruct(shape, array.dtype)
        self.partners = [(axis,)]

    def moves(self, source, target, send, recv):
        other = {self.axis: 1 - lax.axis_index(self.axis)}
        made = [
            pltpu.make_async_remote_copy(
                src_ref=src,
                dst_ref=dst,
                send_sem=send(k),
                recv_sem=recv(k),
                device_id=other,
                device_id_type=pl.DeviceIdType.MESH,
            )
            for k, (src, dst) in enumerate(self.views(source, target))
        ]

        def start():
            for move in made:
                move.start()

        def wait():
            for move in made:
                move.wait()

        return start, wait


def row_ride(array, axis, start, stop):
    count = min(4, (stop - start) // 16)
    cuts = [start + (stop - start) // 16 * k // count * 16 for k in range(count)] + [stop]

    def views(source, target):
        return [
            (source.at[pl.ds(a, b - a)], target.at[pl.ds(a - start, b - a)])
            for a, b in zip(cuts, cuts[1:])
        ]

    return NeighbourRide(array, axis, (stop - start,) + array.shape[1:], views, count)


class TradeRide:
    sems = 3

    def __init__(self, array, zh, q, back):
        self.array, self.zh, self.q, self.back = array, zh, q, back
        streams, part, n = array.shape[0], array.shape[-2], array.shape[-1]
        shape = (2, streams, part, n) if back else (streams, 2, part, n)
        self.shape = jax.ShapeDtypeStruct(shape, array.dtype)
        self.partners = [(q,), (zh,), (q, zh)]

    def moves(self, source, target, send, recv):
        zh, q = lax.axis_index(self.zh), lax.axis_index(self.q)
        same = zh == q

        def remote(k, src, dst, at, to_zh, to_q):
            return pltpu.make_async_remote_copy(
                src_ref=src,
                dst_ref=dst,
                send_sem=send(k),
                recv_sem=recv(at),
                device_id={self.zh: to_zh, self.q: to_q},
                device_id_type=pl.DeviceIdType.MESH,
            )

        if self.back:
            outgoing = [remote(j, source.at[:, j], target.at[zh], zh, q, j) for j in range(2)]
            arriving = [remote(j, source.at[:, j], target.at[j], j, q, j) for j in range(2)]
            local = pltpu.make_async_copy(source.at[:, q], target.at[zh], send(2))
            mine = [jnp.logical_and(same, q == j) for j in range(2)]
        else:
            outgoing = [remote(j, source, target.at[:, q], q, j, zh) for j in range(2)]
            arriving = [remote(j, source, target.at[:, j], j, j, zh) for j in range(2)]
            local = pltpu.make_async_copy(source, target.at[:, q], send(2))
            mine = [jnp.logical_and(same, zh == j) for j in range(2)]

        def start():
            for move, own in zip(outgoing, mine):
                pl.when(jnp.logical_not(own))(move.start)
            pl.when(same)(local.start)

        def wait():
            for move, own in zip(outgoing, mine):
                pl.when(jnp.logical_not(own))(move.wait_send)
            for move, own in zip(arriving, mine):
                pl.when(jnp.logical_not(own))(move.wait_recv)
            pl.when(same)(local.wait)

        return start, wait


def once(shape, index):
    return pl.BlockSpec(shape, index, pipeline_mode=pl.Buffered(1))


def by_stream(w):
    return [(w[0], 0), (w[1], 0)] if isinstance(w, (list, tuple)) else [(w, 0), (w, 1)]


def rows_nn_kernel(nb, img, mode, *refs):
    xs, w0, w1 = refs[:nb], refs[nb], refs[nb + 1]
    rest = refs[nb + 2 :]
    depth, tile = xs[0].shape[1], w0.shape[3]
    text = xs[0].shape[0] - img
    y_text = nn(
        jnp.concatenate([x[img:, :] for x in xs], axis=0), w1[:, 0].reshape(depth, tile)
    )
    w_img = w0[:, 0].reshape(depth, tile)
    if mode == "slope":
        sums = rest[2 * nb]
        total = [jnp.zeros((1, tile), F32), jnp.zeros((1, tile), F32)]
    for b in range(nb):
        for stream, rows in ((0, slice(0, img)), (1, slice(img, img + text))):
            y = nn(xs[b][rows, :], w_img) if stream == 0 else y_text[b * text : (b + 1) * text]
            if mode == "plain":
                rest[b][rows, :] = y.astype(BF)
            elif mode == "bias":
                rest[1 + b][rows, :] = (y + rest[0][stream]).astype(BF)
            elif mode == "gelu":
                v = y + rest[0][stream]
                inner = jnp.tanh(GELU_C * (v + 0.044715 * (v * v * v)))
                half = 0.5 * (1.0 + inner)
                rest[1 + b][rows, :] = (v * half).astype(BF)
                rest[1 + nb + b][rows, :] = half + 0.5 * v * (1.0 - inner * inner) * (
                    GELU_C * (1.0 + 3 * 0.044715 * (v * v))
                )
            else:
                y = (y * rest[b][rows, :]).astype(BF)
                rest[nb + b][rows, :] = y
                total[stream] += jnp.sum(y.astype(F32), axis=0, keepdims=True)
    if mode == "slope":
        sums[0] = total[0]
        sums[1] = total[1]


def rows_nn(xs, w, img, mode, bias=None, slopes=(), rides=(), cid=None):
    (w0, s0), (w1, s1) = by_stream(w)
    n = w0.shape[3]
    tile = 768 if n % 768 == 0 else 384
    nb, (rows, depth) = len(xs), xs[0].shape
    in_specs = [once((rows, depth), lambda j: (0, 0))] * nb
    in_specs += [
        pl.BlockSpec((4, 1, depth // 4, tile), lambda j, at=at: (0, at, 0, j)) for at in (s0, s1)
    ]
    args = list(xs) + [w0, w1]
    out_tile = pl.BlockSpec((rows, tile), lambda j: (0, j))
    vector = pl.BlockSpec((2, 1, tile), lambda j: (0, 0, j))
    shape = lambda dtype: jax.ShapeDtypeStruct((rows, n), dtype)
    if bias is not None:
        in_specs.append(vector)
        args.append(bias.reshape(2, 1, n))
    in_specs += [out_tile] * len(slopes)
    args += list(slopes)
    out_specs, out_shape = [out_tile] * nb, [shape(BF)] * nb
    if mode == "gelu":
        out_specs, out_shape = out_specs + [out_tile] * nb, out_shape + [shape(F32)] * nb
    if mode == "slope":
        out_specs.append(vector)
        out_shape.append(jax.ShapeDtypeStruct((2, 1, n), F32))
    return launch(
        functools.partial(rows_nn_kernel, nb, img, mode),
        (n // tile,),
        in_specs,
        out_specs,
        out_shape,
        args,
        f"rows_{mode}",
        2 * nb * rows * depth * n,
        rides=rides,
        cid=cid,
    )


def rows_nt_kernel(nb, img, *refs):
    xs, w0, w1, outs = refs[:nb], refs[nb], refs[nb + 1], refs[nb + 2 :]
    text = xs[0].shape[0] - img
    y_text = nt(jnp.concatenate([x[img:, :] for x in xs], axis=0), w1[:, 0].reshape(-1, xs[0].shape[1]))
    w_img = w0[:, 0].reshape(-1, xs[0].shape[1])
    for b in range(nb):
        outs[b][:img, :] = nt(xs[b][:img, :], w_img).astype(outs[b].dtype)
        outs[b][img:, :] = y_text[b * text : (b + 1) * text].astype(outs[b].dtype)


def rows_nt(xs, w, img, dtypes, rides=(), cid=None):
    nb, (rows, n) = len(xs), xs[0].shape
    (w0, s0), (w1, s1) = by_stream(w)
    quarter = w0.shape[2]
    return launch(
        functools.partial(rows_nt_kernel, nb, img),
        (2,),
        [once((rows, n), lambda j: (0, 0))] * nb
        + [
            pl.BlockSpec((2, 1, quarter, n), lambda j, at=at: (j, at, 0, 0)) for at in (s0, s1)
        ],
        [pl.BlockSpec((rows, 2 * quarter), lambda j: (0, j))] * nb,
        [jax.ShapeDtypeStruct((rows, 4 * quarter), t) for t in dtypes],
        list(xs) + [w0, w1],
        "rows_back",
        8 * nb * rows * quarter * n,
        rides=rides,
        cid=cid,
    )


def weight_grad_kernel(nb, img, *refs):
    xs, ys, out = refs[:nb], refs[nb : 2 * nb], refs[2 * nb]
    y_img, y_text = refs[2 * nb + 1 :]
    text = xs[0].shape[0] - img

    @pl.when(pl.program_id(0) == 0)
    def _():
        for b in range(nb):
            y_img[b * img : (b + 1) * img, :] = ys[b][:img, :]
            y_text[b * text : (b + 1) * text, :] = ys[b][img:, :]

    x_img = jnp.concatenate([x[:img, :] for x in xs], axis=0)
    x_text = jnp.concatenate([x[img:, :] for x in xs], axis=0)
    out[0, 0] = tn(x_img, y_img[...]).astype(BF)
    out[0, 1] = tn(x_text, y_text[...]).astype(BF)


def weight_grad(xs, ys, img, rides=(), cid=None):
    nb, (rows, d), n = len(xs), xs[0].shape, ys[0].shape[1]
    (out,), rode = launch(
        functools.partial(weight_grad_kernel, nb, img),
        (4,),
        [pl.BlockSpec((rows, d // 4), lambda j: (0, j))] * nb
        + [once((rows, n), lambda j: (0, 0))] * nb,
        [pl.BlockSpec((1, 2, d // 4, n), lambda j: (j, 0, 0, 0))],
        [jax.ShapeDtypeStruct((4, 2, d // 4, n), BF)],
        list(xs) + list(ys),
        "weight_grad",
        2 * nb * rows * d * n,
        scratch=[pltpu.VMEM((nb * img, n), BF), pltpu.VMEM((nb * (rows - img), n), BF)],
        rides=rides,
        cid=cid,
    )
    return out, rode


def pad_key(position, padded, real):
    return lax.rem(position, padded) >= real


def head_of(refs, img, h):
    cols = slice(h * HEAD_DIM, (h + 1) * HEAD_DIM)
    whole = [r[...] for r in refs]
    return (
        jnp.concatenate([w[:img, cols] for w in whole], axis=0),
        jnp.concatenate([w[img:, cols] for w in whole], axis=0),
    )


def attend_kernel(chunk, img, txt, q0, k0, v0, q1, k1, v1, o0, o1, lse_i, lse_t):
    per = img // chunk
    tp = q0.shape[0] - img
    keys = [head_of((k0, k1), img, h) for h in range(2)]
    vals = [head_of((v0, v1), img, h) for h in range(2)]
    mask = jnp.where(
        pad_key(lax.broadcasted_iota(jnp.int32, (1, 2 * tp), 1), tp, txt), NEG, 0.0
    ).astype(F32)

    def one(q_pair):
        outs, logs = [], []
        for h in range(2):
            q = q_pair[:, h * HEAD_DIM : (h + 1) * HEAD_DIM] * jnp.asarray(SCALE, BF)
            s_i = nt(q, keys[h][0])
            s_t = nt(q, keys[h][1]) + mask
            top = jnp.maximum(
                jnp.max(s_i, axis=1, keepdims=True), jnp.max(s_t, axis=1, keepdims=True)
            )
            p_i = jnp.exp(s_i - top)
            p_t = jnp.exp(s_t - top)
            total = jnp.sum(p_i, axis=1, keepdims=True) + jnp.sum(p_t, axis=1, keepdims=True)
            inv = 1.0 / total
            o = nn((p_i * inv).astype(BF), vals[h][0]) + nn((p_t * inv).astype(BF), vals[h][1])
            outs.append(o.astype(BF))
            logs.append((top + jnp.log(total)).reshape(1, -1))
        return jnp.concatenate(outs, axis=1), logs

    for z, (q_ref, o_ref) in enumerate(((q0, o0), (q1, o1))):

        def step(c, carry, z=z, q_ref=q_ref, o_ref=o_ref):
            r = pl.multiple_of(c * chunk, chunk)
            o, logs = one(q_ref[pl.ds(r, chunk), :])
            o_ref[pl.ds(r, chunk), :] = o
            for h in range(2):
                lse_i[0, h, pl.ds(z * per + c, 1), :] = logs[h]
            return carry

        lax.fori_loop(0, per, step, 0)
    o, logs = one(jnp.concatenate([q0[img:, :], q1[img:, :]], axis=0))
    o0[img:, :] = o[:tp]
    o1[img:, :] = o[tp:]
    for h in range(2):
        lse_t[0, h, 0:1, :] = logs[h]


def attend_back_kernel(
    chunk, img, txt, q0, k0, v0, q1, k1, v1, g0, g1, lse_i, lse_t, d0, d1, sums, dk_i, dv_i, dk_t, dv_t
):
    per = img // chunk
    tp = q0.shape[0] - img
    hp = pl.program_id(0)
    pairs = pl.num_programs(0)
    width = 2 * HEAD_DIM
    keys = [head_of((k0, k1), img, h) for h in range(2)]
    vals = [head_of((v0, v1), img, h) for h in range(2)]
    mask = jnp.where(
        pad_key(lax.broadcasted_iota(jnp.int32, (2 * tp, 1), 0), tp, txt), NEG, 0.0
    ).astype(F32)
    dk_i[...] = jnp.zeros_like(dk_i)
    dv_i[...] = jnp.zeros_like(dv_i)
    dk_t[...] = jnp.zeros_like(dk_t)
    dv_t[...] = jnp.zeros_like(dv_t)

    def one(q_pair, g_pair, logs):
        outs = []
        for h in range(2):
            cols = slice(h * HEAD_DIM, (h + 1) * HEAD_DIM)
            q = q_pair[:, cols] * jnp.asarray(SCALE, BF)
            g = g_pair[:, cols]
            p_i = jnp.exp(nt(keys[h][0], q) - logs[h])
            p_t = jnp.exp(nt(keys[h][1], q) + mask - logs[h])
            dp_i = nt(vals[h][0], g)
            dp_t = nt(vals[h][1], g)
            delta = jnp.sum(p_i * dp_i, axis=0, keepdims=True) + jnp.sum(
                p_t * dp_t, axis=0, keepdims=True
            )
            dv_i[h] += nn(p_i.astype(BF), g)
            dv_t[h] += nn(p_t.astype(BF), g)
            ds_i = (p_i * (dp_i - delta)).astype(BF)
            ds_t = (p_t * (dp_t - delta)).astype(BF)
            dk_i[h] += nn(ds_i, q)
            dk_t[h] += nn(ds_t, q)
            dq = tn(ds_i, keys[h][0]) + tn(ds_t, keys[h][1])
            outs.append((dq * SCALE).astype(BF))
        return jnp.concatenate(outs, axis=1)

    def cols_of(kind):
        return pl.ds(pl.multiple_of((kind * pairs + hp) * width, width), width)

    def column_sum(v):
        return jnp.sum(v.astype(F32), axis=0, keepdims=True)

    q_sum = jnp.zeros((1, width), F32)
    for z, (q_ref, g_ref, d_ref) in enumerate(((q0, g0, d0), (q1, g1, d1))):

        def step(c, total, z=z, q_ref=q_ref, g_ref=g_ref, d_ref=d_ref):
            r = pl.multiple_of(c * chunk, chunk)
            logs = [lse_i[0, h, pl.ds(z * per + c, 1), :] for h in range(2)]
            dq = one(q_ref[pl.ds(r, chunk), :], g_ref[pl.ds(r, chunk), :], logs)
            d_ref[pl.ds(r, chunk), cols_of(0)] = dq
            return total + column_sum(dq)

        q_sum = lax.fori_loop(0, per, step, q_sum)
    logs = [lse_t[0, h, 0:1, :] for h in range(2)]
    dq = one(
        jnp.concatenate([q0[img:, :], q1[img:, :]], axis=0),
        jnp.concatenate([g0[img:, :], g1[img:, :]], axis=0),
        logs,
    )
    d0[img:, cols_of(0)] = dq[:tp]
    d1[img:, cols_of(0)] = dq[tp:]
    sums[0, 0:1] = q_sum
    sums[0, 1:2] = column_sum(dq)
    for kind, image, text in ((1, dk_i, dk_t), (2, dv_i, dv_t)):
        both = jnp.concatenate([image[0].astype(BF), image[1].astype(BF)], axis=1)
        d0[:img, cols_of(kind)] = both[:img]
        d1[:img, cols_of(kind)] = both[img:]
        both_t = jnp.concatenate([text[0].astype(BF), text[1].astype(BF)], axis=1)
        d0[img:, cols_of(kind)] = both_t[:tp]
        d1[img:, cols_of(kind)] = both_t[tp:]
        if kind == 2:
            sums[0, 2:3] = column_sum(both)
            sums[0, 3:4] = column_sum(both_t)


def qkv_specs(rows, pairs):
    width = 2 * HEAD_DIM
    return [
        pl.BlockSpec((rows, width), lambda h, kind=kind: (0, kind * pairs + h)) for kind in range(3)
    ] * 2


def lse_specs(n_chunks, chunk, tp):
    return [
        pl.BlockSpec((1, 2, n_chunks, chunk), lambda h: (h, 0, 0, 0)),
        pl.BlockSpec((1, 2, 1, 2 * tp), lambda h: (h, 0, 0, 0)),
    ]


def attention(near, far, img, txt, chunk, slot, rides=(), cid=None):
    rows, columns = near.shape[0], near.shape[1] // 3
    tp, width = rows - img, 2 * HEAD_DIM
    pairs, n_chunks = columns // width, 2 * img // chunk
    tile = pl.BlockSpec((rows, width), lambda h: (0, h))
    return launch(
        functools.partial(attend_kernel, chunk, img, txt),
        (pairs,),
        qkv_specs(rows, pairs),
        [tile, tile] + lse_specs(n_chunks, chunk, tp),
        [jax.ShapeDtypeStruct((rows, columns), BF)] * 2
        + [
            jax.ShapeDtypeStruct((pairs, 2, n_chunks, chunk), F32),
            jax.ShapeDtypeStruct((pairs, 2, 1, 2 * tp), F32),
        ],
        [near, near, near, far, far, far],
        f"attend_{slot}",
        80 * pairs * rows * rows * HEAD_DIM,
        rides=rides,
        cid=cid,
    )


def attention_back(
    near, far, grad_near, grad_far, lse_i, lse_t, img, txt, chunk, slot, rides=(), cid=None
):
    rows, columns = near.shape[0], near.shape[1] // 3
    tp, width = rows - img, 2 * HEAD_DIM
    pairs, n_chunks = columns // width, 2 * img // chunk
    tile = pl.BlockSpec((rows, width), lambda h: (0, h))
    whole = pl.BlockSpec((rows, 3 * columns), lambda h: (0, 0))
    return launch(
        functools.partial(attend_back_kernel, chunk, img, txt),
        (pairs,),
        qkv_specs(rows, pairs) + [tile, tile] + lse_specs(n_chunks, chunk, tp),
        [whole, whole, pl.BlockSpec((1, 4, width), lambda h: (h, 0, 0))],
        [jax.ShapeDtypeStruct((rows, 3 * columns), BF)] * 2
        + [jax.ShapeDtypeStruct((pairs, 4, width), F32)],
        [near, near, near, far, far, far, grad_near, grad_far, lse_i, lse_t],
        f"attend_back_{slot}",
        200 * pairs * rows * rows * HEAD_DIM,
        scratch=[
            pltpu.VMEM((2, 2 * img, HEAD_DIM), F32),
            pltpu.VMEM((2, 2 * img, HEAD_DIM), F32),
            pltpu.VMEM((2, 2 * tp, HEAD_DIM), F32),
            pltpu.VMEM((2, 2 * tp, HEAD_DIM), F32),
        ],
        rides=rides,
        cid=cid,
    )


class Layout:
    def __init__(self, dp_size, tensor_size):
        dp_bits = dp_size.bit_length() - 1
        t_bits = tensor_size.bit_length() - 1
        self.dp = tuple(f"d{i}" for i in range(dp_bits))
        self.tensor = tuple(f"t{i}" for i in range(t_bits))
        self.names = self.dp + self.tensor
        self.compact = dp_size == 8 and tensor_size == 4
        self.p = self.tensor[-1]
        if self.compact:
            self.y, self.x, self.q = self.dp
            self.zh = self.tensor[0]
            self.upper = ()
        else:
            self.q = self.tensor[-2]
            self.upper = self.tensor[:-2]
        self.rest = tuple(n for n in self.names if n not in (self.p, self.q))

    def my_columns(self, v):
        shards = 2 ** len(self.upper)
        part = v.shape[-1] // (4 * shards)
        v = v.reshape(v.shape[:-1] + (shards, 4, part))
        at = index_of((self.q, self.p))
        v = lax.dynamic_index_in_dim(v, at, v.ndim - 2, keepdims=False)
        return v.reshape(v.shape[:-2] + (shards * part,))

    def all_columns(self, v):
        shards = 2 ** len(self.upper)
        g = gather_bits(v[None], (self.p, self.q))
        g = g.reshape((4,) + v.shape[:-1] + (shards, v.shape[-1] // shards))
        g = jnp.moveaxis(g, 0, -2)
        return g.reshape(v.shape[:-1] + (4 * v.shape[-1],))

    def gather_rows(self, own, end=()):
        pair = after(swap(own, self.p), *end)
        return [[own, swap(own, self.q)], [pair, swap(pair, self.q)]]

    def sum_far(self, w, blocks, img):
        (send, keep), unused = rows_nt([blocks[1][1], blocks[1][0]], w, img, (BF, F32))
        return (keep + swap(send, self.q).astype(F32)).astype(BF)

    def sum_near(self, w, blocks, img, rides=(), cid=None):
        (send, keep), rode = rows_nt([blocks[0][1], blocks[0][0]], w, img, (BF, F32), rides, cid)
        return keep + swap(send, self.q).astype(F32), rode

    def gather_weight(self, w):
        w = lax.all_gather(w, self.dp, axis=1, tiled=True)
        if self.upper:
            w = lax.all_gather(w, self.upper, axis=3, tiled=True)
        return jnp.swapaxes(w.reshape(2, 4, w.shape[1] // 4, -1), 0, 1)

    def trade_shards(self, w, end=()):
        w = w.reshape(w.shape[0], w.shape[1], -1)
        joint = (self.q, self.zh)
        same = lax.axis_index(self.zh) == lax.axis_index(self.q)
        cross = lax.ppermute(w, joint, [(1, 2), (2, 1)])
        second = lax.ppermute(w, joint, [(0, 1), (3, 2), (2, 0), (1, 3)])
        cross, second = after((cross, second), *end)
        first = jnp.where(same, w, cross)
        low = lax.axis_index(self.zh) == 0
        return jnp.concatenate(
            [jnp.where(low, first, second), jnp.where(low, second, first)], axis=1
        )

    def spread_near(self, own):
        return [swap(own[0], self.x), swap(own[1], self.y)]

    def spread_rows(self, own, nears):
        x, y = lax.axis_index(self.x), lax.axis_index(self.y)
        whole = jnp.zeros((4,) + own.shape, BF)
        for stream, far_axis in enumerate((self.y, self.x)):
            mine, near = own[stream], nears[stream]
            both, far = swap(near, far_axis), swap(mine, far_axis)
            dx, dy = (near, far) if stream == 0 else (far, near)
            for block, at in (
                (mine, 2 * y + x),
                (dx, 2 * y + 1 - x),
                (dy, 2 * (1 - y) + x),
                (both, 2 * (1 - y) + 1 - x),
            ):
                whole = lax.dynamic_update_slice(whole, block[None, None], (at, stream, 0, 0))
        return whole

    def spread_rows_async(self, own):
        own = own.reshape(own.shape[0], -1, own.shape[-1])
        return lax.all_gather(own, (self.y, self.x), axis=0, tiled=False)

    def trade_ride(self, array, back=False):
        if back:
            array = array.reshape(2, 2, -1, array.shape[-1])
        return TradeRide(array, self.zh, self.q, back)

    def scatter_generic(self, g, kinds):
        g = jnp.swapaxes(g.astype(F32), 0, 1).reshape(2, 4 * g.shape[2], kinds, -1)
        g = lax.psum_scatter(g, self.dp, scatter_dimension=1, tiled=True)
        if self.upper:
            g = lax.psum_scatter(g, self.upper, scatter_dimension=3, tiled=True)
        return g

    def sum_plane_async(self, g):
        return lax.psum_scatter(g, (self.y, self.x), scatter_dimension=0, tiled=False)

    def plane_rides(self, g):
        g = g.reshape((2, 2) + g.shape[1:])
        shape = (2,) + g.shape[3:]

        def along_x(source, target):
            x = 1 - lax.axis_index(self.x)
            return [(source.at[k, x, 0], target.at[k]) for k in range(2)]

        def along_y(source, target):
            y = 1 - lax.axis_index(self.y)
            return [(source.at[y, k, 1], target.at[k]) for k in range(2)]

        return [
            NeighbourRide(g, self.x, shape, along_x, 2),
            NeighbourRide(g, self.y, shape, along_y, 2),
        ]

    def sum_plane(self, g, arrived):
        x, y = lax.axis_index(self.x), lax.axis_index(self.y)
        pick = lambda v, i, dim: lax.dynamic_index_in_dim(v, i, dim, keepdims=False)
        g = g.reshape((2, 2) + g.shape[1:])
        done = []
        for stream in range(2):
            near, dim, far_axis, far = ((x, 1, self.y, y), (y, 0, self.x, x))[stream]
            at = (0, near, stream, 0, 0) if dim == 1 else (near, 0, stream, 0, 0)
            size = (2, 1) if dim == 1 else (1, 2)
            v = lax.dynamic_slice(g, at, size + (1,) + g.shape[3:]).reshape(arrived[stream].shape)
            v = v.astype(F32) + arrived[stream].astype(F32)
            v = pick(v, far, 0) + swap(pick(v, 1 - far, 0).astype(BF), far_axis).astype(F32)
            done.append(v)
        return jnp.stack(done)

    def trade_parts(self, g):
        g = g.reshape(2, 2, -1, g.shape[-1])
        zh = lax.axis_index(self.zh)
        return [lax.dynamic_index_in_dim(g, k, 1, keepdims=False) for k in (zh, 1 - zh)]

    def trade_sends(self, g):
        first, second = self.trade_parts(g)
        joint = (self.q, self.zh)
        return [
            lax.ppermute(first.astype(BF), joint, [(1, 2), (2, 1)]),
            lax.ppermute(second.astype(BF), joint, [(1, 0), (2, 3), (0, 2), (3, 1)]),
        ]

    def trade_adds(self, g, arrived, kinds):
        same = lax.axis_index(self.zh) == lax.axis_index(self.q)
        total = jnp.where(same, self.trade_parts(g)[0].astype(F32), arrived[0].astype(F32))
        total += arrived[1].astype(F32)
        return total.reshape(2, total.shape[1], kinds, -1)


def norm_parts(values):
    average = jnp.mean(values, axis=-1, keepdims=True)
    centred = values - average
    variance = jnp.mean(centred * centred, axis=-1, keepdims=True)
    inverse = lax.rsqrt(variance + 1e-06)
    return centred * inverse, inverse


def norm_back(normed, inverse, grad_in):
    first_mean = jnp.mean(grad_in, axis=-1, keepdims=True)
    cross_mean = jnp.mean(grad_in * normed, axis=-1, keepdims=True)
    return inverse * (grad_in - first_mean - normed * cross_mean)


def body(
    lay,
    image_in,
    text_in,
    condition,
    live_slots,
    ada_weight,
    ada_bias,
    qkv_weight,
    qv_bias,
    proj_weight,
    proj_bias,
    up_weight,
    up_bias,
    down_weight,
    down_bias,
    image_grad,
    text_grad,
):
    width = image_in.shape[1]
    part = qkv_weight.shape[2]
    columns = qkv_weight.shape[3]
    img_rows, txt_rows = image_in.shape[0], text_in.shape[0]
    txt_pad = -(-txt_rows // 16) * 16
    group_slots = condition.shape[0]
    dp_index, t_index = index_of(lay.dp), index_of(lay.tensor)
    t_count = 2 ** len(lay.tensor)
    assert group_slots * 2 == t_count
    my_slot = t_index // 2
    dp_up, t_up = lay.dp[::-1], lay.tensor[::-1]

    rows = img_rows + txt_pad
    is_image = lax.broadcasted_iota(jnp.int32, (rows, 1), 0) < img_rows

    def pack(image, text):
        return jnp.concatenate([image, jnp.pad(text, ((0, txt_pad - txt_rows), (0, 0)))], axis=0)

    def spread(per_stream):
        return jnp.where(is_image, per_stream[0], per_stream[1])

    def total(v):
        return jnp.stack([jnp.sum(v[:img_rows], axis=0), jnp.sum(v[img_rows:], axis=0)])

    def flat(blocks):
        return blocks[0] + blocks[1]

    def unflat(v):
        return [list(v[:2]), list(v[2:4])]

    qkv_local = jnp.swapaxes(qkv_weight, 1, 2)
    proj_local = jnp.swapaxes(proj_weight, 1, 2)[:, :, None]
    up_local = up_weight[:, :, None]
    down_local = jnp.swapaxes(down_weight, 1, 2)[:, :, None]
    compact = lay.compact
    if compact:
        qkv_own = lay.trade_shards(qkv_local)
        qkv_near = lay.spread_near(qkv_own)
    else:
        qkv_full, up_full, proj_full, down_full = [
            lay.gather_weight(w) for w in (qkv_local, up_local, proj_local, down_local)
        ]

    cond_all = gather_bits(condition, dp_up).astype(F32)
    silu_all = jax.nn.silu(cond_all).astype(BF)
    silu_mine = lax.dynamic_slice_in_dim(silu_all, dp_index * part, part, 1)
    mod = jnp.einsum("sd,tdkc->stkc", silu_mine, ada_weight, preferred_element_type=F32)
    mod = scatter_bits(mod, lay.dp)
    if compact:
        mod = after(mod, qkv_own)
    mod = gather_bits(mod[None], t_up)
    mod = lax.dynamic_index_in_dim(mod, my_slot, 1, keepdims=False)
    mod = jnp.moveaxis(mod, 0, 2).reshape(2, 6, width) + ada_bias.astype(F32)
    live = lax.dynamic_index_in_dim(live_slots, my_slot, 0, keepdims=False).astype(F32)

    mods = [spread(mod[:, k]) for k in range(6)]
    shift_one, scale_one, gate_one, shift_two, scale_two, gate_two = mods

    inputs = pack(image_in, text_in).astype(F32)
    grad_out = live * pack(image_grad, text_grad).astype(F32)
    grad_two = (gate_two * grad_out).astype(BF)

    first_norm = norm_parts(inputs)
    first_hidden = (first_norm[0] * (1.0 + scale_one) + shift_one).astype(BF)
    if compact:
        first_hidden = after(first_hidden, qkv_near)
    first = lay.gather_rows(first_hidden)
    if compact:
        qkv_full = lay.spread_rows(qkv_own, qkv_near)
    qv = lay.my_columns(qv_bias.astype(F32))
    qkv_bias = jnp.concatenate([qv[:, 0], jnp.zeros_like(qv[:, 0]), qv[:, 1]], axis=1)
    heads_n = qv.shape[2]
    img = img_rows

    def ride(array, start, stop):
        return row_ride(array, lay.p, start, stop)

    cut = rows // 3 // 16 * 16
    extra = [[], [], []]
    if compact:
        extra = [
            [lay.trade_ride(w.reshape(w.shape[0], part, -1))]
            for w in (proj_local, up_local[:1], up_local[1:])
        ]
    qkv, rode = rows_nn(
        flat(first), qkv_full, img, "bias", bias=qkv_bias, rides=extra[0], cid=1
    )
    qkv = unflat(qkv)
    chunk = min(256, img_rows)
    if compact:
        proj_full = lay.spread_rows_async(rode[0])
    other, rode = attention(
        qkv[0][1], qkv[1][1], img, txt_rows, chunk, 1, rides=extra[1], cid=2
    )
    if compact:
        up_full = [lay.spread_rows_async(rode[0])]
        qkv, other = after((qkv, other), proj_full)
    mine, rode = attention(
        qkv[0][0],
        qkv[1][0],
        img,
        txt_rows,
        chunk,
        0,
        rides=[ride(grad_two, 0, cut)] + extra[2],
        cid=10,
    )
    grad_two_pair = rode[:1]
    heads_out = [[mine[z], other[z]] for z in range(2)]
    if compact:
        up_full.append(lay.spread_rows_async(rode[1]))
        down_own = lay.trade_shards(after(down_local, mine))

    far = swap(lay.sum_far(proj_full, heads_out, img), lay.p)
    near, unused = lay.sum_near(proj_full, heads_out, img)
    branch_one = near + far.astype(F32) + spread(proj_bias.astype(F32))
    middle = inputs + gate_one * branch_one
    second_norm = norm_parts(middle)
    second_hidden = (second_norm[0] * (1.0 + scale_two) + shift_two).astype(BF)
    if compact:
        second_hidden, down_own = tie(second_hidden, down_own)
        down_full = lay.spread_rows_async(down_own)
    second = lay.gather_rows(second_hidden)
    up_mine = lay.my_columns(up_bias.astype(F32))
    up_n = up_mine.shape[1]
    up_out, rode = rows_nn(
        flat(second), up_full, img, "gelu", bias=up_mine, rides=[ride(grad_two, cut, rows)], cid=13
    )
    grad_two_pair = jnp.concatenate(grad_two_pair + rode, axis=0)
    grad_two_blocks = [
        [grad_two, swap(grad_two, lay.q)], [grad_two_pair, swap(grad_two_pair, lay.q)]
    ]
    activated, slopes = up_out[:4], up_out[4:]
    far = lay.sum_far(down_full, unflat(activated), img)
    cut = rows * 21 // 37 // 16 * 16
    back_out, rode = rows_nn(
        flat(grad_two_blocks), down_full, img, "slope", slopes=slopes, rides=[ride(far, 0, cut)], cid=3
    )
    grad_inner, up_part = back_out[:4], back_out[4].reshape(2, up_n)
    down_grads, rode_two = weight_grad(
        after(flat(grad_two_blocks), grad_inner), activated, img, rides=[ride(far, cut, rows)], cid=4
    )
    far = jnp.concatenate(rode + rode_two, axis=0)
    if compact:
        down_plane = lay.sum_plane_async(down_grads)
    far_two = lay.sum_far(up_full, after(unflat(grad_inner), down_grads), img)
    cut, cut_two = rows * 11 // 37 // 16 * 16, rows * 22 // 37 // 16 * 16
    near_two, rode = lay.sum_near(up_full, unflat(grad_inner), img, [ride(far_two, 0, cut)], 5)
    up_grads, rode_two = weight_grad(
        after(flat(second), near_two), grad_inner, img, rides=[ride(far_two, cut_two, rows)], cid=6
    )
    if compact:
        up_plane = lay.sum_plane_async(up_grads)
    near, rode_three = lay.sum_near(
        down_full, after(unflat(activated), up_grads), img, [ride(far_two, cut, cut_two)], 7
    )
    far_two = jnp.concatenate(rode + rode_three + rode_two, axis=0)
    branch_two = near + far.astype(F32) + spread(down_bias.astype(F32))
    outputs = (live * (middle + gate_two * branch_two)).astype(BF)
    grad_hidden_two = near_two + far_two.astype(F32)
    grad_middle = grad_out + norm_back(
        second_norm[0], second_norm[1], grad_hidden_two * (1.0 + scale_two)
    )
    grad_one = (gate_one * grad_middle).astype(BF)
    if compact:
        grad_one = after(grad_one, down_plane)
    grad_one_blocks = lay.gather_rows(grad_one)
    grad_heads = unflat(rows_nn(flat(grad_one_blocks), proj_full, img, "plain")[0])

    def back(c, saved, heads, rides, cid):
        return attention_back(
            qkv[0][c],
            qkv[1][c],
            heads[0][c],
            heads[1][c],
            saved[2],
            saved[3],
            img,
            txt_rows,
            chunk,
            c,
            rides,
            cid,
        )

    grad_other, down_sums = back(
        1, other, grad_heads, [lay.trade_ride(down_plane, True)] if compact else (), 11
    )
    proj_grads, unused = weight_grad(
        after(flat(grad_one_blocks), grad_other), flat(heads_out), img
    )
    if compact:
        proj_plane = lay.sum_plane_async(proj_grads)
    grad_mine, up_sums = back(
        0,
        mine,
        after(grad_heads, proj_grads),
        [lay.trade_ride(up_plane, True)] if compact else (),
        12,
    )
    grad_qkv = [[grad_mine[z], grad_other[z]] for z in range(2)]
    far = lay.sum_far(qkv_full, grad_qkv, img)
    cut = rows * 16 // 37 // 16 * 16
    rides = [ride(far, 0, cut)]
    if compact:
        rides.append(lay.trade_ride(proj_plane, True))
    qkv_grads, rode = weight_grad(flat(first), flat(grad_qkv), img, rides=rides, cid=8)
    rides = [ride(far, cut, rows)]
    if compact:
        proj_sums = rode[1]
        rides += lay.plane_rides(qkv_grads)
    near, rode_two = lay.sum_near(qkv_full, after(grad_qkv, qkv_grads), img, rides, 9)
    far = jnp.concatenate(rode[:1] + rode_two[:1], axis=0)
    if compact:
        down_grad, up_grad, proj_grad = [
            (v[0].astype(F32) + v[1].astype(F32))[:, :, None]
            for v in (down_sums[0], up_sums[0], proj_sums)
        ]
        qkv_plane = lay.sum_plane(qkv_grads, rode_two[1:3])
    else:
        down_grad, up_grad, proj_grad = [
            lay.scatter_generic(g, 1) for g in (down_grads, up_grads, proj_grads)
        ]
        qkv_grad = lay.scatter_generic(qkv_grads, 3)
    grad_hidden_one = near + far.astype(F32)
    input_grads = grad_middle + norm_back(
        first_norm[0], first_norm[1], grad_hidden_one * (1.0 + scale_one)
    )

    grad_mod = jnp.stack(
        [
            total(grad_hidden_one),
            total(grad_hidden_one * first_norm[0]),
            total(branch_one * grad_middle),
            total(grad_hidden_two),
            total(grad_hidden_two * second_norm[0]),
            total(branch_two * grad_out),
        ],
        axis=1,
    )
    grad_mod = sum_bits(grad_mod, (lay.p,))
    grad_mod = gather_bits(grad_mod[None], t_up[1:])
    if compact:
        qkv_plane, grad_mod = tie(qkv_plane, grad_mod)
    grad_mod = lax.dynamic_slice_in_dim(grad_mod, t_index * columns, columns, 3)
    grad_mod = gather_bits(grad_mod, dp_up)
    high = lax.Precision.HIGHEST
    ada_grad = jnp.einsum("sd,stkc->tdkc", silu_mine.astype(F32), grad_mod, precision=high)
    cond_terms = jnp.einsum("stkc,tdkc->sd", grad_mod, ada_weight.astype(F32), precision=high)
    cond_terms = gather_bits(cond_terms[None], dp_up)
    cond_terms = lax.dynamic_slice_in_dim(cond_terms, dp_index * group_slots, group_slots, 1)
    cond_terms = jnp.swapaxes(cond_terms, 0, 1).reshape(group_slots, width)
    if compact:
        arrived = lay.trade_sends(qkv_plane)
        cond_terms, arrived = tie(cond_terms, arrived)
        qkv_grad = lay.trade_adds(qkv_plane, arrived, 3)
    down_grad = jnp.swapaxes(down_grad[:, :, 0], 1, 2)
    proj_grad = jnp.swapaxes(proj_grad[:, :, 0], 1, 2)
    up_grad = up_grad[:, :, 0]
    qkv_grad = jnp.swapaxes(qkv_grad, 1, 2)
    cond_terms = sum_bits(cond_terms, t_up)
    cond_terms = lax.dynamic_slice_in_dim(cond_terms, t_index * columns, columns, 1)
    cond_slice = lax.dynamic_slice_in_dim(condition.astype(F32), t_index * columns, columns, 1)
    unused, silu_pull = jax.vjp(jax.nn.silu, cond_slice)
    condition_grad = silu_pull(cond_terms)[0]
    ada_bias_grad = gather_bits(jnp.sum(grad_mod, axis=0)[None], t_up)
    ada_bias_grad = jnp.moveaxis(ada_bias_grad, 0, 2).reshape(2, 6, width)

    own_part = sum_bits(
        jnp.stack([total(grad_one.astype(F32)), total(grad_two.astype(F32))]), (lay.p, lay.q)
    )
    sums = grad_mine[2] + grad_other[2]
    pairs = sums.shape[0]
    qv_part = jnp.transpose(sums.reshape(pairs, 2, 2, -1), (2, 1, 0, 3)).reshape(2, 2, heads_n)
    if compact:
        qv_part = after(qv_part, near)
    packed = jnp.concatenate([qv_part.reshape(-1), up_part.reshape(-1), own_part.reshape(-1)])
    packed = sum_bits(packed.reshape(-1, 128), lay.rest).reshape(-1)
    cut_one, cut_two = qv_part.size, qv_part.size + up_part.size
    qv_bias_grad = lay.all_columns(packed[:cut_one].reshape(qv_part.shape))
    up_bias_grad = lay.all_columns(packed[cut_one:cut_two].reshape(up_part.shape))
    own_part = packed[cut_two:].reshape(own_part.shape)
    return (
        outputs[:img_rows],
        outputs[img_rows : img_rows + txt_rows],
        input_grads[:img_rows],
        input_grads[img_rows : img_rows + txt_rows],
        condition_grad,
        ada_grad,
        ada_bias_grad,
        qkv_grad,
        qv_bias_grad,
        proj_grad,
        own_part[0],
        up_grad,
        up_bias_grad,
        down_grad,
        own_part[1],
    )


def solution(mesh):
    lay = Layout(mesh.shape["dp"], mesh.shape["tensor"])
    bits = Mesh(mesh.devices.reshape((2,) * len(lay.names)), lay.names)
    dp, tensor, every = lay.dp, lay.tensor, lay.names
    in_specs = (
        P(every, None),
        P(every, None),
        P(dp, None),
        P(dp),
        P(None, dp, None, tensor),
        P(),
        P(None, None, dp, tensor),
        P(),
        P(None, tensor, dp),
        P(),
        P(None, dp, tensor),
        P(),
        P(None, tensor, dp),
        P(),
        P(every, None),
        P(every, None),
    )
    out_specs = (
        P(every, None),
        P(every, None),
        P(every, None),
        P(every, None),
        P(dp, tensor),
        P(None, dp, None, tensor),
        P(),
        P(None, None, dp, tensor),
        P(),
        P(None, tensor, dp),
        P(),
        P(None, dp, tensor),
        P(),
        P(None, tensor, dp),
        P(),
    )
    return jax.shard_map(
        functools.partial(body, lay), mesh=bits, in_specs=in_specs, out_specs=out_specs, check_vma=False
    )
```

```python
import functools

import jax
import jax.numpy as jnp
from jax import lax
from jax.experimental import pallas as pl
from jax.experimental.pallas import tpu as pltpu
from jax.sharding import Mesh
from jax.sharding import PartitionSpec as P

HEAD_DIM = 64
SCALE = HEAD_DIM ** (-0.5)
BF = jnp.bfloat16
F32 = jnp.float32
NEG = -1e30


def swap(v, axis):
    return lax.ppermute(v, axis, [(0, 1), (1, 0)])


def gather_bits(v, axes):
    for axis in axes:
        other = swap(v, axis)
        first = lax.axis_index(axis) == 0
        v = jnp.concatenate([jnp.where(first, v, other), jnp.where(first, other, v)], 0)
    return v


def scatter_bits(v, axes):
    for axis in axes:
        first = lax.axis_index(axis) == 0
        half = v.shape[0] // 2
        low, high = v[:half], v[half:]
        v = jnp.where(first, low, high) + swap(jnp.where(first, high, low), axis)
    return v


def sum_bits(v, axes):
    for axis in axes:
        v = v + swap(v, axis)
    return v


def after(v, *deps):
    return lax.optimization_barrier((v,) + deps)[0]


def tie(*vs):
    return lax.optimization_barrier(vs)


def index_of(axes):
    out = 0
    for axis in axes:
        out = out * 2 + lax.axis_index(axis)
    return out


def nt(a, b):
    return lax.dot_general(a, b, (((1,), (1,)), ((), ())), preferred_element_type=F32)


def nn(a, b):
    return lax.dot_general(a, b, (((1,), (0,)), ((), ())), preferred_element_type=F32)


def tn(a, b):
    return lax.dot_general(a, b, (((0,), (0,)), ((), ())), preferred_element_type=F32)


VMEM_LIMIT = 52 * 2**20
GELU_C = 0.7978845608028654


def launch(kernel, grid, in_specs, out_specs, out_shape, args, name, flops, scratch=(), rides=(), cid=None):
    n_in, n_out = len(args), len(out_shape)
    params = dict(vmem_limit_bytes=VMEM_LIMIT)
    cost = pl.CostEstimate(flops=flops, bytes_accessed=flops // 512, transcendentals=0)
    if not rides:
        outs = pl.pallas_call(
            kernel,
            grid=grid,
            in_specs=in_specs,
            out_specs=out_specs,
            out_shape=out_shape,
            scratch_shapes=list(scratch),
            compiler_params=pltpu.CompilerParams(**params),
            cost_estimate=cost,
            name=name,
        )(*args)
        return list(outs), []
    partners = sorted({partner for ride in rides for partner in ride.partners})
    n_rides, sems = len(rides), sum(ride.sems for ride in rides)

    def body(*refs):
        ins, rest = refs[:n_in], refs[n_in:]
        sources, rest = rest[:n_rides], rest[n_rides:]
        outs, rest = rest[:n_out], rest[n_out:]
        targets, rest = rest[:n_rides], rest[n_rides:]
        own, (send, recv) = rest[:-2], rest[-2:]
        steps, at = [], 0
        for source, target, ride in zip(sources, targets, rides):
            steps.append(ride.moves(source, target, lambda k, at=at: send.at[at + k], lambda k, at=at: recv.at[at + k]))
            at += ride.sems

        barrier = pltpu.get_barrier_semaphore()
        for partner in partners:
            pl.semaphore_signal(
                barrier,
                1,
                device_id={axis: 1 - lax.axis_index(axis) for axis in partner},
                device_id_type=pl.DeviceIdType.MESH,
            )
        pl.semaphore_wait(barrier, len(partners))
        for start, unused in steps:
            start()
        pltpu.emit_pipeline(
            lambda *blocks: kernel(*blocks, *own),
            grid=grid,
            in_specs=list(in_specs),
            out_specs=list(out_specs),
        )(*ins, *outs)
        for unused, wait in steps:
            wait()

    anywhere = pl.BlockSpec(memory_space=pl.ANY)
    outs = pl.pallas_call(
        body,
        in_specs=[anywhere] * (n_in + n_rides),
        out_specs=[anywhere] * (n_out + n_rides),
        out_shape=list(out_shape) + [ride.shape for ride in rides],
        scratch_shapes=list(scratch)
        + [pltpu.SemaphoreType.DMA((sems,)), pltpu.SemaphoreType.DMA((sems,))],
        compiler_params=pltpu.CompilerParams(collective_id=cid, has_side_effects=True, **params),
        cost_estimate=cost,
        name=f"{name}_{cid}",
    )(*args, *[ride.array for ride in rides])
    return list(outs[:n_out]), list(outs[n_out:])


class NeighbourRide:
    def __init__(self, array, axis, shape, views, sems):
        self.array, self.axis, self.views, self.sems = array, axis, views, sems
        self.shape = jax.ShapeDtypeStruct(shape, array.dtype)
        self.partners = [(axis,)]

    def moves(self, source, target, send, recv):
        other = {self.axis: 1 - lax.axis_index(self.axis)}
        made = [
            pltpu.make_async_remote_copy(
                src_ref=src,
                dst_ref=dst,
                send_sem=send(k),
                recv_sem=recv(k),
                device_id=other,
                device_id_type=pl.DeviceIdType.MESH,
            )
            for k, (src, dst) in enumerate(self.views(source, target))
        ]

        def start():
            for move in made:
                move.start()

        def wait():
            for move in made:
                move.wait()

        return start, wait


def row_ride(array, axis, start, stop):
    count = min(4, (stop - start) // 16)
    cuts = [start + (stop - start) // 16 * k // count * 16 for k in range(count)] + [stop]

    def views(source, target):
        return [
            (source.at[pl.ds(a, b - a)], target.at[pl.ds(a - start, b - a)])
            for a, b in zip(cuts, cuts[1:])
        ]

    return NeighbourRide(array, axis, (stop - start,) + array.shape[1:], views, count)


class TradeRide:
    sems = 3

    def __init__(self, array, zh, q, back):
        self.array, self.zh, self.q, self.back = array, zh, q, back
        streams, part, n = array.shape[0], array.shape[-2], array.shape[-1]
        shape = (2, streams, part, n) if back else (streams, 2, part, n)
        self.shape = jax.ShapeDtypeStruct(shape, array.dtype)
        self.partners = [(q,), (zh,), (q, zh)]

    def moves(self, source, target, send, recv):
        zh, q = lax.axis_index(self.zh), lax.axis_index(self.q)
        same = zh == q

        def remote(k, src, dst, at, to_zh, to_q):
            return pltpu.make_async_remote_copy(
                src_ref=src,
                dst_ref=dst,
                send_sem=send(k),
                recv_sem=recv(at),
                device_id={self.zh: to_zh, self.q: to_q},
                device_id_type=pl.DeviceIdType.MESH,
            )

        if self.back:
            outgoing = [remote(j, source.at[:, j], target.at[zh], zh, q, j) for j in range(2)]
            arriving = [remote(j, source.at[:, j], target.at[j], j, q, j) for j in range(2)]
            local = pltpu.make_async_copy(source.at[:, q], target.at[zh], send(2))
            mine = [jnp.logical_and(same, q == j) for j in range(2)]
        else:
            outgoing = [remote(j, source, target.at[:, q], q, j, zh) for j in range(2)]
            arriving = [remote(j, source, target.at[:, j], j, j, zh) for j in range(2)]
            local = pltpu.make_async_copy(source, target.at[:, q], send(2))
            mine = [jnp.logical_and(same, zh == j) for j in range(2)]

        def start():
            for move, own in zip(outgoing, mine):
                pl.when(jnp.logical_not(own))(move.start)
            pl.when(same)(local.start)

        def wait():
            for move, own in zip(outgoing, mine):
                pl.when(jnp.logical_not(own))(move.wait_send)
            for move, own in zip(arriving, mine):
                pl.when(jnp.logical_not(own))(move.wait_recv)
            pl.when(same)(local.wait)

        return start, wait


def once(shape, index):
    return pl.BlockSpec(shape, index, pipeline_mode=pl.Buffered(1))


def by_stream(w):
    return [(w[0], 0), (w[1], 0)] if isinstance(w, (list, tuple)) else [(w, 0), (w, 1)]


def rows_nn_kernel(nb, img, mode, *refs):
    xs, w0, w1 = refs[:nb], refs[nb], refs[nb + 1]
    rest = refs[nb + 2 :]
    depth, tile = xs[0].shape[1], w0.shape[3]
    text = xs[0].shape[0] - img
    y_text = nn(
        jnp.concatenate([x[img:, :] for x in xs], axis=0), w1[:, 0].reshape(depth, tile)
    )
    w_img = w0[:, 0].reshape(depth, tile)
    if mode == "slope":
        sums = rest[2 * nb]
        total = [jnp.zeros((1, tile), F32), jnp.zeros((1, tile), F32)]
    for b in range(nb):
        for stream, rows in ((0, slice(0, img)), (1, slice(img, img + text))):
            y = nn(xs[b][rows, :], w_img) if stream == 0 else y_text[b * text : (b + 1) * text]
            if mode == "plain":
                rest[b][rows, :] = y.astype(BF)
            elif mode == "bias":
                rest[1 + b][rows, :] = (y + rest[0][stream]).astype(BF)
            elif mode == "gelu":
                v = y + rest[0][stream]
                inner = jnp.tanh(GELU_C * (v + 0.044715 * (v * v * v)))
                half = 0.5 * (1.0 + inner)
                rest[1 + b][rows, :] = (v * half).astype(BF)
                rest[1 + nb + b][rows, :] = half + 0.5 * v * (1.0 - inner * inner) * (
                    GELU_C * (1.0 + 3 * 0.044715 * (v * v))
                )
            else:
                y = (y * rest[b][rows, :]).astype(BF)
                rest[nb + b][rows, :] = y
                total[stream] += jnp.sum(y.astype(F32), axis=0, keepdims=True)
    if mode == "slope":
        sums[0] = total[0]
        sums[1] = total[1]


def rows_nn(xs, w, img, mode, bias=None, slopes=(), rides=(), cid=None):
    (w0, s0), (w1, s1) = by_stream(w)
    n = w0.shape[3]
    tile = 768 if n % 768 == 0 else 384
    nb, (rows, depth) = len(xs), xs[0].shape
    in_specs = [once((rows, depth), lambda j: (0, 0))] * nb
    in_specs += [
        pl.BlockSpec((4, 1, depth // 4, tile), lambda j, at=at: (0, at, 0, j)) for at in (s0, s1)
    ]
    args = list(xs) + [w0, w1]
    out_tile = pl.BlockSpec((rows, tile), lambda j: (0, j))
    vector = pl.BlockSpec((2, 1, tile), lambda j: (0, 0, j))
    shape = lambda dtype: jax.ShapeDtypeStruct((rows, n), dtype)
    if bias is not None:
        in_specs.append(vector)
        args.append(bias.reshape(2, 1, n))
    in_specs += [out_tile] * len(slopes)
    args += list(slopes)
    out_specs, out_shape = [out_tile] * nb, [shape(BF)] * nb
    if mode == "gelu":
        out_specs, out_shape = out_specs + [out_tile] * nb, out_shape + [shape(F32)] * nb
    if mode == "slope":
        out_specs.append(vector)
        out_shape.append(jax.ShapeDtypeStruct((2, 1, n), F32))
    return launch(
        functools.partial(rows_nn_kernel, nb, img, mode),
        (n // tile,),
        in_specs,
        out_specs,
        out_shape,
        args,
        f"rows_{mode}",
        2 * nb * rows * depth * n,
        rides=rides,
        cid=cid,
    )


def rows_nt_kernel(nb, img, *refs):
    xs, w0, w1, outs = refs[:nb], refs[nb], refs[nb + 1], refs[nb + 2 :]
    text = xs[0].shape[0] - img
    y_text = nt(jnp.concatenate([x[img:, :] for x in xs], axis=0), w1[:, 0].reshape(-1, xs[0].shape[1]))
    w_img = w0[:, 0].reshape(-1, xs[0].shape[1])
    for b in range(nb):
        outs[b][:img, :] = nt(xs[b][:img, :], w_img).astype(outs[b].dtype)
        outs[b][img:, :] = y_text[b * text : (b + 1) * text].astype(outs[b].dtype)


def rows_nt(xs, w, img, dtypes, rides=(), cid=None):
    nb, (rows, n) = len(xs), xs[0].shape
    (w0, s0), (w1, s1) = by_stream(w)
    quarter = w0.shape[2]
    return launch(
        functools.partial(rows_nt_kernel, nb, img),
        (2,),
        [once((rows, n), lambda j: (0, 0))] * nb
        + [
            pl.BlockSpec((2, 1, quarter, n), lambda j, at=at: (j, at, 0, 0)) for at in (s0, s1)
        ],
        [pl.BlockSpec((rows, 2 * quarter), lambda j: (0, j))] * nb,
        [jax.ShapeDtypeStruct((rows, 4 * quarter), t) for t in dtypes],
        list(xs) + [w0, w1],
        "rows_back",
        8 * nb * rows * quarter * n,
        rides=rides,
        cid=cid,
    )


def weight_grad_kernel(nb, img, *refs):
    xs, ys, out = refs[:nb], refs[nb : 2 * nb], refs[2 * nb]
    y_img, y_text = refs[2 * nb + 1 :]
    text = xs[0].shape[0] - img

    @pl.when(pl.program_id(0) == 0)
    def _():
        for b in range(nb):
            y_img[b * img : (b + 1) * img, :] = ys[b][:img, :]
            y_text[b * text : (b + 1) * text, :] = ys[b][img:, :]

    x_img = jnp.concatenate([x[:img, :] for x in xs], axis=0)
    x_text = jnp.concatenate([x[img:, :] for x in xs], axis=0)
    out[0, 0] = tn(x_img, y_img[...]).astype(BF)
    out[0, 1] = tn(x_text, y_text[...]).astype(BF)


def weight_grad(xs, ys, img, rides=(), cid=None):
    nb, (rows, d), n = len(xs), xs[0].shape, ys[0].shape[1]
    (out,), rode = launch(
        functools.partial(weight_grad_kernel, nb, img),
        (4,),
        [pl.BlockSpec((rows, d // 4), lambda j: (0, j))] * nb
        + [once((rows, n), lambda j: (0, 0))] * nb,
        [pl.BlockSpec((1, 2, d // 4, n), lambda j: (j, 0, 0, 0))],
        [jax.ShapeDtypeStruct((4, 2, d // 4, n), BF)],
        list(xs) + list(ys),
        "weight_grad",
        2 * nb * rows * d * n,
        scratch=[pltpu.VMEM((nb * img, n), BF), pltpu.VMEM((nb * (rows - img), n), BF)],
        rides=rides,
        cid=cid,
    )
    return out, rode


def pad_key(position, padded, real):
    return lax.rem(position, padded) >= real


def head_of(refs, img, h):
    cols = slice(h * HEAD_DIM, (h + 1) * HEAD_DIM)
    whole = [r[...] for r in refs]
    return (
        jnp.concatenate([w[:img, cols] for w in whole], axis=0),
        jnp.concatenate([w[img:, cols] for w in whole], axis=0),
    )


def attend_kernel(chunk, img, txt, q0, k0, v0, q1, k1, v1, o0, o1, lse_i, lse_t):
    per = img // chunk
    tp = q0.shape[0] - img
    keys = [head_of((k0, k1), img, h) for h in range(2)]
    vals = [head_of((v0, v1), img, h) for h in range(2)]
    mask = jnp.where(
        pad_key(lax.broadcasted_iota(jnp.int32, (1, 2 * tp), 1), tp, txt), NEG, 0.0
    ).astype(F32)

    def one(q_pair):
        outs, logs = [], []
        for h in range(2):
            q = q_pair[:, h * HEAD_DIM : (h + 1) * HEAD_DIM] * jnp.asarray(SCALE, BF)
            s_i = nt(q, keys[h][0])
            s_t = nt(q, keys[h][1]) + mask
            top = jnp.maximum(
                jnp.max(s_i, axis=1, keepdims=True), jnp.max(s_t, axis=1, keepdims=True)
            )
            p_i = jnp.exp(s_i - top)
            p_t = jnp.exp(s_t - top)
            total = jnp.sum(p_i, axis=1, keepdims=True) + jnp.sum(p_t, axis=1, keepdims=True)
            inv = 1.0 / total
            o = nn((p_i * inv).astype(BF), vals[h][0]) + nn((p_t * inv).astype(BF), vals[h][1])
            outs.append(o.astype(BF))
            logs.append((top + jnp.log(total)).reshape(1, -1))
        return jnp.concatenate(outs, axis=1), logs

    for z, (q_ref, o_ref) in enumerate(((q0, o0), (q1, o1))):

        def step(c, carry, z=z, q_ref=q_ref, o_ref=o_ref):
            r = pl.multiple_of(c * chunk, chunk)
            o, logs = one(q_ref[pl.ds(r, chunk), :])
            o_ref[pl.ds(r, chunk), :] = o
            for h in range(2):
                lse_i[0, h, pl.ds(z * per + c, 1), :] = logs[h]
            return carry

        lax.fori_loop(0, per, step, 0)
    o, logs = one(jnp.concatenate([q0[img:, :], q1[img:, :]], axis=0))
    o0[img:, :] = o[:tp]
    o1[img:, :] = o[tp:]
    for h in range(2):
        lse_t[0, h, 0:1, :] = logs[h]


def attend_back_kernel(
    chunk, img, txt, q0, k0, v0, q1, k1, v1, g0, g1, lse_i, lse_t, d0, d1, sums, dk_i, dv_i, dk_t, dv_t
):
    per = img // chunk
    tp = q0.shape[0] - img
    hp = pl.program_id(0)
    pairs = pl.num_programs(0)
    width = 2 * HEAD_DIM
    keys = [head_of((k0, k1), img, h) for h in range(2)]
    vals = [head_of((v0, v1), img, h) for h in range(2)]
    mask = jnp.where(
        pad_key(lax.broadcasted_iota(jnp.int32, (2 * tp, 1), 0), tp, txt), NEG, 0.0
    ).astype(F32)
    dk_i[...] = jnp.zeros_like(dk_i)
    dv_i[...] = jnp.zeros_like(dv_i)
    dk_t[...] = jnp.zeros_like(dk_t)
    dv_t[...] = jnp.zeros_like(dv_t)

    def one(q_pair, g_pair, logs):
        outs = []
        for h in range(2):
            cols = slice(h * HEAD_DIM, (h + 1) * HEAD_DIM)
            q = q_pair[:, cols] * jnp.asarray(SCALE, BF)
            g = g_pair[:, cols]
            p_i = jnp.exp(nt(keys[h][0], q) - logs[h])
            p_t = jnp.exp(nt(keys[h][1], q) + mask - logs[h])
            dp_i = nt(vals[h][0], g)
            dp_t = nt(vals[h][1], g)
            delta = jnp.sum(p_i * dp_i, axis=0, keepdims=True) + jnp.sum(
                p_t * dp_t, axis=0, keepdims=True
            )
            dv_i[h] += nn(p_i.astype(BF), g)
            dv_t[h] += nn(p_t.astype(BF), g)
            ds_i = (p_i * (dp_i - delta)).astype(BF)
            ds_t = (p_t * (dp_t - delta)).astype(BF)
            dk_i[h] += nn(ds_i, q)
            dk_t[h] += nn(ds_t, q)
            dq = tn(ds_i, keys[h][0]) + tn(ds_t, keys[h][1])
            outs.append((dq * SCALE).astype(BF))
        return jnp.concatenate(outs, axis=1)

    def cols_of(kind):
        return pl.ds(pl.multiple_of((kind * pairs + hp) * width, width), width)

    def column_sum(v):
        return jnp.sum(v.astype(F32), axis=0, keepdims=True)

    q_sum = jnp.zeros((1, width), F32)
    for z, (q_ref, g_ref, d_ref) in enumerate(((q0, g0, d0), (q1, g1, d1))):

        def step(c, total, z=z, q_ref=q_ref, g_ref=g_ref, d_ref=d_ref):
            r = pl.multiple_of(c * chunk, chunk)
            logs = [lse_i[0, h, pl.ds(z * per + c, 1), :] for h in range(2)]
            dq = one(q_ref[pl.ds(r, chunk), :], g_ref[pl.ds(r, chunk), :], logs)
            d_ref[pl.ds(r, chunk), cols_of(0)] = dq
            return total + column_sum(dq)

        q_sum = lax.fori_loop(0, per, step, q_sum)
    logs = [lse_t[0, h, 0:1, :] for h in range(2)]
    dq = one(
        jnp.concatenate([q0[img:, :], q1[img:, :]], axis=0),
        jnp.concatenate([g0[img:, :], g1[img:, :]], axis=0),
        logs,
    )
    d0[img:, cols_of(0)] = dq[:tp]
    d1[img:, cols_of(0)] = dq[tp:]
    sums[0, 0:1] = q_sum
    sums[0, 1:2] = column_sum(dq)
    for kind, image, text in ((1, dk_i, dk_t), (2, dv_i, dv_t)):
        both = jnp.concatenate([image[0].astype(BF), image[1].astype(BF)], axis=1)
        d0[:img, cols_of(kind)] = both[:img]
        d1[:img, cols_of(kind)] = both[img:]
        both_t = jnp.concatenate([text[0].astype(BF), text[1].astype(BF)], axis=1)
        d0[img:, cols_of(kind)] = both_t[:tp]
        d1[img:, cols_of(kind)] = both_t[tp:]
        if kind == 2:
            sums[0, 2:3] = column_sum(both)
            sums[0, 3:4] = column_sum(both_t)


def qkv_specs(rows, pairs):
    width = 2 * HEAD_DIM
    return [
        pl.BlockSpec((rows, width), lambda h, kind=kind: (0, kind * pairs + h)) for kind in range(3)
    ] * 2


def lse_specs(n_chunks, chunk, tp):
    return [
        pl.BlockSpec((1, 2, n_chunks, chunk), lambda h: (h, 0, 0, 0)),
        pl.BlockSpec((1, 2, 1, 2 * tp), lambda h: (h, 0, 0, 0)),
    ]


def attention(near, far, img, txt, chunk, slot, rides=(), cid=None):
    rows, columns = near.shape[0], near.shape[1] // 3
    tp, width = rows - img, 2 * HEAD_DIM
    pairs, n_chunks = columns // width, 2 * img // chunk
    tile = pl.BlockSpec((rows, width), lambda h: (0, h))
    return launch(
        functools.partial(attend_kernel, chunk, img, txt),
        (pairs,),
        qkv_specs(rows, pairs),
        [tile, tile] + lse_specs(n_chunks, chunk, tp),
        [jax.ShapeDtypeStruct((rows, columns), BF)] * 2
        + [
            jax.ShapeDtypeStruct((pairs, 2, n_chunks, chunk), F32),
            jax.ShapeDtypeStruct((pairs, 2, 1, 2 * tp), F32),
        ],
        [near, near, near, far, far, far],
        f"attend_{slot}",
        80 * pairs * rows * rows * HEAD_DIM,
        rides=rides,
        cid=cid,
    )


def attention_back(
    near, far, grad_near, grad_far, lse_i, lse_t, img, txt, chunk, slot, rides=(), cid=None
):
    rows, columns = near.shape[0], near.shape[1] // 3
    tp, width = rows - img, 2 * HEAD_DIM
    pairs, n_chunks = columns // width, 2 * img // chunk
    tile = pl.BlockSpec((rows, width), lambda h: (0, h))
    whole = pl.BlockSpec((rows, 3 * columns), lambda h: (0, 0))
    return launch(
        functools.partial(attend_back_kernel, chunk, img, txt),
        (pairs,),
        qkv_specs(rows, pairs) + [tile, tile] + lse_specs(n_chunks, chunk, tp),
        [whole, whole, pl.BlockSpec((1, 4, width), lambda h: (h, 0, 0))],
        [jax.ShapeDtypeStruct((rows, 3 * columns), BF)] * 2
        + [jax.ShapeDtypeStruct((pairs, 4, width), F32)],
        [near, near, near, far, far, far, grad_near, grad_far, lse_i, lse_t],
        f"attend_back_{slot}",
        200 * pairs * rows * rows * HEAD_DIM,
        scratch=[
            pltpu.VMEM((2, 2 * img, HEAD_DIM), F32),
            pltpu.VMEM((2, 2 * img, HEAD_DIM), F32),
            pltpu.VMEM((2, 2 * tp, HEAD_DIM), F32),
            pltpu.VMEM((2, 2 * tp, HEAD_DIM), F32),
        ],
        rides=rides,
        cid=cid,
    )


class Layout:
    def __init__(self, dp_size, tensor_size):
        dp_bits = dp_size.bit_length() - 1
        t_bits = tensor_size.bit_length() - 1
        self.dp = tuple(f"d{i}" for i in range(dp_bits))
        self.tensor = tuple(f"t{i}" for i in range(t_bits))
        self.names = self.dp + self.tensor
        self.compact = dp_size == 8 and tensor_size == 4
        self.p = self.tensor[-1]
        if self.compact:
            self.y, self.x, self.q = self.dp
            self.zh = self.tensor[0]
            self.upper = ()
        else:
            self.q = self.tensor[-2]
            self.upper = self.tensor[:-2]
        self.rest = tuple(n for n in self.names if n not in (self.p, self.q))

    def my_columns(self, v):
        shards = 2 ** len(self.upper)
        part = v.shape[-1] // (4 * shards)
        v = v.reshape(v.shape[:-1] + (shards, 4, part))
        at = index_of((self.q, self.p))
        v = lax.dynamic_index_in_dim(v, at, v.ndim - 2, keepdims=False)
        return v.reshape(v.shape[:-2] + (shards * part,))

    def all_columns(self, v):
        shards = 2 ** len(self.upper)
        g = gather_bits(v[None], (self.p, self.q))
        g = g.reshape((4,) + v.shape[:-1] + (shards, v.shape[-1] // shards))
        g = jnp.moveaxis(g, 0, -2)
        return g.reshape(v.shape[:-1] + (4 * v.shape[-1],))

    def gather_rows(self, own, end=()):
        pair = after(swap(own, self.p), *end)
        return [[own, swap(own, self.q)], [pair, swap(pair, self.q)]]

    def sum_far(self, w, blocks, img):
        (send, keep), unused = rows_nt([blocks[1][1], blocks[1][0]], w, img, (BF, F32))
        return (keep + swap(send, self.q).astype(F32)).astype(BF)

    def sum_near(self, w, blocks, img, rides=(), cid=None):
        (send, keep), rode = rows_nt([blocks[0][1], blocks[0][0]], w, img, (BF, F32), rides, cid)
        return keep + swap(send, self.q).astype(F32), rode

    def gather_weight(self, w):
        w = lax.all_gather(w, self.dp, axis=1, tiled=True)
        if self.upper:
            w = lax.all_gather(w, self.upper, axis=3, tiled=True)
        return jnp.swapaxes(w.reshape(2, 4, w.shape[1] // 4, -1), 0, 1)

    def trade_shards(self, w, end=()):
        w = w.reshape(w.shape[0], w.shape[1], -1)
        joint = (self.q, self.zh)
        same = lax.axis_index(self.zh) == lax.axis_index(self.q)
        cross = lax.ppermute(w, joint, [(1, 2), (2, 1)])
        second = lax.ppermute(w, joint, [(0, 1), (3, 2), (2, 0), (1, 3)])
        cross, second = after((cross, second), *end)
        first = jnp.where(same, w, cross)
        low = lax.axis_index(self.zh) == 0
        return jnp.concatenate(
            [jnp.where(low, first, second), jnp.where(low, second, first)], axis=1
        )

    def spread_near(self, own):
        return [swap(own[0], self.x), swap(own[1], self.y)]

    def spread_rows(self, own, nears):
        x, y = lax.axis_index(self.x), lax.axis_index(self.y)
        whole = jnp.zeros((4,) + own.shape, BF)
        for stream, far_axis in enumerate((self.y, self.x)):
            mine, near = own[stream], nears[stream]
            both, far = swap(near, far_axis), swap(mine, far_axis)
            dx, dy = (near, far) if stream == 0 else (far, near)
            for block, at in (
                (mine, 2 * y + x),
                (dx, 2 * y + 1 - x),
                (dy, 2 * (1 - y) + x),
                (both, 2 * (1 - y) + 1 - x),
            ):
                whole = lax.dynamic_update_slice(whole, block[None, None], (at, stream, 0, 0))
        return whole

    def spread_rows_async(self, own):
        own = own.reshape(own.shape[0], -1, own.shape[-1])
        return lax.all_gather(own, (self.y, self.x), axis=0, tiled=False)

    def trade_ride(self, array, back=False):
        if back:
            array = array.reshape(2, 2, -1, array.shape[-1])
        return TradeRide(array, self.zh, self.q, back)

    def scatter_generic(self, g, kinds):
        g = jnp.swapaxes(g.astype(F32), 0, 1).reshape(2, 4 * g.shape[2], kinds, -1)
        g = lax.psum_scatter(g, self.dp, scatter_dimension=1, tiled=True)
        if self.upper:
            g = lax.psum_scatter(g, self.upper, scatter_dimension=3, tiled=True)
        return g

    def sum_plane_async(self, g):
        return lax.psum_scatter(g, (self.y, self.x), scatter_dimension=0, tiled=False)

    def plane_rides(self, g):
        g = g.reshape((2, 2) + g.shape[1:])
        shape = (2,) + g.shape[3:]

        def along_x(source, target):
            x = 1 - lax.axis_index(self.x)
            return [(source.at[k, x, 0], target.at[k]) for k in range(2)]

        def along_y(source, target):
            y = 1 - lax.axis_index(self.y)
            return [(source.at[y, k, 1], target.at[k]) for k in range(2)]

        return [
            NeighbourRide(g, self.x, shape, along_x, 2),
            NeighbourRide(g, self.y, shape, along_y, 2),
        ]

    def sum_plane_first(self, g, arrived):
        x, y = lax.axis_index(self.x), lax.axis_index(self.y)
        g = g.reshape((2, 2) + g.shape[1:])
        sums = []
        for stream in range(2):
            at, size = (((0, x, 0), (2, 1)), ((y, 0, 1), (1, 2)))[stream]
            v = lax.dynamic_slice(g, at + (0, 0), size + (1,) + g.shape[3:])
            v = v.reshape(arrived[stream].shape)
            sums.append(v.astype(F32) + arrived[stream].astype(F32))
        return sums

    def sum_plane_last(self, sums):
        done = []
        for v, axis in zip(sums, (self.y, self.x)):
            at = lax.axis_index(axis)
            low, high = v[0], v[1]
            keep, send = jnp.where(at == 0, low, high), jnp.where(at == 0, high, low)
            done.append(keep + swap(send.astype(BF), axis).astype(F32))
        return jnp.stack(done)

    def trade_parts(self, g):
        g = g.reshape(2, 2, -1, g.shape[-1])
        zh = lax.axis_index(self.zh)
        return [lax.dynamic_index_in_dim(g, k, 1, keepdims=False) for k in (zh, 1 - zh)]

    def trade_sends(self, g):
        first, second = self.trade_parts(g)
        joint = (self.q, self.zh)
        return [
            lax.ppermute(first.astype(BF), joint, [(1, 2), (2, 1)]),
            lax.ppermute(second.astype(BF), joint, [(1, 0), (2, 3), (0, 2), (3, 1)]),
        ]

    def trade_adds(self, g, arrived, kinds):
        same = lax.axis_index(self.zh) == lax.axis_index(self.q)
        total = jnp.where(same, self.trade_parts(g)[0].astype(F32), arrived[0].astype(F32))
        total += arrived[1].astype(F32)
        return total.reshape(2, total.shape[1], kinds, -1)


def norm_parts(values):
    average = jnp.mean(values, axis=-1, keepdims=True)
    centred = values - average
    variance = jnp.mean(centred * centred, axis=-1, keepdims=True)
    inverse = lax.rsqrt(variance + 1e-06)
    return centred * inverse, inverse


def norm_back(normed, inverse, grad_in):
    first_mean = jnp.mean(grad_in, axis=-1, keepdims=True)
    cross_mean = jnp.mean(grad_in * normed, axis=-1, keepdims=True)
    return inverse * (grad_in - first_mean - normed * cross_mean)


def body(
    lay,
    image_in,
    text_in,
    condition,
    live_slots,
    ada_weight,
    ada_bias,
    qkv_weight,
    qv_bias,
    proj_weight,
    proj_bias,
    up_weight,
    up_bias,
    down_weight,
    down_bias,
    image_grad,
    text_grad,
):
    width = image_in.shape[1]
    part = qkv_weight.shape[2]
    columns = qkv_weight.shape[3]
    img_rows, txt_rows = image_in.shape[0], text_in.shape[0]
    txt_pad = -(-txt_rows // 16) * 16
    group_slots = condition.shape[0]
    dp_index, t_index = index_of(lay.dp), index_of(lay.tensor)
    t_count = 2 ** len(lay.tensor)
    assert group_slots * 2 == t_count
    my_slot = t_index // 2
    dp_up, t_up = lay.dp[::-1], lay.tensor[::-1]

    rows = img_rows + txt_pad
    is_image = lax.broadcasted_iota(jnp.int32, (rows, 1), 0) < img_rows

    def pack(image, text):
        return jnp.concatenate([image, jnp.pad(text, ((0, txt_pad - txt_rows), (0, 0)))], axis=0)

    def spread(per_stream):
        return jnp.where(is_image, per_stream[0], per_stream[1])

    def total(v):
        return jnp.stack([jnp.sum(v[:img_rows], axis=0), jnp.sum(v[img_rows:], axis=0)])

    def flat(blocks):
        return blocks[0] + blocks[1]

    def unflat(v):
        return [list(v[:2]), list(v[2:4])]

    qkv_local = jnp.swapaxes(qkv_weight, 1, 2)
    proj_local = jnp.swapaxes(proj_weight, 1, 2)[:, :, None]
    up_local = up_weight[:, :, None]
    down_local = jnp.swapaxes(down_weight, 1, 2)[:, :, None]
    compact = lay.compact
    if compact:
        qkv_own = lay.trade_shards(qkv_local)
        qkv_near = lay.spread_near(qkv_own)
    else:
        qkv_full, up_full, proj_full, down_full = [
            lay.gather_weight(w) for w in (qkv_local, up_local, proj_local, down_local)
        ]

    cond_all = gather_bits(condition, dp_up).astype(F32)
    silu_all = jax.nn.silu(cond_all).astype(BF)
    silu_mine = lax.dynamic_slice_in_dim(silu_all, dp_index * part, part, 1)
    mod = jnp.einsum("sd,tdkc->stkc", silu_mine, ada_weight, preferred_element_type=F32)
    mod = scatter_bits(mod, lay.dp)
    if compact:
        mod = after(mod, qkv_own)
    mod = gather_bits(mod[None], t_up)
    mod = lax.dynamic_index_in_dim(mod, my_slot, 1, keepdims=False)
    mod = jnp.moveaxis(mod, 0, 2).reshape(2, 6, width) + ada_bias.astype(F32)
    live = lax.dynamic_index_in_dim(live_slots, my_slot, 0, keepdims=False).astype(F32)

    mods = [spread(mod[:, k]) for k in range(6)]
    shift_one, scale_one, gate_one, shift_two, scale_two, gate_two = mods

    inputs = pack(image_in, text_in).astype(F32)
    grad_out = live * pack(image_grad, text_grad).astype(F32)
    grad_two = (gate_two * grad_out).astype(BF)

    first_norm = norm_parts(inputs)
    first_hidden = (first_norm[0] * (1.0 + scale_one) + shift_one).astype(BF)
    if compact:
        first_hidden = after(first_hidden, qkv_near)
    first = lay.gather_rows(first_hidden)
    if compact:
        qkv_full = lay.spread_rows(qkv_own, qkv_near)
    qv = lay.my_columns(qv_bias.astype(F32))
    qkv_bias = jnp.concatenate([qv[:, 0], jnp.zeros_like(qv[:, 0]), qv[:, 1]], axis=1)
    heads_n = qv.shape[2]
    img = img_rows

    def ride(array, start, stop):
        return row_ride(array, lay.p, start, stop)

    cut = rows // 3 // 16 * 16
    extra = [[], [], []]
    if compact:
        extra = [
            [lay.trade_ride(w.reshape(w.shape[0], part, -1))]
            for w in (proj_local, up_local[:1], up_local[1:])
        ]
    qkv, rode = rows_nn(
        flat(first), qkv_full, img, "bias", bias=qkv_bias, rides=extra[0], cid=1
    )
    qkv = unflat(qkv)
    chunk = min(256, img_rows)
    if compact:
        proj_full = lay.spread_rows_async(rode[0])
    other, rode = attention(
        qkv[0][1], qkv[1][1], img, txt_rows, chunk, 1, rides=extra[1], cid=2
    )
    if compact:
        up_full = [lay.spread_rows_async(rode[0])]
        qkv, other = after((qkv, other), proj_full)
    mine, rode = attention(
        qkv[0][0],
        qkv[1][0],
        img,
        txt_rows,
        chunk,
        0,
        rides=[ride(grad_two, 0, cut)] + extra[2],
        cid=10,
    )
    grad_two_pair = rode[:1]
    heads_out = [[mine[z], other[z]] for z in range(2)]
    if compact:
        up_full.append(lay.spread_rows_async(rode[1]))
        down_own = lay.trade_shards(after(down_local, mine))

    far = swap(lay.sum_far(proj_full, heads_out, img), lay.p)
    near, unused = lay.sum_near(proj_full, heads_out, img)
    branch_one = near + far.astype(F32) + spread(proj_bias.astype(F32))
    middle = inputs + gate_one * branch_one
    second_norm = norm_parts(middle)
    second_hidden = (second_norm[0] * (1.0 + scale_two) + shift_two).astype(BF)
    if compact:
        second_hidden, down_own = tie(second_hidden, down_own)
        down_full = lay.spread_rows_async(down_own)
    second = lay.gather_rows(second_hidden)
    up_mine = lay.my_columns(up_bias.astype(F32))
    up_n = up_mine.shape[1]
    up_out, rode = rows_nn(
        flat(second), up_full, img, "gelu", bias=up_mine, rides=[ride(grad_two, cut, rows)], cid=13
    )
    grad_two_pair = jnp.concatenate(grad_two_pair + rode, axis=0)
    grad_two_blocks = [
        [grad_two, swap(grad_two, lay.q)], [grad_two_pair, swap(grad_two_pair, lay.q)]
    ]
    activated, slopes = up_out[:4], up_out[4:]
    far = lay.sum_far(down_full, unflat(activated), img)
    cut = rows * 21 // 37 // 16 * 16
    back_out, rode = rows_nn(
        flat(grad_two_blocks), down_full, img, "slope", slopes=slopes, rides=[ride(far, 0, cut)], cid=3
    )
    grad_inner, up_part = back_out[:4], back_out[4].reshape(2, up_n)
    down_grads, rode_two = weight_grad(
        after(flat(grad_two_blocks), grad_inner), activated, img, rides=[ride(far, cut, rows)], cid=4
    )
    far = jnp.concatenate(rode + rode_two, axis=0)
    if compact:
        down_plane = lay.sum_plane_async(down_grads)
    far_two = lay.sum_far(up_full, after(unflat(grad_inner), down_grads), img)
    cut, cut_two = rows * 11 // 37 // 16 * 16, rows * 22 // 37 // 16 * 16
    near_two, rode = lay.sum_near(up_full, unflat(grad_inner), img, [ride(far_two, 0, cut)], 5)
    up_grads, rode_two = weight_grad(
        after(flat(second), near_two), grad_inner, img, rides=[ride(far_two, cut_two, rows)], cid=6
    )
    if compact:
        up_plane = lay.sum_plane_async(up_grads)
    near, rode_three = lay.sum_near(
        down_full, after(unflat(activated), up_grads), img, [ride(far_two, cut, cut_two)], 7
    )
    far_two = jnp.concatenate(rode + rode_three + rode_two, axis=0)
    branch_two = near + far.astype(F32) + spread(down_bias.astype(F32))
    outputs = (live * (middle + gate_two * branch_two)).astype(BF)
    grad_hidden_two = near_two + far_two.astype(F32)
    grad_middle = grad_out + norm_back(
        second_norm[0], second_norm[1], grad_hidden_two * (1.0 + scale_two)
    )
    grad_one = (gate_one * grad_middle).astype(BF)
    if compact:
        grad_one = after(grad_one, down_plane)
    grad_one_blocks = lay.gather_rows(grad_one)
    grad_heads = unflat(rows_nn(flat(grad_one_blocks), proj_full, img, "plain")[0])

    def back(c, saved, heads, rides, cid):
        return attention_back(
            qkv[0][c],
            qkv[1][c],
            heads[0][c],
            heads[1][c],
            saved[2],
            saved[3],
            img,
            txt_rows,
            chunk,
            c,
            rides,
            cid,
        )

    grad_other, down_sums = back(
        1, other, grad_heads, [lay.trade_ride(down_plane, True)] if compact else (), 11
    )
    proj_grads, unused = weight_grad(
        after(flat(grad_one_blocks), grad_other), flat(heads_out), img
    )
    if compact:
        proj_plane = lay.sum_plane_async(proj_grads)
    grad_mine, up_sums = back(
        0,
        mine,
        after(grad_heads, proj_grads),
        [lay.trade_ride(up_plane, True)] if compact else (),
        12,
    )
    grad_qkv = [[grad_mine[z], grad_other[z]] for z in range(2)]
    far = lay.sum_far(qkv_full, grad_qkv, img)
    cut = rows * 16 // 37 // 16 * 16
    rides = [ride(far, 0, cut)]
    if compact:
        rides.append(lay.trade_ride(proj_plane, True))
    qkv_grads, rode = weight_grad(flat(first), flat(grad_qkv), img, rides=rides, cid=8)
    rides = [ride(far, cut, rows)]
    if compact:
        proj_sums = rode[1]
        rides += lay.plane_rides(qkv_grads)
    near, rode_two = lay.sum_near(qkv_full, after(grad_qkv, qkv_grads), img, rides, 9)
    far = jnp.concatenate(rode[:1] + rode_two[:1], axis=0)
    if compact:
        down_grad, up_grad, proj_grad = [
            (v[0].astype(F32) + v[1].astype(F32))[:, :, None]
            for v in (down_sums[0], up_sums[0], proj_sums)
        ]
        plane_sums = lay.sum_plane_first(qkv_grads, rode_two[1:3])
    else:
        down_grad, up_grad, proj_grad = [
            lay.scatter_generic(g, 1) for g in (down_grads, up_grads, proj_grads)
        ]
        qkv_grad = lay.scatter_generic(qkv_grads, 3)
    grad_hidden_one = near + far.astype(F32)
    input_grads = grad_middle + norm_back(
        first_norm[0], first_norm[1], grad_hidden_one * (1.0 + scale_one)
    )

    grad_mod = jnp.stack(
        [
            total(grad_hidden_one),
            total(grad_hidden_one * first_norm[0]),
            total(branch_one * grad_middle),
            total(grad_hidden_two),
            total(grad_hidden_two * second_norm[0]),
            total(branch_two * grad_out),
        ],
        axis=1,
    )
    if compact:
        plane_sums, grad_mod = tie(plane_sums, grad_mod)
        qkv_plane = lay.sum_plane_last(plane_sums)
    grad_mod_own = grad_mod
    grad_mod = sum_bits(grad_mod, (lay.p,))
    grad_mod = gather_bits(grad_mod[None], t_up[1:])
    if compact:
        qkv_plane, grad_mod = tie(qkv_plane, grad_mod)
    grad_mod = lax.dynamic_slice_in_dim(grad_mod, t_index * columns, columns, 3)
    grad_mod = gather_bits(grad_mod, dp_up)
    high = lax.Precision.HIGHEST
    ada_grad = jnp.einsum("sd,stkc->tdkc", silu_mine.astype(F32), grad_mod, precision=high)
    cond_terms = jnp.einsum("stkc,tdkc->sd", grad_mod, ada_weight.astype(F32), precision=high)
    cond_terms = gather_bits(cond_terms[None], dp_up)
    cond_terms = lax.dynamic_slice_in_dim(cond_terms, dp_index * group_slots, group_slots, 1)
    cond_terms = jnp.swapaxes(cond_terms, 0, 1).reshape(group_slots, width)
    if compact:
        arrived = lay.trade_sends(qkv_plane)
        cond_terms, arrived = tie(cond_terms, arrived)
        qkv_grad = lay.trade_adds(qkv_plane, arrived, 3)
    down_grad = jnp.swapaxes(down_grad[:, :, 0], 1, 2)
    proj_grad = jnp.swapaxes(proj_grad[:, :, 0], 1, 2)
    up_grad = up_grad[:, :, 0]
    qkv_grad = jnp.swapaxes(qkv_grad, 1, 2)
    cond_terms = sum_bits(cond_terms, t_up)
    cond_terms = lax.dynamic_slice_in_dim(cond_terms, t_index * columns, columns, 1)
    cond_slice = lax.dynamic_slice_in_dim(condition.astype(F32), t_index * columns, columns, 1)
    unused, silu_pull = jax.vjp(jax.nn.silu, cond_slice)
    condition_grad = silu_pull(cond_terms)[0]
    own_part = [total(grad_one.astype(F32))[:, None], total(grad_two.astype(F32))[:, None]]
    own_part = sum_bits(jnp.concatenate(own_part + [grad_mod_own], axis=1), (lay.p, lay.q))
    sums = grad_mine[2] + grad_other[2]
    pairs = sums.shape[0]
    qv_part = jnp.transpose(sums.reshape(pairs, 2, 2, -1), (2, 1, 0, 3)).reshape(2, 2, heads_n)
    if compact:
        qv_part = after(qv_part, near)
    packed = jnp.concatenate([qv_part.reshape(-1), up_part.reshape(-1), own_part.reshape(-1)])
    packed = sum_bits(packed.reshape(-1, 128), lay.rest).reshape(-1)
    cut_one, cut_two = qv_part.size, qv_part.size + up_part.size
    qv_bias_grad = lay.all_columns(packed[:cut_one].reshape(qv_part.shape))
    up_bias_grad = lay.all_columns(packed[cut_one:cut_two].reshape(up_part.shape))
    own_part = packed[cut_two:].reshape(own_part.shape)
    return (
        outputs[:img_rows],
        outputs[img_rows : img_rows + txt_rows],
        input_grads[:img_rows],
        input_grads[img_rows : img_rows + txt_rows],
        condition_grad,
        ada_grad,
        own_part[:, 2:],
        qkv_grad,
        qv_bias_grad,
        proj_grad,
        own_part[:, 0],
        up_grad,
        up_bias_grad,
        down_grad,
        own_part[:, 1],
    )


def solution(mesh):
    lay = Layout(mesh.shape["dp"], mesh.shape["tensor"])
    bits = Mesh(mesh.devices.reshape((2,) * len(lay.names)), lay.names)
    dp, tensor, every = lay.dp, lay.tensor, lay.names
    in_specs = (
        P(every, None),
        P(every, None),
        P(dp, None),
        P(dp),
        P(None, dp, None, tensor),
        P(),
        P(None, None, dp, tensor),
        P(),
        P(None, tensor, dp),
        P(),
        P(None, dp, tensor),
        P(),
        P(None, tensor, dp),
        P(),
        P(every, None),
        P(every, None),
    )
    out_specs = (
        P(every, None),
        P(every, None),
        P(every, None),
        P(every, None),
        P(dp, tensor),
        P(None, dp, None, tensor),
        P(),
        P(None, None, dp, tensor),
        P(),
        P(None, tensor, dp),
        P(),
        P(None, dp, tensor),
        P(),
        P(None, tensor, dp),
        P(),
    )
    return jax.shard_map(
        functools.partial(body, lay), mesh=bits, in_specs=in_specs, out_specs=out_specs, check_vma=False
    )
```

```python
import functools

import jax
import jax.numpy as jnp
from jax import lax
from jax.experimental import pallas as pl
from jax.experimental.pallas import tpu as pltpu
from jax.sharding import Mesh
from jax.sharding import PartitionSpec as P

HEAD_DIM = 64
SCALE = HEAD_DIM ** (-0.5)
BF = jnp.bfloat16
F32 = jnp.float32
NEG = -1e30


def swap(v, axis):
    return lax.ppermute(v, axis, [(0, 1), (1, 0)])


def gather_bits(v, axes):
    for axis in axes:
        other = swap(v, axis)
        first = lax.axis_index(axis) == 0
        v = jnp.concatenate([jnp.where(first, v, other), jnp.where(first, other, v)], 0)
    return v


def scatter_bits(v, axes):
    for axis in axes:
        first = lax.axis_index(axis) == 0
        half = v.shape[0] // 2
        low, high = v[:half], v[half:]
        v = jnp.where(first, low, high) + swap(jnp.where(first, high, low), axis)
    return v


def sum_bits(v, axes):
    for axis in axes:
        v = v + swap(v, axis)
    return v


def after(v, *deps):
    return lax.optimization_barrier((v,) + deps)[0]


def tie(*vs):
    return lax.optimization_barrier(vs)


def index_of(axes):
    out = 0
    for axis in axes:
        out = out * 2 + lax.axis_index(axis)
    return out


def nt(a, b):
    return lax.dot_general(a, b, (((1,), (1,)), ((), ())), preferred_element_type=F32)


def nn(a, b):
    return lax.dot_general(a, b, (((1,), (0,)), ((), ())), preferred_element_type=F32)


def tn(a, b):
    return lax.dot_general(a, b, (((0,), (0,)), ((), ())), preferred_element_type=F32)


VMEM_LIMIT = 52 * 2**20
GELU_C = 0.7978845608028654


def launch(kernel, grid, in_specs, out_specs, out_shape, args, name, flops, scratch=(), rides=(), cid=None):
    n_in, n_out = len(args), len(out_shape)
    params = dict(vmem_limit_bytes=VMEM_LIMIT)
    cost = pl.CostEstimate(flops=flops, bytes_accessed=flops // 512, transcendentals=0)
    if not rides:
        outs = pl.pallas_call(
            kernel,
            grid=grid,
            in_specs=in_specs,
            out_specs=out_specs,
            out_shape=out_shape,
            scratch_shapes=list(scratch),
            compiler_params=pltpu.CompilerParams(**params),
            cost_estimate=cost,
            name=name,
        )(*args)
        return list(outs), []
    partners = sorted({partner for ride in rides for partner in ride.partners})
    n_rides, sems = len(rides), sum(ride.sems for ride in rides)

    def body(*refs):
        ins, rest = refs[:n_in], refs[n_in:]
        sources, rest = rest[:n_rides], rest[n_rides:]
        outs, rest = rest[:n_out], rest[n_out:]
        targets, rest = rest[:n_rides], rest[n_rides:]
        own, (send, recv) = rest[:-2], rest[-2:]
        steps, at = [], 0
        for source, target, ride in zip(sources, targets, rides):
            steps.append(ride.moves(source, target, lambda k, at=at: send.at[at + k], lambda k, at=at: recv.at[at + k]))
            at += ride.sems

        barrier = pltpu.get_barrier_semaphore()
        for partner in partners:
            pl.semaphore_signal(
                barrier,
                1,
                device_id={axis: 1 - lax.axis_index(axis) for axis in partner},
                device_id_type=pl.DeviceIdType.MESH,
            )
        pl.semaphore_wait(barrier, len(partners))
        for start, unused in steps:
            start()
        pltpu.emit_pipeline(
            lambda *blocks: kernel(*blocks, *own),
            grid=grid,
            in_specs=list(in_specs),
            out_specs=list(out_specs),
        )(*ins, *outs)
        for unused, wait in steps:
            wait()

    anywhere = pl.BlockSpec(memory_space=pl.ANY)
    outs = pl.pallas_call(
        body,
        in_specs=[anywhere] * (n_in + n_rides),
        out_specs=[anywhere] * (n_out + n_rides),
        out_shape=list(out_shape) + [ride.shape for ride in rides],
        scratch_shapes=list(scratch)
        + [pltpu.SemaphoreType.DMA((sems,)), pltpu.SemaphoreType.DMA((sems,))],
        compiler_params=pltpu.CompilerParams(collective_id=cid, has_side_effects=True, **params),
        cost_estimate=cost,
        name=f"{name}_{cid}",
    )(*args, *[ride.array for ride in rides])
    return list(outs[:n_out]), list(outs[n_out:])


class NeighbourRide:
    def __init__(self, array, axis, shape, views, sems):
        self.array, self.axis, self.views, self.sems = array, axis, views, sems
        self.shape = jax.ShapeDtypeStruct(shape, array.dtype)
        self.partners = [(axis,)]

    def moves(self, source, target, send, recv):
        other = {self.axis: 1 - lax.axis_index(self.axis)}
        made = [
            pltpu.make_async_remote_copy(
                src_ref=src,
                dst_ref=dst,
                send_sem=send(k),
                recv_sem=recv(k),
                device_id=other,
                device_id_type=pl.DeviceIdType.MESH,
            )
            for k, (src, dst) in enumerate(self.views(source, target))
        ]

        def start():
            for move in made:
                move.start()

        def wait():
            for move in made:
                move.wait()

        return start, wait


def row_ride(array, axis, start, stop):
    count = min(4, (stop - start) // 16)
    cuts = [start + (stop - start) // 16 * k // count * 16 for k in range(count)] + [stop]

    def views(source, target):
        return [
            (source.at[pl.ds(a, b - a)], target.at[pl.ds(a - start, b - a)])
            for a, b in zip(cuts, cuts[1:])
        ]

    return NeighbourRide(array, axis, (stop - start,) + array.shape[1:], views, count)


class TradeRide:
    sems = 3

    def __init__(self, array, zh, q, back):
        self.array, self.zh, self.q, self.back = array, zh, q, back
        streams, part, n = array.shape[0], array.shape[-2], array.shape[-1]
        shape = (2, streams, part, n) if back else (streams, 2, part, n)
        self.shape = jax.ShapeDtypeStruct(shape, array.dtype)
        self.partners = [(q,), (zh,), (q, zh)]

    def moves(self, source, target, send, recv):
        zh, q = lax.axis_index(self.zh), lax.axis_index(self.q)
        same = zh == q

        def remote(k, src, dst, at, to_zh, to_q):
            return pltpu.make_async_remote_copy(
                src_ref=src,
                dst_ref=dst,
                send_sem=send(k),
                recv_sem=recv(at),
                device_id={self.zh: to_zh, self.q: to_q},
                device_id_type=pl.DeviceIdType.MESH,
            )

        if self.back:
            outgoing = [remote(j, source.at[:, j], target.at[zh], zh, q, j) for j in range(2)]
            arriving = [remote(j, source.at[:, j], target.at[j], j, q, j) for j in range(2)]
            local = pltpu.make_async_copy(source.at[:, q], target.at[zh], send(2))
            mine = [jnp.logical_and(same, q == j) for j in range(2)]
        else:
            outgoing = [remote(j, source, target.at[:, q], q, j, zh) for j in range(2)]
            arriving = [remote(j, source, target.at[:, j], j, j, zh) for j in range(2)]
            local = pltpu.make_async_copy(source, target.at[:, q], send(2))
            mine = [jnp.logical_and(same, zh == j) for j in range(2)]

        def start():
            for move, own in zip(outgoing, mine):
                pl.when(jnp.logical_not(own))(move.start)
            pl.when(same)(local.start)

        def wait():
            for move, own in zip(outgoing, mine):
                pl.when(jnp.logical_not(own))(move.wait_send)
            for move, own in zip(arriving, mine):
                pl.when(jnp.logical_not(own))(move.wait_recv)
            pl.when(same)(local.wait)

        return start, wait


def once(shape, index):
    return pl.BlockSpec(shape, index, pipeline_mode=pl.Buffered(1))


def by_stream(w):
    return [(w[0], 0), (w[1], 0)] if isinstance(w, (list, tuple)) else [(w, 0), (w, 1)]


def rows_nn_kernel(nb, img, mode, *refs):
    xs, w0, w1 = refs[:nb], refs[nb], refs[nb + 1]
    rest = refs[nb + 2 :]
    depth, tile = xs[0].shape[1], w0.shape[3]
    text = xs[0].shape[0] - img
    y_text = nn(
        jnp.concatenate([x[img:, :] for x in xs], axis=0), w1[:, 0].reshape(depth, tile)
    )
    w_img = w0[:, 0].reshape(depth, tile)
    if mode == "slope":
        sums = rest[2 * nb]
        total = [jnp.zeros((1, tile), F32), jnp.zeros((1, tile), F32)]
    for b in range(nb):
        for stream, rows in ((0, slice(0, img)), (1, slice(img, img + text))):
            y = nn(xs[b][rows, :], w_img) if stream == 0 else y_text[b * text : (b + 1) * text]
            if mode == "plain":
                rest[b][rows, :] = y.astype(BF)
            elif mode == "bias":
                rest[1 + b][rows, :] = (y + rest[0][stream]).astype(BF)
            elif mode == "gelu":
                v = y + rest[0][stream]
                inner = jnp.tanh(GELU_C * (v + 0.044715 * (v * v * v)))
                half = 0.5 * (1.0 + inner)
                rest[1 + b][rows, :] = (v * half).astype(BF)
                rest[1 + nb + b][rows, :] = half + 0.5 * v * (1.0 - inner * inner) * (
                    GELU_C * (1.0 + 3 * 0.044715 * (v * v))
                )
            else:
                y = (y * rest[b][rows, :]).astype(BF)
                rest[nb + b][rows, :] = y
                total[stream] += jnp.sum(y.astype(F32), axis=0, keepdims=True)
    if mode == "slope":
        sums[0] = total[0]
        sums[1] = total[1]


def rows_nn(xs, w, img, mode, bias=None, slopes=(), rides=(), cid=None):
    (w0, s0), (w1, s1) = by_stream(w)
    n = w0.shape[3]
    tile = 768 if n % 768 == 0 else 384
    nb, (rows, depth) = len(xs), xs[0].shape
    in_specs = [once((rows, depth), lambda j: (0, 0))] * nb
    in_specs += [
        pl.BlockSpec((4, 1, depth // 4, tile), lambda j, at=at: (0, at, 0, j)) for at in (s0, s1)
    ]
    args = list(xs) + [w0, w1]
    out_tile = pl.BlockSpec((rows, tile), lambda j: (0, j))
    vector = pl.BlockSpec((2, 1, tile), lambda j: (0, 0, j))
    shape = lambda dtype: jax.ShapeDtypeStruct((rows, n), dtype)
    if bias is not None:
        in_specs.append(vector)
        args.append(bias.reshape(2, 1, n))
    in_specs += [out_tile] * len(slopes)
    args += list(slopes)
    out_specs, out_shape = [out_tile] * nb, [shape(BF)] * nb
    if mode == "gelu":
        out_specs, out_shape = out_specs + [out_tile] * nb, out_shape + [shape(F32)] * nb
    if mode == "slope":
        out_specs.append(vector)
        out_shape.append(jax.ShapeDtypeStruct((2, 1, n), F32))
    return launch(
        functools.partial(rows_nn_kernel, nb, img, mode),
        (n // tile,),
        in_specs,
        out_specs,
        out_shape,
        args,
        f"rows_{mode}",
        2 * nb * rows * depth * n,
        rides=rides,
        cid=cid,
    )


def rows_nt_kernel(nb, img, *refs):
    xs, w0, w1, outs = refs[:nb], refs[nb], refs[nb + 1], refs[nb + 2 :]
    text = xs[0].shape[0] - img
    y_text = nt(jnp.concatenate([x[img:, :] for x in xs], axis=0), w1[:, 0].reshape(-1, xs[0].shape[1]))
    w_img = w0[:, 0].reshape(-1, xs[0].shape[1])
    for b in range(nb):
        outs[b][:img, :] = nt(xs[b][:img, :], w_img).astype(outs[b].dtype)
        outs[b][img:, :] = y_text[b * text : (b + 1) * text].astype(outs[b].dtype)


def rows_nt(xs, w, img, dtypes, rides=(), cid=None):
    nb, (rows, n) = len(xs), xs[0].shape
    (w0, s0), (w1, s1) = by_stream(w)
    quarter = w0.shape[2]
    return launch(
        functools.partial(rows_nt_kernel, nb, img),
        (2,),
        [once((rows, n), lambda j: (0, 0))] * nb
        + [
            pl.BlockSpec((2, 1, quarter, n), lambda j, at=at: (j, at, 0, 0)) for at in (s0, s1)
        ],
        [pl.BlockSpec((rows, 2 * quarter), lambda j: (0, j))] * nb,
        [jax.ShapeDtypeStruct((rows, 4 * quarter), t) for t in dtypes],
        list(xs) + [w0, w1],
        "rows_back",
        8 * nb * rows * quarter * n,
        rides=rides,
        cid=cid,
    )


def weight_grad_kernel(nb, img, *refs):
    xs, ys, out = refs[:nb], refs[nb : 2 * nb], refs[2 * nb]
    y_img, y_text = refs[2 * nb + 1 :]
    text = xs[0].shape[0] - img

    @pl.when(pl.program_id(0) == 0)
    def _():
        for b in range(nb):
            y_img[b * img : (b + 1) * img, :] = ys[b][:img, :]
            y_text[b * text : (b + 1) * text, :] = ys[b][img:, :]

    x_img = jnp.concatenate([x[:img, :] for x in xs], axis=0)
    x_text = jnp.concatenate([x[img:, :] for x in xs], axis=0)
    out[0, 0] = tn(x_img, y_img[...]).astype(BF)
    out[0, 1] = tn(x_text, y_text[...]).astype(BF)


def weight_grad(xs, ys, img, rides=(), cid=None):
    nb, (rows, d), n = len(xs), xs[0].shape, ys[0].shape[1]
    (out,), rode = launch(
        functools.partial(weight_grad_kernel, nb, img),
        (4,),
        [pl.BlockSpec((rows, d // 4), lambda j: (0, j))] * nb
        + [once((rows, n), lambda j: (0, 0))] * nb,
        [pl.BlockSpec((1, 2, d // 4, n), lambda j: (j, 0, 0, 0))],
        [jax.ShapeDtypeStruct((4, 2, d // 4, n), BF)],
        list(xs) + list(ys),
        "weight_grad",
        2 * nb * rows * d * n,
        scratch=[pltpu.VMEM((nb * img, n), BF), pltpu.VMEM((nb * (rows - img), n), BF)],
        rides=rides,
        cid=cid,
    )
    return out, rode


def pad_key(position, padded, real):
    return lax.rem(position, padded) >= real


def head_of(refs, img, h):
    cols = slice(h * HEAD_DIM, (h + 1) * HEAD_DIM)
    whole = [r[...] for r in refs]
    return (
        jnp.concatenate([w[:img, cols] for w in whole], axis=0),
        jnp.concatenate([w[img:, cols] for w in whole], axis=0),
    )


def attend_kernel(chunk, img, txt, q0, k0, v0, q1, k1, v1, o0, o1, lse_i, lse_t):
    per = img // chunk
    tp = q0.shape[0] - img
    keys = [head_of((k0, k1), img, h) for h in range(2)]
    vals = [head_of((v0, v1), img, h) for h in range(2)]
    mask = jnp.where(
        pad_key(lax.broadcasted_iota(jnp.int32, (1, 2 * tp), 1), tp, txt), NEG, 0.0
    ).astype(F32)

    def one(q_pair):
        outs, logs = [], []
        for h in range(2):
            q = q_pair[:, h * HEAD_DIM : (h + 1) * HEAD_DIM] * jnp.asarray(SCALE, BF)
            s_i = nt(q, keys[h][0])
            s_t = nt(q, keys[h][1]) + mask
            top = jnp.maximum(
                jnp.max(s_i, axis=1, keepdims=True), jnp.max(s_t, axis=1, keepdims=True)
            )
            p_i = jnp.exp(s_i - top)
            p_t = jnp.exp(s_t - top)
            total = jnp.sum(p_i, axis=1, keepdims=True) + jnp.sum(p_t, axis=1, keepdims=True)
            inv = 1.0 / total
            o = nn((p_i * inv).astype(BF), vals[h][0]) + nn((p_t * inv).astype(BF), vals[h][1])
            outs.append(o.astype(BF))
            logs.append((top + jnp.log(total)).reshape(1, -1))
        return jnp.concatenate(outs, axis=1), logs

    for z, (q_ref, o_ref) in enumerate(((q0, o0), (q1, o1))):

        def step(c, carry, z=z, q_ref=q_ref, o_ref=o_ref):
            r = pl.multiple_of(c * chunk, chunk)
            o, logs = one(q_ref[pl.ds(r, chunk), :])
            o_ref[pl.ds(r, chunk), :] = o
            for h in range(2):
                lse_i[0, h, pl.ds(z * per + c, 1), :] = logs[h]
            return carry

        lax.fori_loop(0, per, step, 0)
    o, logs = one(jnp.concatenate([q0[img:, :], q1[img:, :]], axis=0))
    o0[img:, :] = o[:tp]
    o1[img:, :] = o[tp:]
    for h in range(2):
        lse_t[0, h, 0:1, :] = logs[h]


def attend_back_kernel(
    chunk, img, txt, q0, k0, v0, q1, k1, v1, g0, g1, lse_i, lse_t, d0, d1, sums, dk_i, dv_i, dk_t, dv_t
):
    per = img // chunk
    tp = q0.shape[0] - img
    hp = pl.program_id(0)
    pairs = pl.num_programs(0)
    width = 2 * HEAD_DIM
    keys = [head_of((k0, k1), img, h) for h in range(2)]
    vals = [head_of((v0, v1), img, h) for h in range(2)]
    mask = jnp.where(
        pad_key(lax.broadcasted_iota(jnp.int32, (2 * tp, 1), 0), tp, txt), NEG, 0.0
    ).astype(F32)
    dk_i[...] = jnp.zeros_like(dk_i)
    dv_i[...] = jnp.zeros_like(dv_i)
    dk_t[...] = jnp.zeros_like(dk_t)
    dv_t[...] = jnp.zeros_like(dv_t)

    def one(q_pair, g_pair, logs):
        outs = []
        for h in range(2):
            cols = slice(h * HEAD_DIM, (h + 1) * HEAD_DIM)
            q = q_pair[:, cols] * jnp.asarray(SCALE, BF)
            g = g_pair[:, cols]
            p_i = jnp.exp(nt(keys[h][0], q) - logs[h])
            p_t = jnp.exp(nt(keys[h][1], q) + mask - logs[h])
            dp_i = nt(vals[h][0], g)
            dp_t = nt(vals[h][1], g)
            delta = jnp.sum(p_i * dp_i, axis=0, keepdims=True) + jnp.sum(
                p_t * dp_t, axis=0, keepdims=True
            )
            dv_i[h] += nn(p_i.astype(BF), g)
            dv_t[h] += nn(p_t.astype(BF), g)
            ds_i = (p_i * (dp_i - delta)).astype(BF)
            ds_t = (p_t * (dp_t - delta)).astype(BF)
            dk_i[h] += nn(ds_i, q)
            dk_t[h] += nn(ds_t, q)
            dq = tn(ds_i, keys[h][0]) + tn(ds_t, keys[h][1])
            outs.append((dq * SCALE).astype(BF))
        return jnp.concatenate(outs, axis=1)

    def cols_of(kind):
        return pl.ds(pl.multiple_of((kind * pairs + hp) * width, width), width)

    def column_sum(v):
        return jnp.sum(v.astype(F32), axis=0, keepdims=True)

    q_sum = jnp.zeros((1, width), F32)
    for z, (q_ref, g_ref, d_ref) in enumerate(((q0, g0, d0), (q1, g1, d1))):

        def step(c, total, z=z, q_ref=q_ref, g_ref=g_ref, d_ref=d_ref):
            r = pl.multiple_of(c * chunk, chunk)
            logs = [lse_i[0, h, pl.ds(z * per + c, 1), :] for h in range(2)]
            dq = one(q_ref[pl.ds(r, chunk), :], g_ref[pl.ds(r, chunk), :], logs)
            d_ref[pl.ds(r, chunk), cols_of(0)] = dq
            return total + column_sum(dq)

        q_sum = lax.fori_loop(0, per, step, q_sum)
    logs = [lse_t[0, h, 0:1, :] for h in range(2)]
    dq = one(
        jnp.concatenate([q0[img:, :], q1[img:, :]], axis=0),
        jnp.concatenate([g0[img:, :], g1[img:, :]], axis=0),
        logs,
    )
    d0[img:, cols_of(0)] = dq[:tp]
    d1[img:, cols_of(0)] = dq[tp:]
    sums[0, 0:1] = q_sum
    sums[0, 1:2] = column_sum(dq)
    for kind, image, text in ((1, dk_i, dk_t), (2, dv_i, dv_t)):
        both = jnp.concatenate([image[0].astype(BF), image[1].astype(BF)], axis=1)
        d0[:img, cols_of(kind)] = both[:img]
        d1[:img, cols_of(kind)] = both[img:]
        both_t = jnp.concatenate([text[0].astype(BF), text[1].astype(BF)], axis=1)
        d0[img:, cols_of(kind)] = both_t[:tp]
        d1[img:, cols_of(kind)] = both_t[tp:]
        if kind == 2:
            sums[0, 2:3] = column_sum(both)
            sums[0, 3:4] = column_sum(both_t)


def qkv_specs(rows, pairs):
    width = 2 * HEAD_DIM
    return [
        pl.BlockSpec((rows, width), lambda h, kind=kind: (0, kind * pairs + h)) for kind in range(3)
    ] * 2


def lse_specs(n_chunks, chunk, tp):
    return [
        pl.BlockSpec((1, 2, n_chunks, chunk), lambda h: (h, 0, 0, 0)),
        pl.BlockSpec((1, 2, 1, 2 * tp), lambda h: (h, 0, 0, 0)),
    ]


def attention(near, far, img, txt, chunk, slot, rides=(), cid=None):
    rows, columns = near.shape[0], near.shape[1] // 3
    tp, width = rows - img, 2 * HEAD_DIM
    pairs, n_chunks = columns // width, 2 * img // chunk
    tile = pl.BlockSpec((rows, width), lambda h: (0, h))
    return launch(
        functools.partial(attend_kernel, chunk, img, txt),
        (pairs,),
        qkv_specs(rows, pairs),
        [tile, tile] + lse_specs(n_chunks, chunk, tp),
        [jax.ShapeDtypeStruct((rows, columns), BF)] * 2
        + [
            jax.ShapeDtypeStruct((pairs, 2, n_chunks, chunk), F32),
            jax.ShapeDtypeStruct((pairs, 2, 1, 2 * tp), F32),
        ],
        [near, near, near, far, far, far],
        f"attend_{slot}",
        80 * pairs * rows * rows * HEAD_DIM,
        rides=rides,
        cid=cid,
    )


def attention_back(
    near, far, grad_near, grad_far, lse_i, lse_t, img, txt, chunk, slot, rides=(), cid=None
):
    rows, columns = near.shape[0], near.shape[1] // 3
    tp, width = rows - img, 2 * HEAD_DIM
    pairs, n_chunks = columns // width, 2 * img // chunk
    tile = pl.BlockSpec((rows, width), lambda h: (0, h))
    whole = pl.BlockSpec((rows, 3 * columns), lambda h: (0, 0))
    return launch(
        functools.partial(attend_back_kernel, chunk, img, txt),
        (pairs,),
        qkv_specs(rows, pairs) + [tile, tile] + lse_specs(n_chunks, chunk, tp),
        [whole, whole, pl.BlockSpec((1, 4, width), lambda h: (h, 0, 0))],
        [jax.ShapeDtypeStruct((rows, 3 * columns), BF)] * 2
        + [jax.ShapeDtypeStruct((pairs, 4, width), F32)],
        [near, near, near, far, far, far, grad_near, grad_far, lse_i, lse_t],
        f"attend_back_{slot}",
        200 * pairs * rows * rows * HEAD_DIM,
        scratch=[
            pltpu.VMEM((2, 2 * img, HEAD_DIM), F32),
            pltpu.VMEM((2, 2 * img, HEAD_DIM), F32),
            pltpu.VMEM((2, 2 * tp, HEAD_DIM), F32),
            pltpu.VMEM((2, 2 * tp, HEAD_DIM), F32),
        ],
        rides=rides,
        cid=cid,
    )


class Layout:
    def __init__(self, dp_size, tensor_size):
        dp_bits = dp_size.bit_length() - 1
        t_bits = tensor_size.bit_length() - 1
        self.dp = tuple(f"d{i}" for i in range(dp_bits))
        self.tensor = tuple(f"t{i}" for i in range(t_bits))
        self.names = self.dp + self.tensor
        self.compact = dp_size == 8 and tensor_size == 4
        self.p = self.tensor[-1]
        if self.compact:
            self.y, self.x, self.q = self.dp
            self.zh = self.tensor[0]
            self.upper = ()
        else:
            self.q = self.tensor[-2]
            self.upper = self.tensor[:-2]
        self.rest = tuple(n for n in self.names if n not in (self.p, self.q))

    def my_columns(self, v):
        shards = 2 ** len(self.upper)
        part = v.shape[-1] // (4 * shards)
        v = v.reshape(v.shape[:-1] + (shards, 4, part))
        at = index_of((self.q, self.p))
        v = lax.dynamic_index_in_dim(v, at, v.ndim - 2, keepdims=False)
        return v.reshape(v.shape[:-2] + (shards * part,))

    def all_columns(self, v):
        shards = 2 ** len(self.upper)
        g = gather_bits(v[None], (self.p, self.q))
        g = g.reshape((4,) + v.shape[:-1] + (shards, v.shape[-1] // shards))
        g = jnp.moveaxis(g, 0, -2)
        return g.reshape(v.shape[:-1] + (4 * v.shape[-1],))

    def gather_rows(self, own, end=()):
        pair = after(swap(own, self.p), *end)
        return [[own, swap(own, self.q)], [pair, swap(pair, self.q)]]

    def sum_far(self, w, blocks, img, rides=(), cid=None):
        (send, keep), rode = rows_nt([blocks[1][1], blocks[1][0]], w, img, (BF, F32), rides, cid)
        return (keep + swap(send, self.q).astype(F32)).astype(BF), rode

    def sum_near(self, w, blocks, img, rides=(), cid=None):
        (send, keep), rode = rows_nt([blocks[0][1], blocks[0][0]], w, img, (BF, F32), rides, cid)
        return keep + swap(send, self.q).astype(F32), rode

    def gather_weight(self, w):
        w = lax.all_gather(w, self.dp, axis=1, tiled=True)
        if self.upper:
            w = lax.all_gather(w, self.upper, axis=3, tiled=True)
        return jnp.swapaxes(w.reshape(2, 4, w.shape[1] // 4, -1), 0, 1)

    def trade_shards(self, w, end=()):
        w = w.reshape(w.shape[0], w.shape[1], -1)
        joint = (self.q, self.zh)
        same = lax.axis_index(self.zh) == lax.axis_index(self.q)
        cross = lax.ppermute(w, joint, [(1, 2), (2, 1)])
        second = lax.ppermute(w, joint, [(0, 1), (3, 2), (2, 0), (1, 3)])
        cross, second = after((cross, second), *end)
        first = jnp.where(same, w, cross)
        low = lax.axis_index(self.zh) == 0
        return jnp.concatenate(
            [jnp.where(low, first, second), jnp.where(low, second, first)], axis=1
        )

    def spread_near(self, own):
        return [swap(own[0], self.x), swap(own[1], self.y)]

    def spread_rows(self, own, nears):
        x, y = lax.axis_index(self.x), lax.axis_index(self.y)
        whole = jnp.zeros((4,) + own.shape, BF)
        for stream, far_axis in enumerate((self.y, self.x)):
            mine, near = own[stream], nears[stream]
            both, far = swap(near, far_axis), swap(mine, far_axis)
            dx, dy = (near, far) if stream == 0 else (far, near)
            for block, at in (
                (mine, 2 * y + x),
                (dx, 2 * y + 1 - x),
                (dy, 2 * (1 - y) + x),
                (both, 2 * (1 - y) + 1 - x),
            ):
                whole = lax.dynamic_update_slice(whole, block[None, None], (at, stream, 0, 0))
        return whole

    def spread_rows_async(self, own):
        own = own.reshape(own.shape[0], -1, own.shape[-1])
        return lax.all_gather(own, (self.y, self.x), axis=0, tiled=False)

    def trade_ride(self, array, back=False):
        if back:
            array = array.reshape(2, 2, -1, array.shape[-1])
        return TradeRide(array, self.zh, self.q, back)

    def scatter_generic(self, g, kinds):
        g = jnp.swapaxes(g.astype(F32), 0, 1).reshape(2, 4 * g.shape[2], kinds, -1)
        g = lax.psum_scatter(g, self.dp, scatter_dimension=1, tiled=True)
        if self.upper:
            g = lax.psum_scatter(g, self.upper, scatter_dimension=3, tiled=True)
        return g

    def sum_plane_async(self, g):
        return lax.psum_scatter(g, (self.y, self.x), scatter_dimension=0, tiled=False)

    def plane_rides(self, g):
        g = g.reshape((2, 2) + g.shape[1:])
        shape = (2,) + g.shape[3:]

        def along_x(source, target):
            x = 1 - lax.axis_index(self.x)
            return [(source.at[k, x, 0], target.at[k]) for k in range(2)]

        def along_y(source, target):
            y = 1 - lax.axis_index(self.y)
            return [(source.at[y, k, 1], target.at[k]) for k in range(2)]

        return [
            NeighbourRide(g, self.x, shape, along_x, 2),
            NeighbourRide(g, self.y, shape, along_y, 2),
        ]

    def sum_plane(self, g, arrived):
        x, y = lax.axis_index(self.x), lax.axis_index(self.y)
        pick = lambda v, i, dim: lax.dynamic_index_in_dim(v, i, dim, keepdims=False)
        g = g.reshape((2, 2) + g.shape[1:])
        done = []
        for stream in range(2):
            near, dim, far_axis, far = ((x, 1, self.y, y), (y, 0, self.x, x))[stream]
            at = (0, near, stream, 0, 0) if dim == 1 else (near, 0, stream, 0, 0)
            size = (2, 1) if dim == 1 else (1, 2)
            v = lax.dynamic_slice(g, at, size + (1,) + g.shape[3:]).reshape(arrived[stream].shape)
            v = v.astype(F32) + arrived[stream].astype(F32)
            v = pick(v, far, 0) + swap(pick(v, 1 - far, 0).astype(BF), far_axis).astype(F32)
            done.append(v)
        return jnp.stack(done)

    def trade_parts(self, g):
        g = g.reshape(2, 2, -1, g.shape[-1])
        zh = lax.axis_index(self.zh)
        return [lax.dynamic_index_in_dim(g, k, 1, keepdims=False) for k in (zh, 1 - zh)]

    def trade_sends(self, g):
        first, second = self.trade_parts(g)
        joint = (self.q, self.zh)
        return [
            lax.ppermute(first.astype(BF), joint, [(1, 2), (2, 1)]),
            lax.ppermute(second.astype(BF), joint, [(1, 0), (2, 3), (0, 2), (3, 1)]),
        ]

    def trade_adds(self, g, arrived, kinds):
        same = lax.axis_index(self.zh) == lax.axis_index(self.q)
        total = jnp.where(same, self.trade_parts(g)[0].astype(F32), arrived[0].astype(F32))
        total += arrived[1].astype(F32)
        return total.reshape(2, total.shape[1], kinds, -1)


def norm_parts(values):
    average = jnp.mean(values, axis=-1, keepdims=True)
    centred = values - average
    variance = jnp.mean(centred * centred, axis=-1, keepdims=True)
    inverse = lax.rsqrt(variance + 1e-06)
    return centred * inverse, inverse


def norm_back(normed, inverse, grad_in):
    first_mean = jnp.mean(grad_in, axis=-1, keepdims=True)
    cross_mean = jnp.mean(grad_in * normed, axis=-1, keepdims=True)
    return inverse * (grad_in - first_mean - normed * cross_mean)


def body(
    lay,
    image_in,
    text_in,
    condition,
    live_slots,
    ada_weight,
    ada_bias,
    qkv_weight,
    qv_bias,
    proj_weight,
    proj_bias,
    up_weight,
    up_bias,
    down_weight,
    down_bias,
    image_grad,
    text_grad,
):
    width = image_in.shape[1]
    part = qkv_weight.shape[2]
    columns = qkv_weight.shape[3]
    img_rows, txt_rows = image_in.shape[0], text_in.shape[0]
    txt_pad = -(-txt_rows // 16) * 16
    group_slots = condition.shape[0]
    dp_index, t_index = index_of(lay.dp), index_of(lay.tensor)
    t_count = 2 ** len(lay.tensor)
    assert group_slots * 2 == t_count
    my_slot = t_index // 2
    dp_up, t_up = lay.dp[::-1], lay.tensor[::-1]

    rows = img_rows + txt_pad
    is_image = lax.broadcasted_iota(jnp.int32, (rows, 1), 0) < img_rows

    def pack(image, text):
        return jnp.concatenate([image, jnp.pad(text, ((0, txt_pad - txt_rows), (0, 0)))], axis=0)

    def spread(per_stream):
        return jnp.where(is_image, per_stream[0], per_stream[1])

    def total(v):
        return jnp.stack([jnp.sum(v[:img_rows], axis=0), jnp.sum(v[img_rows:], axis=0)])

    def flat(blocks):
        return blocks[0] + blocks[1]

    def unflat(v):
        return [list(v[:2]), list(v[2:4])]

    qkv_local = jnp.swapaxes(qkv_weight, 1, 2)
    proj_local = jnp.swapaxes(proj_weight, 1, 2)[:, :, None]
    up_local = up_weight[:, :, None]
    down_local = jnp.swapaxes(down_weight, 1, 2)[:, :, None]
    compact = lay.compact
    if compact:
        qkv_own = lay.trade_shards(qkv_local)
        qkv_near = lay.spread_near(qkv_own)
    else:
        qkv_full, up_full, proj_full, down_full = [
            lay.gather_weight(w) for w in (qkv_local, up_local, proj_local, down_local)
        ]

    cond_all = gather_bits(condition, dp_up).astype(F32)
    silu_all = jax.nn.silu(cond_all).astype(BF)
    silu_mine = lax.dynamic_slice_in_dim(silu_all, dp_index * part, part, 1)
    mod = jnp.einsum("sd,tdkc->stkc", silu_mine, ada_weight, preferred_element_type=F32)
    mod = scatter_bits(mod, lay.dp)
    if compact:
        mod = after(mod, qkv_own)
    mod = gather_bits(mod[None], t_up)
    mod = lax.dynamic_index_in_dim(mod, my_slot, 1, keepdims=False)
    mod = jnp.moveaxis(mod, 0, 2).reshape(2, 6, width) + ada_bias.astype(F32)
    live = lax.dynamic_index_in_dim(live_slots, my_slot, 0, keepdims=False).astype(F32)

    mods = [spread(mod[:, k]) for k in range(6)]
    shift_one, scale_one, gate_one, shift_two, scale_two, gate_two = mods

    inputs = pack(image_in, text_in).astype(F32)
    grad_out = live * pack(image_grad, text_grad).astype(F32)
    grad_two = (gate_two * grad_out).astype(BF)

    first_norm = norm_parts(inputs)
    first_hidden = (first_norm[0] * (1.0 + scale_one) + shift_one).astype(BF)
    if compact:
        first_hidden = after(first_hidden, qkv_near)
    first = lay.gather_rows(first_hidden)
    if compact:
        qkv_full = lay.spread_rows(qkv_own, qkv_near)
    qv = lay.my_columns(qv_bias.astype(F32))
    qkv_bias = jnp.concatenate([qv[:, 0], jnp.zeros_like(qv[:, 0]), qv[:, 1]], axis=1)
    heads_n = qv.shape[2]
    img = img_rows

    def ride(array, start, stop):
        return row_ride(array, lay.p, start, stop)

    cut = rows // 3 // 16 * 16
    extra = [[], [], []]
    if compact:
        extra = [
            [lay.trade_ride(w.reshape(w.shape[0], part, -1))]
            for w in (proj_local, up_local[:1], up_local[1:])
        ]
    qkv, rode = rows_nn(
        flat(first), qkv_full, img, "bias", bias=qkv_bias, rides=extra[0], cid=1
    )
    qkv = unflat(qkv)
    chunk = min(256, img_rows)
    if compact:
        proj_full = lay.spread_rows_async(rode[0])
    other, rode = attention(
        qkv[0][1], qkv[1][1], img, txt_rows, chunk, 1, rides=extra[1], cid=2
    )
    if compact:
        up_full = [lay.spread_rows_async(rode[0])]
        qkv, other = after((qkv, other), proj_full)
    mine, rode = attention(
        qkv[0][0],
        qkv[1][0],
        img,
        txt_rows,
        chunk,
        0,
        rides=[ride(grad_two, 0, cut)] + extra[2],
        cid=10,
    )
    grad_two_pair = rode[:1]
    heads_out = [[mine[z], other[z]] for z in range(2)]
    if compact:
        up_full.append(lay.spread_rows_async(rode[1]))
        down_own = lay.trade_shards(after(down_local, mine))

    far = swap(lay.sum_far(proj_full, heads_out, img)[0], lay.p)
    near, unused = lay.sum_near(proj_full, heads_out, img)
    branch_one = near + far.astype(F32) + spread(proj_bias.astype(F32))
    middle = inputs + gate_one * branch_one
    second_norm = norm_parts(middle)
    second_hidden = (second_norm[0] * (1.0 + scale_two) + shift_two).astype(BF)
    if compact:
        second_hidden, down_own = tie(second_hidden, down_own)
        down_full = lay.spread_rows_async(down_own)
    second = lay.gather_rows(second_hidden)
    up_mine = lay.my_columns(up_bias.astype(F32))
    up_n = up_mine.shape[1]
    up_out, rode = rows_nn(
        flat(second), up_full, img, "gelu", bias=up_mine, rides=[ride(grad_two, cut, rows)], cid=13
    )
    grad_two_pair = jnp.concatenate(grad_two_pair + rode, axis=0)
    grad_two_blocks = [
        [grad_two, swap(grad_two, lay.q)], [grad_two_pair, swap(grad_two_pair, lay.q)]
    ]
    activated, slopes = up_out[:4], up_out[4:]
    grad_two_flat = flat(grad_two_blocks)
    back_out, unused = rows_nn(grad_two_flat, down_full, img, "slope", slopes=slopes)
    grad_inner, up_part = back_out[:4], back_out[4].reshape(2, up_n)
    far_two, unused = lay.sum_far(up_full, unflat(grad_inner), img)
    cut = rows * 15 // 37 // 16 * 16
    near_two, rode = lay.sum_near(up_full, unflat(grad_inner), img, [ride(far_two, 0, cut)], 5)
    down_grads, rode_two = weight_grad(
        after(grad_two_flat, near_two), activated, img, rides=[ride(far_two, cut, rows)], cid=4
    )
    if compact:
        down_plane = lay.sum_plane_async(down_grads)
    grad_hidden_two = near_two + jnp.concatenate(rode + rode_two, axis=0).astype(F32)
    grad_middle = grad_out + norm_back(
        second_norm[0], second_norm[1], grad_hidden_two * (1.0 + scale_two)
    )
    grad_one = (gate_one * grad_middle).astype(BF)
    cut, cut_two = rows * 17 // 37 // 16 * 16, rows * 27 // 37 // 16 * 16
    up_grads, rode = weight_grad(
        after(flat(second), grad_one), grad_inner, img, rides=[ride(grad_one, 0, cut)], cid=6
    )
    if compact:
        up_plane = lay.sum_plane_async(up_grads)
    near, rode_two = lay.sum_near(
        down_full, after(unflat(activated), up_grads), img, [ride(grad_one, cut, cut_two)], 7
    )
    deps = (near, down_plane) if compact else (near,)
    far, rode_three = lay.sum_far(
        down_full, after(unflat(activated), *deps), img, [ride(grad_one, cut_two, rows)], 3
    )
    grad_one_pair = jnp.concatenate(rode + rode_two + rode_three, axis=0)
    grad_one_blocks = [
        [grad_one, swap(grad_one, lay.q)], [grad_one_pair, swap(grad_one_pair, lay.q)]
    ]
    grad_heads = unflat(rows_nn(flat(grad_one_blocks), proj_full, img, "plain")[0])

    def back(c, saved, heads, rides, cid):
        return attention_back(
            qkv[0][c],
            qkv[1][c],
            heads[0][c],
            heads[1][c],
            saved[2],
            saved[3],
            img,
            txt_rows,
            chunk,
            c,
            rides,
            cid,
        )

    half = rows // 32 * 16
    rides, rides_two = [ride(far, 0, half)], [ride(far, half, rows)]
    if compact:
        rides.append(lay.trade_ride(down_plane, True))
        rides_two.append(lay.trade_ride(up_plane, True))
    grad_other, down_sums = back(1, other, grad_heads, rides, 11)
    proj_grads, unused = weight_grad(
        after(flat(grad_one_blocks), grad_other), flat(heads_out), img
    )
    if compact:
        proj_plane = lay.sum_plane_async(proj_grads)
    grad_mine, up_sums = back(
        0,
        mine,
        after(grad_heads, proj_grads),
        rides_two,
        12,
    )
    far = jnp.concatenate(down_sums[:1] + up_sums[:1], axis=0)
    branch_two = near + far.astype(F32) + spread(down_bias.astype(F32))
    outputs = (live * (middle + gate_two * branch_two)).astype(BF)
    grad_qkv = [[grad_mine[z], grad_other[z]] for z in range(2)]
    far, unused = lay.sum_far(qkv_full, grad_qkv, img)
    cut = rows * 16 // 37 // 16 * 16
    rides = [ride(far, 0, cut)]
    if compact:
        rides.append(lay.trade_ride(proj_plane, True))
    qkv_grads, rode = weight_grad(flat(first), flat(grad_qkv), img, rides=rides, cid=8)
    rides = [ride(far, cut, rows)]
    if compact:
        proj_sums = rode[1]
        rides += lay.plane_rides(qkv_grads)
    near, rode_two = lay.sum_near(qkv_full, after(grad_qkv, qkv_grads), img, rides, 9)
    far = jnp.concatenate(rode[:1] + rode_two[:1], axis=0)
    if compact:
        down_grad, up_grad, proj_grad = [
            (v[0].astype(F32) + v[1].astype(F32))[:, :, None]
            for v in (down_sums[1], up_sums[1], proj_sums)
        ]
        qkv_plane = lay.sum_plane(qkv_grads, rode_two[1:3])
    else:
        down_grad, up_grad, proj_grad = [
            lay.scatter_generic(g, 1) for g in (down_grads, up_grads, proj_grads)
        ]
        qkv_grad = lay.scatter_generic(qkv_grads, 3)
    grad_hidden_one = near + far.astype(F32)
    input_grads = grad_middle + norm_back(
        first_norm[0], first_norm[1], grad_hidden_one * (1.0 + scale_one)
    )

    grad_mod = jnp.stack(
        [
            total(grad_hidden_one),
            total(grad_hidden_one * first_norm[0]),
            total(branch_one * grad_middle),
            total(grad_hidden_two),
            total(grad_hidden_two * second_norm[0]),
            total(branch_two * grad_out),
        ],
        axis=1,
    )
    grad_mod = sum_bits(grad_mod, (lay.p,))
    grad_mod = gather_bits(grad_mod[None], t_up[1:])
    if compact:
        qkv_plane, grad_mod = tie(qkv_plane, grad_mod)
    grad_mod = lax.dynamic_slice_in_dim(grad_mod, t_index * columns, columns, 3)
    grad_mod = gather_bits(grad_mod, dp_up)
    high = lax.Precision.HIGHEST
    ada_grad = jnp.einsum("sd,stkc->tdkc", silu_mine.astype(F32), grad_mod, precision=high)
    cond_terms = jnp.einsum("stkc,tdkc->sd", grad_mod, ada_weight.astype(F32), precision=high)
    cond_terms = gather_bits(cond_terms[None], dp_up)
    cond_terms = lax.dynamic_slice_in_dim(cond_terms, dp_index * group_slots, group_slots, 1)
    cond_terms = jnp.swapaxes(cond_terms, 0, 1).reshape(group_slots, width)
    if compact:
        arrived = lay.trade_sends(qkv_plane)
        cond_terms, arrived = tie(cond_terms, arrived)
        qkv_grad = lay.trade_adds(qkv_plane, arrived, 3)
    down_grad = jnp.swapaxes(down_grad[:, :, 0], 1, 2)
    proj_grad = jnp.swapaxes(proj_grad[:, :, 0], 1, 2)
    up_grad = up_grad[:, :, 0]
    qkv_grad = jnp.swapaxes(qkv_grad, 1, 2)
    cond_terms = sum_bits(cond_terms, t_up)
    cond_terms = lax.dynamic_slice_in_dim(cond_terms, t_index * columns, columns, 1)
    cond_slice = lax.dynamic_slice_in_dim(condition.astype(F32), t_index * columns, columns, 1)
    unused, silu_pull = jax.vjp(jax.nn.silu, cond_slice)
    condition_grad = silu_pull(cond_terms)[0]
    ada_bias_grad = gather_bits(jnp.sum(grad_mod, axis=0)[None], t_up)
    ada_bias_grad = jnp.moveaxis(ada_bias_grad, 0, 2).reshape(2, 6, width)

    own_part = sum_bits(
        jnp.stack([total(grad_one.astype(F32)), total(grad_two.astype(F32))]), (lay.p, lay.q)
    )
    sums = grad_mine[2] + grad_other[2]
    pairs = sums.shape[0]
    qv_part = jnp.transpose(sums.reshape(pairs, 2, 2, -1), (2, 1, 0, 3)).reshape(2, 2, heads_n)
    if compact:
        qv_part = after(qv_part, near)
    packed = jnp.concatenate([qv_part.reshape(-1), up_part.reshape(-1), own_part.reshape(-1)])
    packed = sum_bits(packed.reshape(-1, 128), lay.rest).reshape(-1)
    cut_one, cut_two = qv_part.size, qv_part.size + up_part.size
    qv_bias_grad = lay.all_columns(packed[:cut_one].reshape(qv_part.shape))
    up_bias_grad = lay.all_columns(packed[cut_one:cut_two].reshape(up_part.shape))
    own_part = packed[cut_two:].reshape(own_part.shape)
    return (
        outputs[:img_rows],
        outputs[img_rows : img_rows + txt_rows],
        input_grads[:img_rows],
        input_grads[img_rows : img_rows + txt_rows],
        condition_grad,
        ada_grad,
        ada_bias_grad,
        qkv_grad,
        qv_bias_grad,
        proj_grad,
        own_part[0],
        up_grad,
        up_bias_grad,
        down_grad,
        own_part[1],
    )


def solution(mesh):
    lay = Layout(mesh.shape["dp"], mesh.shape["tensor"])
    bits = Mesh(mesh.devices.reshape((2,) * len(lay.names)), lay.names)
    dp, tensor, every = lay.dp, lay.tensor, lay.names
    in_specs = (
        P(every, None),
        P(every, None),
        P(dp, None),
        P(dp),
        P(None, dp, None, tensor),
        P(),
        P(None, None, dp, tensor),
        P(),
        P(None, tensor, dp),
        P(),
        P(None, dp, tensor),
        P(),
        P(None, tensor, dp),
        P(),
        P(every, None),
        P(every, None),
    )
    out_specs = (
        P(every, None),
        P(every, None),
        P(every, None),
        P(every, None),
        P(dp, tensor),
        P(None, dp, None, tensor),
        P(),
        P(None, None, dp, tensor),
        P(),
        P(None, tensor, dp),
        P(),
        P(None, dp, tensor),
        P(),
        P(None, tensor, dp),
        P(),
    )
    return jax.shard_map(
        functools.partial(body, lay), mesh=bits, in_specs=in_specs, out_specs=out_specs, check_vma=False
    )
```

```python
import functools

import jax
import jax.numpy as jnp
from jax import lax
from jax.experimental import pallas as pl
from jax.experimental.pallas import tpu as pltpu
from jax.sharding import Mesh
from jax.sharding import PartitionSpec as P

HEAD_DIM = 64
SCALE = HEAD_DIM ** (-0.5)
BF = jnp.bfloat16
F32 = jnp.float32
NEG = -1e30


def swap(v, axis):
    return lax.ppermute(v, axis, [(0, 1), (1, 0)])


def gather_bits(v, axes):
    for axis in axes:
        other = swap(v, axis)
        first = lax.axis_index(axis) == 0
        v = jnp.concatenate([jnp.where(first, v, other), jnp.where(first, other, v)], 0)
    return v


def scatter_bits(v, axes):
    for axis in axes:
        first = lax.axis_index(axis) == 0
        half = v.shape[0] // 2
        low, high = v[:half], v[half:]
        v = jnp.where(first, low, high) + swap(jnp.where(first, high, low), axis)
    return v


def sum_bits(v, axes):
    for axis in axes:
        v = v + swap(v, axis)
    return v


def after(v, *deps):
    return lax.optimization_barrier((v,) + deps)[0]


def tie(*vs):
    return lax.optimization_barrier(vs)


def index_of(axes):
    out = 0
    for axis in axes:
        out = out * 2 + lax.axis_index(axis)
    return out


def nt(a, b):
    return lax.dot_general(a, b, (((1,), (1,)), ((), ())), preferred_element_type=F32)


def nn(a, b):
    return lax.dot_general(a, b, (((1,), (0,)), ((), ())), preferred_element_type=F32)


def tn(a, b):
    return lax.dot_general(a, b, (((0,), (0,)), ((), ())), preferred_element_type=F32)


VMEM_LIMIT = 52 * 2**20
GELU_C = 0.7978845608028654


def launch(kernel, grid, in_specs, out_specs, out_shape, args, name, flops, scratch=(), rides=(), cid=None):
    n_in, n_out = len(args), len(out_shape)
    params = dict(vmem_limit_bytes=VMEM_LIMIT)
    cost = pl.CostEstimate(flops=flops, bytes_accessed=flops // 512, transcendentals=0)
    if not rides:
        outs = pl.pallas_call(
            kernel,
            grid=grid,
            in_specs=in_specs,
            out_specs=out_specs,
            out_shape=out_shape,
            scratch_shapes=list(scratch),
            compiler_params=pltpu.CompilerParams(**params),
            cost_estimate=cost,
            name=name,
        )(*args)
        return list(outs), []
    partners = sorted({partner for ride in rides for partner in ride.partners})
    n_rides, sems = len(rides), sum(ride.sems for ride in rides)

    def body(*refs):
        ins, rest = refs[:n_in], refs[n_in:]
        sources, rest = rest[:n_rides], rest[n_rides:]
        outs, rest = rest[:n_out], rest[n_out:]
        targets, rest = rest[:n_rides], rest[n_rides:]
        own, (send, recv) = rest[:-2], rest[-2:]
        steps, at = [], 0
        for source, target, ride in zip(sources, targets, rides):
            steps.append(ride.moves(source, target, lambda k, at=at: send.at[at + k], lambda k, at=at: recv.at[at + k]))
            at += ride.sems

        barrier = pltpu.get_barrier_semaphore()
        for partner in partners:
            pl.semaphore_signal(
                barrier,
                1,
                device_id={axis: 1 - lax.axis_index(axis) for axis in partner},
                device_id_type=pl.DeviceIdType.MESH,
            )
        pl.semaphore_wait(barrier, len(partners))
        for start, unused in steps:
            start()
        pltpu.emit_pipeline(
            lambda *blocks: kernel(*blocks, *own),
            grid=grid,
            in_specs=list(in_specs),
            out_specs=list(out_specs),
        )(*ins, *outs)
        for unused, wait in steps:
            wait()

    anywhere = pl.BlockSpec(memory_space=pl.ANY)
    outs = pl.pallas_call(
        body,
        in_specs=[anywhere] * (n_in + n_rides),
        out_specs=[anywhere] * (n_out + n_rides),
        out_shape=list(out_shape) + [ride.shape for ride in rides],
        scratch_shapes=list(scratch)
        + [pltpu.SemaphoreType.DMA((sems,)), pltpu.SemaphoreType.DMA((sems,))],
        compiler_params=pltpu.CompilerParams(collective_id=cid, has_side_effects=True, **params),
        cost_estimate=cost,
        name=f"{name}_{cid}",
    )(*args, *[ride.array for ride in rides])
    return list(outs[:n_out]), list(outs[n_out:])


class NeighbourRide:
    def __init__(self, array, axis, shape, views, sems):
        self.array, self.axis, self.views, self.sems = array, axis, views, sems
        self.shape = jax.ShapeDtypeStruct(shape, array.dtype)
        self.partners = [(axis,)]

    def moves(self, source, target, send, recv):
        other = {self.axis: 1 - lax.axis_index(self.axis)}
        made = [
            pltpu.make_async_remote_copy(
                src_ref=src,
                dst_ref=dst,
                send_sem=send(k),
                recv_sem=recv(k),
                device_id=other,
                device_id_type=pl.DeviceIdType.MESH,
            )
            for k, (src, dst) in enumerate(self.views(source, target))
        ]

        def start():
            for move in made:
                move.start()

        def wait():
            for move in made:
                move.wait()

        return start, wait


def row_ride(array, axis, start, stop):
    count = min(4, (stop - start) // 16)
    cuts = [start + (stop - start) // 16 * k // count * 16 for k in range(count)] + [stop]

    def views(source, target):
        return [
            (source.at[pl.ds(a, b - a)], target.at[pl.ds(a - start, b - a)])
            for a, b in zip(cuts, cuts[1:])
        ]

    return NeighbourRide(array, axis, (stop - start,) + array.shape[1:], views, count)


class TradeRide:
    sems = 3

    def __init__(self, array, zh, q, back):
        self.array, self.zh, self.q, self.back = array, zh, q, back
        streams, part, n = array.shape[0], array.shape[-2], array.shape[-1]
        shape = (2, streams, part, n) if back else (streams, 2, part, n)
        self.shape = jax.ShapeDtypeStruct(shape, array.dtype)
        self.partners = [(q,), (zh,), (q, zh)]

    def moves(self, source, target, send, recv):
        zh, q = lax.axis_index(self.zh), lax.axis_index(self.q)
        same = zh == q

        def remote(k, src, dst, at, to_zh, to_q):
            return pltpu.make_async_remote_copy(
                src_ref=src,
                dst_ref=dst,
                send_sem=send(k),
                recv_sem=recv(at),
                device_id={self.zh: to_zh, self.q: to_q},
                device_id_type=pl.DeviceIdType.MESH,
            )

        if self.back:
            outgoing = [remote(j, source.at[:, j], target.at[zh], zh, q, j) for j in range(2)]
            arriving = [remote(j, source.at[:, j], target.at[j], j, q, j) for j in range(2)]
            local = pltpu.make_async_copy(source.at[:, q], target.at[zh], send(2))
            mine = [jnp.logical_and(same, q == j) for j in range(2)]
        else:
            outgoing = [remote(j, source, target.at[:, q], q, j, zh) for j in range(2)]
            arriving = [remote(j, source, target.at[:, j], j, j, zh) for j in range(2)]
            local = pltpu.make_async_copy(source, target.at[:, q], send(2))
            mine = [jnp.logical_and(same, zh == j) for j in range(2)]

        def start():
            for move, own in zip(outgoing, mine):
                pl.when(jnp.logical_not(own))(move.start)
            pl.when(same)(local.start)

        def wait():
            for move, own in zip(outgoing, mine):
                pl.when(jnp.logical_not(own))(move.wait_send)
            for move, own in zip(arriving, mine):
                pl.when(jnp.logical_not(own))(move.wait_recv)
            pl.when(same)(local.wait)

        return start, wait


def once(shape, index):
    return pl.BlockSpec(shape, index, pipeline_mode=pl.Buffered(1))


def by_stream(w):
    return [(w[0], 0), (w[1], 0)] if isinstance(w, (list, tuple)) else [(w, 0), (w, 1)]


def rows_nn_kernel(nb, img, mode, *refs):
    xs, w0, w1 = refs[:nb], refs[nb], refs[nb + 1]
    rest = refs[nb + 2 :]
    depth, tile = xs[0].shape[1], w0.shape[3]
    text = xs[0].shape[0] - img
    y_text = nn(
        jnp.concatenate([x[img:, :] for x in xs], axis=0), w1[:, 0].reshape(depth, tile)
    )
    w_img = w0[:, 0].reshape(depth, tile)
    if mode == "slope":
        sums = rest[2 * nb]
        total = [jnp.zeros((1, tile), F32), jnp.zeros((1, tile), F32)]
    for b in range(nb):
        for stream, rows in ((0, slice(0, img)), (1, slice(img, img + text))):
            y = nn(xs[b][rows, :], w_img) if stream == 0 else y_text[b * text : (b + 1) * text]
            if mode == "plain":
                rest[b][rows, :] = y.astype(BF)
            elif mode == "bias":
                rest[1 + b][rows, :] = (y + rest[0][stream]).astype(BF)
            elif mode == "gelu":
                v = y + rest[0][stream]
                inner = jnp.tanh(GELU_C * (v + 0.044715 * (v * v * v)))
                half = 0.5 * (1.0 + inner)
                rest[1 + b][rows, :] = (v * half).astype(BF)
                rest[1 + nb + b][rows, :] = half + 0.5 * v * (1.0 - inner * inner) * (
                    GELU_C * (1.0 + 3 * 0.044715 * (v * v))
                )
            else:
                y = (y * rest[b][rows, :]).astype(BF)
                rest[nb + b][rows, :] = y
                total[stream] += jnp.sum(y.astype(F32), axis=0, keepdims=True)
    if mode == "slope":
        sums[0] = total[0]
        sums[1] = total[1]


def rows_nn(xs, w, img, mode, bias=None, slopes=(), rides=(), cid=None):
    (w0, s0), (w1, s1) = by_stream(w)
    n = w0.shape[3]
    tile = 768 if n % 768 == 0 else 384
    nb, (rows, depth) = len(xs), xs[0].shape
    in_specs = [once((rows, depth), lambda j: (0, 0))] * nb
    in_specs += [
        pl.BlockSpec((4, 1, depth // 4, tile), lambda j, at=at: (0, at, 0, j)) for at in (s0, s1)
    ]
    args = list(xs) + [w0, w1]
    out_tile = pl.BlockSpec((rows, tile), lambda j: (0, j))
    vector = pl.BlockSpec((2, 1, tile), lambda j: (0, 0, j))
    shape = lambda dtype: jax.ShapeDtypeStruct((rows, n), dtype)
    if bias is not None:
        in_specs.append(vector)
        args.append(bias.reshape(2, 1, n))
    in_specs += [out_tile] * len(slopes)
    args += list(slopes)
    out_specs, out_shape = [out_tile] * nb, [shape(BF)] * nb
    if mode == "gelu":
        out_specs, out_shape = out_specs + [out_tile] * nb, out_shape + [shape(F32)] * nb
    if mode == "slope":
        out_specs.append(vector)
        out_shape.append(jax.ShapeDtypeStruct((2, 1, n), F32))
    return launch(
        functools.partial(rows_nn_kernel, nb, img, mode),
        (n // tile,),
        in_specs,
        out_specs,
        out_shape,
        args,
        f"rows_{mode}",
        2 * nb * rows * depth * n,
        rides=rides,
        cid=cid,
    )


def rows_nt_kernel(nb, img, *refs):
    xs, w0, w1, outs = refs[:nb], refs[nb], refs[nb + 1], refs[nb + 2 :]
    text = xs[0].shape[0] - img
    y_text = nt(jnp.concatenate([x[img:, :] for x in xs], axis=0), w1[:, 0].reshape(-1, xs[0].shape[1]))
    w_img = w0[:, 0].reshape(-1, xs[0].shape[1])
    for b in range(nb):
        outs[b][:img, :] = nt(xs[b][:img, :], w_img).astype(outs[b].dtype)
        outs[b][img:, :] = y_text[b * text : (b + 1) * text].astype(outs[b].dtype)


def rows_nt(xs, w, img, dtypes, rides=(), cid=None):
    nb, (rows, n) = len(xs), xs[0].shape
    (w0, s0), (w1, s1) = by_stream(w)
    quarter = w0.shape[2]
    return launch(
        functools.partial(rows_nt_kernel, nb, img),
        (2,),
        [once((rows, n), lambda j: (0, 0))] * nb
        + [
            pl.BlockSpec((2, 1, quarter, n), lambda j, at=at: (j, at, 0, 0)) for at in (s0, s1)
        ],
        [pl.BlockSpec((rows, 2 * quarter), lambda j: (0, j))] * nb,
        [jax.ShapeDtypeStruct((rows, 4 * quarter), t) for t in dtypes],
        list(xs) + [w0, w1],
        "rows_back",
        8 * nb * rows * quarter * n,
        rides=rides,
        cid=cid,
    )


def weight_grad_kernel(nb, img, *refs):
    xs, ys, out = refs[:nb], refs[nb : 2 * nb], refs[2 * nb]
    y_img, y_text = refs[2 * nb + 1 :]
    text = xs[0].shape[0] - img

    @pl.when(pl.program_id(0) == 0)
    def _():
        for b in range(nb):
            y_img[b * img : (b + 1) * img, :] = ys[b][:img, :]
            y_text[b * text : (b + 1) * text, :] = ys[b][img:, :]

    x_img = jnp.concatenate([x[:img, :] for x in xs], axis=0)
    x_text = jnp.concatenate([x[img:, :] for x in xs], axis=0)
    out[0, 0] = tn(x_img, y_img[...]).astype(BF)
    out[0, 1] = tn(x_text, y_text[...]).astype(BF)


def weight_grad(xs, ys, img, rides=(), cid=None):
    nb, (rows, d), n = len(xs), xs[0].shape, ys[0].shape[1]
    (out,), rode = launch(
        functools.partial(weight_grad_kernel, nb, img),
        (4,),
        [pl.BlockSpec((rows, d // 4), lambda j: (0, j))] * nb
        + [once((rows, n), lambda j: (0, 0))] * nb,
        [pl.BlockSpec((1, 2, d // 4, n), lambda j: (j, 0, 0, 0))],
        [jax.ShapeDtypeStruct((4, 2, d // 4, n), BF)],
        list(xs) + list(ys),
        "weight_grad",
        2 * nb * rows * d * n,
        scratch=[pltpu.VMEM((nb * img, n), BF), pltpu.VMEM((nb * (rows - img), n), BF)],
        rides=rides,
        cid=cid,
    )
    return out, rode


def pad_key(position, padded, real):
    return lax.rem(position, padded) >= real


def head_of(refs, img, h):
    cols = slice(h * HEAD_DIM, (h + 1) * HEAD_DIM)
    whole = [r[...] for r in refs]
    return (
        jnp.concatenate([w[:img, cols] for w in whole], axis=0),
        jnp.concatenate([w[img:, cols] for w in whole], axis=0),
    )


def attend_kernel(chunk, img, txt, q0, k0, v0, q1, k1, v1, o0, o1, lse_i, lse_t):
    per = img // chunk
    tp = q0.shape[0] - img
    keys = [head_of((k0, k1), img, h) for h in range(2)]
    vals = [head_of((v0, v1), img, h) for h in range(2)]
    mask = jnp.where(
        pad_key(lax.broadcasted_iota(jnp.int32, (1, 2 * tp), 1), tp, txt), NEG, 0.0
    ).astype(F32)

    def one(q_pair):
        outs, logs = [], []
        for h in range(2):
            q = q_pair[:, h * HEAD_DIM : (h + 1) * HEAD_DIM] * jnp.asarray(SCALE, BF)
            s_i = nt(q, keys[h][0])
            s_t = nt(q, keys[h][1]) + mask
            top = jnp.maximum(
                jnp.max(s_i, axis=1, keepdims=True), jnp.max(s_t, axis=1, keepdims=True)
            )
            p_i = jnp.exp(s_i - top)
            p_t = jnp.exp(s_t - top)
            total = jnp.sum(p_i, axis=1, keepdims=True) + jnp.sum(p_t, axis=1, keepdims=True)
            inv = 1.0 / total
            o = nn((p_i * inv).astype(BF), vals[h][0]) + nn((p_t * inv).astype(BF), vals[h][1])
            outs.append(o.astype(BF))
            logs.append((top + jnp.log(total)).reshape(1, -1))
        return jnp.concatenate(outs, axis=1), logs

    for z, (q_ref, o_ref) in enumerate(((q0, o0), (q1, o1))):

        def step(c, carry, z=z, q_ref=q_ref, o_ref=o_ref):
            r = pl.multiple_of(c * chunk, chunk)
            o, logs = one(q_ref[pl.ds(r, chunk), :])
            o_ref[pl.ds(r, chunk), :] = o
            for h in range(2):
                lse_i[0, h, pl.ds(z * per + c, 1), :] = logs[h]
            return carry

        lax.fori_loop(0, per, step, 0)
    o, logs = one(jnp.concatenate([q0[img:, :], q1[img:, :]], axis=0))
    o0[img:, :] = o[:tp]
    o1[img:, :] = o[tp:]
    for h in range(2):
        lse_t[0, h, 0:1, :] = logs[h]


def attend_back_kernel(
    chunk, img, txt, q0, k0, v0, q1, k1, v1, g0, g1, lse_i, lse_t, d0, d1, sums, dk_i, dv_i, dk_t, dv_t
):
    per = img // chunk
    tp = q0.shape[0] - img
    hp = pl.program_id(0)
    pairs = pl.num_programs(0)
    width = 2 * HEAD_DIM
    keys = [head_of((k0, k1), img, h) for h in range(2)]
    vals = [head_of((v0, v1), img, h) for h in range(2)]
    mask = jnp.where(
        pad_key(lax.broadcasted_iota(jnp.int32, (2 * tp, 1), 0), tp, txt), NEG, 0.0
    ).astype(F32)
    dk_i[...] = jnp.zeros_like(dk_i)
    dv_i[...] = jnp.zeros_like(dv_i)
    dk_t[...] = jnp.zeros_like(dk_t)
    dv_t[...] = jnp.zeros_like(dv_t)

    def one(q_pair, g_pair, logs):
        outs = []
        for h in range(2):
            cols = slice(h * HEAD_DIM, (h + 1) * HEAD_DIM)
            q = q_pair[:, cols] * jnp.asarray(SCALE, BF)
            g = g_pair[:, cols]
            p_i = jnp.exp(nt(keys[h][0], q) - logs[h])
            p_t = jnp.exp(nt(keys[h][1], q) + mask - logs[h])
            dp_i = nt(vals[h][0], g)
            dp_t = nt(vals[h][1], g)
            delta = jnp.sum(p_i * dp_i, axis=0, keepdims=True) + jnp.sum(
                p_t * dp_t, axis=0, keepdims=True
            )
            dv_i[h] += nn(p_i.astype(BF), g)
            dv_t[h] += nn(p_t.astype(BF), g)
            ds_i = (p_i * (dp_i - delta)).astype(BF)
            ds_t = (p_t * (dp_t - delta)).astype(BF)
            dk_i[h] += nn(ds_i, q)
            dk_t[h] += nn(ds_t, q)
            dq = tn(ds_i, keys[h][0]) + tn(ds_t, keys[h][1])
            outs.append((dq * SCALE).astype(BF))
        return jnp.concatenate(outs, axis=1)

    def cols_of(kind):
        return pl.ds(pl.multiple_of((kind * pairs + hp) * width, width), width)

    def column_sum(v):
        return jnp.sum(v.astype(F32), axis=0, keepdims=True)

    q_sum = jnp.zeros((1, width), F32)
    for z, (q_ref, g_ref, d_ref) in enumerate(((q0, g0, d0), (q1, g1, d1))):

        def step(c, total, z=z, q_ref=q_ref, g_ref=g_ref, d_ref=d_ref):
            r = pl.multiple_of(c * chunk, chunk)
            logs = [lse_i[0, h, pl.ds(z * per + c, 1), :] for h in range(2)]
            dq = one(q_ref[pl.ds(r, chunk), :], g_ref[pl.ds(r, chunk), :], logs)
            d_ref[pl.ds(r, chunk), cols_of(0)] = dq
            return total + column_sum(dq)

        q_sum = lax.fori_loop(0, per, step, q_sum)
    logs = [lse_t[0, h, 0:1, :] for h in range(2)]
    dq = one(
        jnp.concatenate([q0[img:, :], q1[img:, :]], axis=0),
        jnp.concatenate([g0[img:, :], g1[img:, :]], axis=0),
        logs,
    )
    d0[img:, cols_of(0)] = dq[:tp]
    d1[img:, cols_of(0)] = dq[tp:]
    sums[0, 0:1] = q_sum
    sums[0, 1:2] = column_sum(dq)
    for kind, image, text in ((1, dk_i, dk_t), (2, dv_i, dv_t)):
        both = jnp.concatenate([image[0].astype(BF), image[1].astype(BF)], axis=1)
        d0[:img, cols_of(kind)] = both[:img]
        d1[:img, cols_of(kind)] = both[img:]
        both_t = jnp.concatenate([text[0].astype(BF), text[1].astype(BF)], axis=1)
        d0[img:, cols_of(kind)] = both_t[:tp]
        d1[img:, cols_of(kind)] = both_t[tp:]
        if kind == 2:
            sums[0, 2:3] = column_sum(both)
            sums[0, 3:4] = column_sum(both_t)


def qkv_specs(rows, pairs):
    width = 2 * HEAD_DIM
    return [
        pl.BlockSpec((rows, width), lambda h, kind=kind: (0, kind * pairs + h)) for kind in range(3)
    ] * 2


def lse_specs(n_chunks, chunk, tp):
    return [
        pl.BlockSpec((1, 2, n_chunks, chunk), lambda h: (h, 0, 0, 0)),
        pl.BlockSpec((1, 2, 1, 2 * tp), lambda h: (h, 0, 0, 0)),
    ]


def attention(near, far, img, txt, chunk, slot, rides=(), cid=None):
    rows, columns = near.shape[0], near.shape[1] // 3
    tp, width = rows - img, 2 * HEAD_DIM
    pairs, n_chunks = columns // width, 2 * img // chunk
    tile = pl.BlockSpec((rows, width), lambda h: (0, h))
    return launch(
        functools.partial(attend_kernel, chunk, img, txt),
        (pairs,),
        qkv_specs(rows, pairs),
        [tile, tile] + lse_specs(n_chunks, chunk, tp),
        [jax.ShapeDtypeStruct((rows, columns), BF)] * 2
        + [
            jax.ShapeDtypeStruct((pairs, 2, n_chunks, chunk), F32),
            jax.ShapeDtypeStruct((pairs, 2, 1, 2 * tp), F32),
        ],
        [near, near, near, far, far, far],
        f"attend_{slot}",
        80 * pairs * rows * rows * HEAD_DIM,
        rides=rides,
        cid=cid,
    )


def attention_back(
    near, far, grad_near, grad_far, lse_i, lse_t, img, txt, chunk, slot, rides=(), cid=None
):
    rows, columns = near.shape[0], near.shape[1] // 3
    tp, width = rows - img, 2 * HEAD_DIM
    pairs, n_chunks = columns // width, 2 * img // chunk
    tile = pl.BlockSpec((rows, width), lambda h: (0, h))
    whole = pl.BlockSpec((rows, 3 * columns), lambda h: (0, 0))
    return launch(
        functools.partial(attend_back_kernel, chunk, img, txt),
        (pairs,),
        qkv_specs(rows, pairs) + [tile, tile] + lse_specs(n_chunks, chunk, tp),
        [whole, whole, pl.BlockSpec((1, 4, width), lambda h: (h, 0, 0))],
        [jax.ShapeDtypeStruct((rows, 3 * columns), BF)] * 2
        + [jax.ShapeDtypeStruct((pairs, 4, width), F32)],
        [near, near, near, far, far, far, grad_near, grad_far, lse_i, lse_t],
        f"attend_back_{slot}",
        200 * pairs * rows * rows * HEAD_DIM,
        scratch=[
            pltpu.VMEM((2, 2 * img, HEAD_DIM), F32),
            pltpu.VMEM((2, 2 * img, HEAD_DIM), F32),
            pltpu.VMEM((2, 2 * tp, HEAD_DIM), F32),
            pltpu.VMEM((2, 2 * tp, HEAD_DIM), F32),
        ],
        rides=rides,
        cid=cid,
    )


class Layout:
    def __init__(self, dp_size, tensor_size):
        dp_bits = dp_size.bit_length() - 1
        t_bits = tensor_size.bit_length() - 1
        self.dp = tuple(f"d{i}" for i in range(dp_bits))
        self.tensor = tuple(f"t{i}" for i in range(t_bits))
        self.names = self.dp + self.tensor
        self.compact = dp_size == 8 and tensor_size == 4
        self.p = self.tensor[-1]
        if self.compact:
            self.y, self.x, self.q = self.dp
            self.zh = self.tensor[0]
            self.upper = ()
        else:
            self.q = self.tensor[-2]
            self.upper = self.tensor[:-2]
        self.rest = tuple(n for n in self.names if n not in (self.p, self.q))

    def my_columns(self, v):
        shards = 2 ** len(self.upper)
        part = v.shape[-1] // (4 * shards)
        v = v.reshape(v.shape[:-1] + (shards, 4, part))
        at = index_of((self.q, self.p))
        v = lax.dynamic_index_in_dim(v, at, v.ndim - 2, keepdims=False)
        return v.reshape(v.shape[:-2] + (shards * part,))

    def all_columns(self, v):
        shards = 2 ** len(self.upper)
        g = gather_bits(v[None], (self.p, self.q))
        g = g.reshape((4,) + v.shape[:-1] + (shards, v.shape[-1] // shards))
        g = jnp.moveaxis(g, 0, -2)
        return g.reshape(v.shape[:-1] + (4 * v.shape[-1],))

    def gather_rows(self, own, end=()):
        pair = after(swap(own, self.p), *end)
        return [[own, swap(own, self.q)], [pair, swap(pair, self.q)]]

    def sum_far(self, w, blocks, img, rides=(), cid=None):
        (send, keep), rode = rows_nt([blocks[1][1], blocks[1][0]], w, img, (BF, F32), rides, cid)
        return (keep + swap(send, self.q).astype(F32)).astype(BF), rode

    def sum_near(self, w, blocks, img, rides=(), cid=None):
        (send, keep), rode = rows_nt([blocks[0][1], blocks[0][0]], w, img, (BF, F32), rides, cid)
        return keep + swap(send, self.q).astype(F32), rode

    def gather_weight(self, w):
        w = lax.all_gather(w, self.dp, axis=1, tiled=True)
        if self.upper:
            w = lax.all_gather(w, self.upper, axis=3, tiled=True)
        return jnp.swapaxes(w.reshape(2, 4, w.shape[1] // 4, -1), 0, 1)

    def trade_shards(self, w, end=()):
        w = w.reshape(w.shape[0], w.shape[1], -1)
        joint = (self.q, self.zh)
        same = lax.axis_index(self.zh) == lax.axis_index(self.q)
        cross = lax.ppermute(w, joint, [(1, 2), (2, 1)])
        second = lax.ppermute(w, joint, [(0, 1), (3, 2), (2, 0), (1, 3)])
        cross, second = after((cross, second), *end)
        first = jnp.where(same, w, cross)
        low = lax.axis_index(self.zh) == 0
        return jnp.concatenate(
            [jnp.where(low, first, second), jnp.where(low, second, first)], axis=1
        )

    def spread_near(self, own):
        return [swap(own[0], self.x), swap(own[1], self.y)]

    def spread_rows(self, own, nears):
        x, y = lax.axis_index(self.x), lax.axis_index(self.y)
        whole = jnp.zeros((4,) + own.shape, BF)
        for stream, far_axis in enumerate((self.y, self.x)):
            mine, near = own[stream], nears[stream]
            both, far = swap(near, far_axis), swap(mine, far_axis)
            dx, dy = (near, far) if stream == 0 else (far, near)
            for block, at in (
                (mine, 2 * y + x),
                (dx, 2 * y + 1 - x),
                (dy, 2 * (1 - y) + x),
                (both, 2 * (1 - y) + 1 - x),
            ):
                whole = lax.dynamic_update_slice(whole, block[None, None], (at, stream, 0, 0))
        return whole

    def spread_rows_async(self, own):
        own = own.reshape(own.shape[0], -1, own.shape[-1])
        return lax.all_gather(own, (self.y, self.x), axis=0, tiled=False)

    def trade_ride(self, array, back=False):
        if back:
            array = array.reshape(2, 2, -1, array.shape[-1])
        return TradeRide(array, self.zh, self.q, back)

    def scatter_generic(self, g, kinds):
        g = jnp.swapaxes(g.astype(F32), 0, 1).reshape(2, 4 * g.shape[2], kinds, -1)
        g = lax.psum_scatter(g, self.dp, scatter_dimension=1, tiled=True)
        if self.upper:
            g = lax.psum_scatter(g, self.upper, scatter_dimension=3, tiled=True)
        return g

    def sum_plane_async(self, g):
        return lax.psum_scatter(g, (self.y, self.x), scatter_dimension=0, tiled=False)

    def plane_rides(self, g):
        g = g.reshape((2, 2) + g.shape[1:])
        shape = (2,) + g.shape[3:]

        def along_x(source, target):
            x = 1 - lax.axis_index(self.x)
            return [(source.at[k, x, 0], target.at[k]) for k in range(2)]

        def along_y(source, target):
            y = 1 - lax.axis_index(self.y)
            return [(source.at[y, k, 1], target.at[k]) for k in range(2)]

        return [
            NeighbourRide(g, self.x, shape, along_x, 2),
            NeighbourRide(g, self.y, shape, along_y, 2),
        ]

    def sum_plane(self, g, arrived):
        x, y = lax.axis_index(self.x), lax.axis_index(self.y)
        pick = lambda v, i, dim: lax.dynamic_index_in_dim(v, i, dim, keepdims=False)
        g = g.reshape((2, 2) + g.shape[1:])
        done = []
        for stream in range(2):
            near, dim, far_axis, far = ((x, 1, self.y, y), (y, 0, self.x, x))[stream]
            at = (0, near, stream, 0, 0) if dim == 1 else (near, 0, stream, 0, 0)
            size = (2, 1) if dim == 1 else (1, 2)
            v = lax.dynamic_slice(g, at, size + (1,) + g.shape[3:]).reshape(arrived[stream].shape)
            v = v.astype(F32) + arrived[stream].astype(F32)
            v = pick(v, far, 0) + swap(pick(v, 1 - far, 0).astype(BF), far_axis).astype(F32)
            done.append(v)
        return jnp.stack(done)

    def trade_parts(self, g):
        g = g.reshape(2, 2, -1, g.shape[-1])
        zh = lax.axis_index(self.zh)
        return [lax.dynamic_index_in_dim(g, k, 1, keepdims=False) for k in (zh, 1 - zh)]

    def trade_sends(self, g):
        first, second = self.trade_parts(g)
        joint = (self.q, self.zh)
        return [
            lax.ppermute(first.astype(BF), joint, [(1, 2), (2, 1)]),
            lax.ppermute(second.astype(BF), joint, [(1, 0), (2, 3), (0, 2), (3, 1)]),
        ]

    def trade_adds(self, g, arrived, kinds):
        same = lax.axis_index(self.zh) == lax.axis_index(self.q)
        total = jnp.where(same, self.trade_parts(g)[0].astype(F32), arrived[0].astype(F32))
        total += arrived[1].astype(F32)
        return total.reshape(2, total.shape[1], kinds, -1)


def norm_parts(values):
    average = jnp.mean(values, axis=-1, keepdims=True)
    centred = values - average
    variance = jnp.mean(centred * centred, axis=-1, keepdims=True)
    inverse = lax.rsqrt(variance + 1e-06)
    return centred * inverse, inverse


def norm_back(normed, inverse, grad_in):
    first_mean = jnp.mean(grad_in, axis=-1, keepdims=True)
    cross_mean = jnp.mean(grad_in * normed, axis=-1, keepdims=True)
    return inverse * (grad_in - first_mean - normed * cross_mean)


def body(
    lay,
    image_in,
    text_in,
    condition,
    live_slots,
    ada_weight,
    ada_bias,
    qkv_weight,
    qv_bias,
    proj_weight,
    proj_bias,
    up_weight,
    up_bias,
    down_weight,
    down_bias,
    image_grad,
    text_grad,
):
    width = image_in.shape[1]
    part = qkv_weight.shape[2]
    columns = qkv_weight.shape[3]
    img_rows, txt_rows = image_in.shape[0], text_in.shape[0]
    txt_pad = -(-txt_rows // 16) * 16
    group_slots = condition.shape[0]
    dp_index, t_index = index_of(lay.dp), index_of(lay.tensor)
    t_count = 2 ** len(lay.tensor)
    assert group_slots * 2 == t_count
    my_slot = t_index // 2
    dp_up, t_up = lay.dp[::-1], lay.tensor[::-1]

    rows = img_rows + txt_pad
    is_image = lax.broadcasted_iota(jnp.int32, (rows, 1), 0) < img_rows

    def pack(image, text):
        return jnp.concatenate([image, jnp.pad(text, ((0, txt_pad - txt_rows), (0, 0)))], axis=0)

    def spread(per_stream):
        return jnp.where(is_image, per_stream[0], per_stream[1])

    def total(v):
        return jnp.stack([jnp.sum(v[:img_rows], axis=0), jnp.sum(v[img_rows:], axis=0)])

    def flat(blocks):
        return blocks[0] + blocks[1]

    def unflat(v):
        return [list(v[:2]), list(v[2:4])]

    qkv_local = jnp.swapaxes(qkv_weight, 1, 2)
    proj_local = jnp.swapaxes(proj_weight, 1, 2)[:, :, None]
    up_local = up_weight[:, :, None]
    down_local = jnp.swapaxes(down_weight, 1, 2)[:, :, None]
    compact = lay.compact
    if compact:
        qkv_own = lay.trade_shards(qkv_local)
        qkv_near = lay.spread_near(qkv_own)
    else:
        qkv_full, up_full, proj_full, down_full = [
            lay.gather_weight(w) for w in (qkv_local, up_local, proj_local, down_local)
        ]

    cond_all = gather_bits(condition, dp_up).astype(F32)
    silu_all = jax.nn.silu(cond_all).astype(BF)
    silu_mine = lax.dynamic_slice_in_dim(silu_all, dp_index * part, part, 1)
    mod = jnp.einsum("sd,tdkc->stkc", silu_mine, ada_weight, preferred_element_type=F32)
    mod = scatter_bits(mod, lay.dp)
    if compact:
        mod = after(mod, qkv_own)
    mod = gather_bits(mod[None], t_up)
    mod = lax.dynamic_index_in_dim(mod, my_slot, 1, keepdims=False)
    mod = jnp.moveaxis(mod, 0, 2).reshape(2, 6, width) + ada_bias.astype(F32)
    live = lax.dynamic_index_in_dim(live_slots, my_slot, 0, keepdims=False).astype(F32)

    mods = [spread(mod[:, k]) for k in range(6)]
    shift_one, scale_one, gate_one, shift_two, scale_two, gate_two = mods

    inputs = pack(image_in, text_in).astype(F32)
    grad_out = live * pack(image_grad, text_grad).astype(F32)
    grad_two = (gate_two * grad_out).astype(BF)

    first_norm = norm_parts(inputs)
    first_hidden = (first_norm[0] * (1.0 + scale_one) + shift_one).astype(BF)
    if compact:
        first_hidden = after(first_hidden, qkv_near)
    first = lay.gather_rows(first_hidden)
    if compact:
        qkv_full = lay.spread_rows(qkv_own, qkv_near)
    qv = lay.my_columns(qv_bias.astype(F32))
    qkv_bias = jnp.concatenate([qv[:, 0], jnp.zeros_like(qv[:, 0]), qv[:, 1]], axis=1)
    heads_n = qv.shape[2]
    img = img_rows

    def ride(array, start, stop):
        return row_ride(array, lay.p, start, stop)

    cut = rows // 3 // 16 * 16
    extra = [[], [], []]
    if compact:
        extra = [
            [lay.trade_ride(w.reshape(w.shape[0], part, -1))]
            for w in (proj_local, up_local[:1], up_local[1:])
        ]
    qkv, rode = rows_nn(
        flat(first), qkv_full, img, "bias", bias=qkv_bias, rides=extra[0], cid=1
    )
    qkv = unflat(qkv)
    chunk = min(256, img_rows)
    if compact:
        proj_full = lay.spread_rows_async(rode[0])
    other, rode = attention(
        qkv[0][1], qkv[1][1], img, txt_rows, chunk, 1, rides=extra[1], cid=2
    )
    if compact:
        up_full = [lay.spread_rows_async(rode[0])]
        qkv, other = after((qkv, other), proj_full)
    mine, rode = attention(
        qkv[0][0],
        qkv[1][0],
        img,
        txt_rows,
        chunk,
        0,
        rides=[ride(grad_two, 0, cut)] + extra[2],
        cid=10,
    )
    grad_two_pair = rode[:1]
    heads_out = [[mine[z], other[z]] for z in range(2)]
    if compact:
        up_full.append(lay.spread_rows_async(rode[1]))
        down_own = lay.trade_shards(after(down_local, mine))

    far = swap(lay.sum_far(proj_full, heads_out, img)[0], lay.p)
    near, unused = lay.sum_near(proj_full, heads_out, img)
    branch_one = near + far.astype(F32) + spread(proj_bias.astype(F32))
    middle = inputs + gate_one * branch_one
    second_norm = norm_parts(middle)
    second_hidden = (second_norm[0] * (1.0 + scale_two) + shift_two).astype(BF)
    if compact:
        second_hidden, down_own = tie(second_hidden, down_own)
        down_full = lay.spread_rows_async(down_own)
    second = lay.gather_rows(second_hidden)
    up_mine = lay.my_columns(up_bias.astype(F32))
    up_n = up_mine.shape[1]
    up_out, rode = rows_nn(
        flat(second), up_full, img, "gelu", bias=up_mine, rides=[ride(grad_two, cut, rows)], cid=13
    )
    grad_two_pair = jnp.concatenate(grad_two_pair + rode, axis=0)
    grad_two_blocks = [
        [grad_two, swap(grad_two, lay.q)], [grad_two_pair, swap(grad_two_pair, lay.q)]
    ]
    activated, slopes = up_out[:4], up_out[4:]
    grad_two_flat = flat(grad_two_blocks)
    back_out, unused = rows_nn(grad_two_flat, down_full, img, "slope", slopes=slopes)
    grad_inner, up_part = back_out[:4], back_out[4].reshape(2, up_n)
    far_two, unused = lay.sum_far(up_full, unflat(grad_inner), img)
    cut = rows * 15 // 37 // 16 * 16
    down_grads, rode_two = weight_grad(
        grad_two_flat, activated, img, rides=[ride(far_two, cut, rows)], cid=4
    )
    if compact:
        down_plane = lay.sum_plane_async(down_grads)
    near_two, rode = lay.sum_near(
        up_full, after(unflat(grad_inner), down_grads), img, [ride(far_two, 0, cut)], 5
    )
    grad_hidden_two = near_two + jnp.concatenate(rode + rode_two, axis=0).astype(F32)
    grad_middle = grad_out + norm_back(
        second_norm[0], second_norm[1], grad_hidden_two * (1.0 + scale_two)
    )
    grad_one = (gate_one * grad_middle).astype(BF)
    cut, cut_two = rows * 17 // 37 // 16 * 16, rows * 27 // 37 // 16 * 16
    up_grads, rode = weight_grad(
        after(flat(second), grad_one), grad_inner, img, rides=[ride(grad_one, 0, cut)], cid=6
    )
    if compact:
        up_plane = lay.sum_plane_async(up_grads)
    near, rode_two = lay.sum_near(
        down_full, after(unflat(activated), up_grads), img, [ride(grad_one, cut, cut_two)], 7
    )
    deps = (near, down_plane) if compact else (near,)
    far, rode_three = lay.sum_far(
        down_full, after(unflat(activated), *deps), img, [ride(grad_one, cut_two, rows)], 3
    )
    grad_one_pair = jnp.concatenate(rode + rode_two + rode_three, axis=0)
    grad_one_blocks = [
        [grad_one, swap(grad_one, lay.q)], [grad_one_pair, swap(grad_one_pair, lay.q)]
    ]
    grad_heads = unflat(rows_nn(flat(grad_one_blocks), proj_full, img, "plain")[0])

    def back(c, saved, heads, rides, cid):
        return attention_back(
            qkv[0][c],
            qkv[1][c],
            heads[0][c],
            heads[1][c],
            saved[2],
            saved[3],
            img,
            txt_rows,
            chunk,
            c,
            rides,
            cid,
        )

    half = rows // 32 * 16
    rides, rides_two = [ride(far, 0, half)], [ride(far, half, rows)]
    if compact:
        rides.append(lay.trade_ride(down_plane, True))
        rides_two.append(lay.trade_ride(up_plane, True))
    grad_other, down_sums = back(1, other, grad_heads, rides, 11)
    proj_grads, unused = weight_grad(
        after(flat(grad_one_blocks), grad_other), flat(heads_out), img
    )
    if compact:
        proj_plane = lay.sum_plane_async(proj_grads)
    grad_mine, up_sums = back(
        0,
        mine,
        after(grad_heads, proj_grads),
        rides_two,
        12,
    )
    far = jnp.concatenate(down_sums[:1] + up_sums[:1], axis=0)
    branch_two = near + far.astype(F32) + spread(down_bias.astype(F32))
    outputs = (live * (middle + gate_two * branch_two)).astype(BF)
    grad_qkv = [[grad_mine[z], grad_other[z]] for z in range(2)]
    far, unused = lay.sum_far(qkv_full, grad_qkv, img)
    cut = rows * 16 // 37 // 16 * 16
    rides = [ride(far, 0, cut)]
    if compact:
        rides.append(lay.trade_ride(proj_plane, True))
    qkv_grads, rode = weight_grad(flat(first), flat(grad_qkv), img, rides=rides, cid=8)
    rides = [ride(far, cut, rows)]
    if compact:
        proj_sums = rode[1]
        rides += lay.plane_rides(qkv_grads)
    near, rode_two = lay.sum_near(qkv_full, after(grad_qkv, qkv_grads), img, rides, 9)
    far = jnp.concatenate(rode[:1] + rode_two[:1], axis=0)
    if compact:
        down_grad, up_grad, proj_grad = [
            (v[0].astype(F32) + v[1].astype(F32))[:, :, None]
            for v in (down_sums[1], up_sums[1], proj_sums)
        ]
        qkv_plane = lay.sum_plane(qkv_grads, rode_two[1:3])
    else:
        down_grad, up_grad, proj_grad = [
            lay.scatter_generic(g, 1) for g in (down_grads, up_grads, proj_grads)
        ]
        qkv_grad = lay.scatter_generic(qkv_grads, 3)
    grad_hidden_one = near + far.astype(F32)
    input_grads = grad_middle + norm_back(
        first_norm[0], first_norm[1], grad_hidden_one * (1.0 + scale_one)
    )

    grad_mod = jnp.stack(
        [
            total(grad_hidden_one),
            total(grad_hidden_one * first_norm[0]),
            total(branch_one * grad_middle),
            total(grad_hidden_two),
            total(grad_hidden_two * second_norm[0]),
            total(branch_two * grad_out),
        ],
        axis=1,
    )
    grad_mod = sum_bits(grad_mod, (lay.p,))
    grad_mod = gather_bits(grad_mod[None], t_up[1:])
    if compact:
        qkv_plane, grad_mod = tie(qkv_plane, grad_mod)
    grad_mod = lax.dynamic_slice_in_dim(grad_mod, t_index * columns, columns, 3)
    grad_mod = gather_bits(grad_mod, dp_up)
    high = lax.Precision.HIGHEST
    ada_grad = jnp.einsum("sd,stkc->tdkc", silu_mine.astype(F32), grad_mod, precision=high)
    cond_terms = jnp.einsum("stkc,tdkc->sd", grad_mod, ada_weight.astype(F32), precision=high)
    cond_terms = gather_bits(cond_terms[None], dp_up)
    cond_terms = lax.dynamic_slice_in_dim(cond_terms, dp_index * group_slots, group_slots, 1)
    cond_terms = jnp.swapaxes(cond_terms, 0, 1).reshape(group_slots, width)
    if compact:
        arrived = lay.trade_sends(qkv_plane)
        cond_terms, arrived = tie(cond_terms, arrived)
        qkv_grad = lay.trade_adds(qkv_plane, arrived, 3)
    down_grad = jnp.swapaxes(down_grad[:, :, 0], 1, 2)
    proj_grad = jnp.swapaxes(proj_grad[:, :, 0], 1, 2)
    up_grad = up_grad[:, :, 0]
    qkv_grad = jnp.swapaxes(qkv_grad, 1, 2)
    cond_terms = sum_bits(cond_terms, t_up)
    cond_terms = lax.dynamic_slice_in_dim(cond_terms, t_index * columns, columns, 1)
    cond_slice = lax.dynamic_slice_in_dim(condition.astype(F32), t_index * columns, columns, 1)
    unused, silu_pull = jax.vjp(jax.nn.silu, cond_slice)
    condition_grad = silu_pull(cond_terms)[0]
    ada_bias_grad = gather_bits(jnp.sum(grad_mod, axis=0)[None], t_up)
    ada_bias_grad = jnp.moveaxis(ada_bias_grad, 0, 2).reshape(2, 6, width)

    own_part = sum_bits(
        jnp.stack([total(grad_one.astype(F32)), total(grad_two.astype(F32))]), (lay.p, lay.q)
    )
    sums = grad_mine[2] + grad_other[2]
    pairs = sums.shape[0]
    qv_part = jnp.transpose(sums.reshape(pairs, 2, 2, -1), (2, 1, 0, 3)).reshape(2, 2, heads_n)
    if compact:
        qv_part = after(qv_part, near)
    packed = jnp.concatenate([qv_part.reshape(-1), up_part.reshape(-1), own_part.reshape(-1)])
    packed = sum_bits(packed.reshape(-1, 128), lay.rest).reshape(-1)
    cut_one, cut_two = qv_part.size, qv_part.size + up_part.size
    qv_bias_grad = lay.all_columns(packed[:cut_one].reshape(qv_part.shape))
    up_bias_grad = lay.all_columns(packed[cut_one:cut_two].reshape(up_part.shape))
    own_part = packed[cut_two:].reshape(own_part.shape)
    return (
        outputs[:img_rows],
        outputs[img_rows : img_rows + txt_rows],
        input_grads[:img_rows],
        input_grads[img_rows : img_rows + txt_rows],
        condition_grad,
        ada_grad,
        ada_bias_grad,
        qkv_grad,
        qv_bias_grad,
        proj_grad,
        own_part[0],
        up_grad,
        up_bias_grad,
        down_grad,
        own_part[1],
    )


def solution(mesh):
    lay = Layout(mesh.shape["dp"], mesh.shape["tensor"])
    bits = Mesh(mesh.devices.reshape((2,) * len(lay.names)), lay.names)
    dp, tensor, every = lay.dp, lay.tensor, lay.names
    in_specs = (
        P(every, None),
        P(every, None),
        P(dp, None),
        P(dp),
        P(None, dp, None, tensor),
        P(),
        P(None, None, dp, tensor),
        P(),
        P(None, tensor, dp),
        P(),
        P(None, dp, tensor),
        P(),
        P(None, tensor, dp),
        P(),
        P(every, None),
        P(every, None),
    )
    out_specs = (
        P(every, None),
        P(every, None),
        P(every, None),
        P(every, None),
        P(dp, tensor),
        P(None, dp, None, tensor),
        P(),
        P(None, None, dp, tensor),
        P(),
        P(None, tensor, dp),
        P(),
        P(None, dp, tensor),
        P(),
        P(None, tensor, dp),
        P(),
    )
    return jax.shard_map(
        functools.partial(body, lay), mesh=bits, in_specs=in_specs, out_specs=out_specs, check_vma=False
    )
```
